128 devices in a mesh: ctx: 8 (over x, z_lo), fsdp: 4 (over y), tp: 4 (over z_hi, core).
Axes of the slice: x: 4, y: 4, z: 4 (z_hi: 2, z_lo: 2; z = z_hi * 2 + z_lo), core: 2. Of those that a mesh axis runs over, the one named last changes fastest.
Arguments:
- base_ids: int32 [4, 2048], P('fsdp', 'ctx'), may hold values from 0 to 511
- embed_table: bfloat16 [512, 8192], P(None, 'tp'), may hold values from -6 to 6
- norm_gain: float32 [8192], replicated, may hold values from 0.1 to 1.9
- in_weight: bfloat16 [8192, 3, 4096], P('fsdp', None, 'tp'), may hold values from -0.0625 to 0.0625
- conv_taps: float32 [3, 3, 4096], P(None, None, 'tp'), may hold values from -3 to 3
- modal_poles: float32 [16, 4096], P(None, 'tp'), may hold values from 0.9 to 1, as said below
- residues: float32 [16, 4096], P(None, 'tp'), may hold values from -0.25 to 0.25
- skip_gain: float32 [4096], P('tp'), may hold values from -4 to 4
Outputs:
- mixed: bfloat16 [4, 2048, 4096], P('fsdp', 'ctx', 'tp')
The draws below stay inside these ranges and needn't reach their ends.
Inputs may be any that keep to these rules, and one draw needn't show every extreme that they name: `modal_poles`: every pole lies strictly between 0 and 1.
All inputs are finite; a program needn't handle non-finite values.
Results may differ from the reference program's by a relative error of at most 0.008.
Values may be sent and summed in bfloat16 or wider, within the bound.
A program may use at most 256 MiB of HBM per device.

```python
import math
import jax
import jax.numpy as jnp
import numpy as np
from jax import lax

D = 8192
POLES = 16
VOCAB = 512
CH = 4096
TAPS = 3
BLOCK = 64
LENGTH = 2048
SEQS = 4


def pole_rates(key, slow_share):
    pick_key, slow_key, fast_key = jax.random.split(jax.random.fold_in(key, 11), 3)
    slow_mask = jax.random.uniform(pick_key, (POLES, CH)) < slow_share
    slow_rate = jnp.exp(jax.random.uniform(slow_key, (POLES, CH), minval=jnp.log(0.2 / LENGTH), maxval=jnp.log(2.0 / LENGTH)))
    fast_rate = jnp.exp(jax.random.uniform(fast_key, (POLES, CH), minval=jnp.log(1.0 / 50.0), maxval=jnp.log(1.0 / 20.0)))
    return jnp.where(slow_mask, slow_rate, fast_rate)


def draw_modal_poles(key, part):
    rates = pole_rates(key, 0.5)
    return jnp.exp(-rates).astype(jnp.float32)


def draw_residues(key, part):
    rates = pole_rates(key, 0.5)
    key = jax.random.fold_in(key, 7)
    normal_vals = jnp.clip(jax.random.normal(key, (POLES, CH), jnp.float32), -3.0, 3.0)
    scale = jnp.sqrt(2.0 * jnp.maximum(rates, 1.0 / LENGTH) / POLES)
    return (normal_vals * scale).astype(jnp.float32)


def plant(drawn, rng, least, largest):
    longest = drawn.shape.index(max(drawn.shape))
    spots = []
    for shift in (0, 1):
        where = [jax.random.randint(jax.random.fold_in(rng, axis), (), 0, length) for axis, length in enumerate(drawn.shape)]
        where[longest] = (where[longest] + shift) % drawn.shape[longest]
        spots.append(tuple(where))
    return drawn.at[spots[0]].set(least).at[spots[1]].set(largest)


def steps_of(key, shape, shards, low, high):
    level, own = 1.0, jax.random.fold_in(key, 6)
    for axis_at, shards_of in shards:
        draws = jnp.exp(jax.random.uniform(jax.random.fold_in(own, axis_at), (shards_of,), jnp.float32, low / len(shards), high / len(shards)))
        level = level * jnp.repeat(draws, shape[axis_at] // shards_of).reshape([-1 if axis == axis_at else 1 for axis in range(len(shape))])
    return level


def rank_table(count, lean):
    weights = [(1 << 20) // math.isqrt(standing ** lean) + 1 for standing in range(1, count + 1)]
    deviation = 1 + sum(weights) // (1 << 30)
    return np.cumsum(np.array([max(1, weight // deviation) for weight in weights]))


def ranked_ids(key, extent, number_of, skew):
    listing = rank_table(number_of, skew)
    pick = jax.random.randint(jax.random.fold_in(key, 1), extent, 0, int(listing[number_of - 1]))
    grade = jnp.searchsorted(jnp.asarray(listing, jnp.int32), pick, side="right")
    return jax.random.permutation(jax.random.fold_in(key, 2), number_of)[grade].astype(jnp.int32)


def gaussian(stream_key, extent, scale, most, pieces=(), held_as=jnp.bfloat16):
    gain = steps_of(stream_key, extent, pieces, -0.22, 0.18) if pieces else 1.0
    result = jax.random.normal(stream_key, extent, jnp.float32) * scale * gain
    return jnp.minimum(jnp.maximum(result, -most), most).astype(held_as)


def setup_inputs(seed: int = 0) -> dict:
    key_list = jax.random.split(jax.random.key(seed), 9)
    return {
        "base_ids": plant(ranked_ids(key_list[0], (SEQS, LENGTH), VOCAB, 2), jax.random.fold_in(key_list[0], 3), 0, VOCAB - 1).astype(jnp.int32),
        "embed_table": gaussian(key_list[1], (VOCAB, D), 1.0, 6.0, ((1, 4),)),
        "norm_gain": jnp.clip(1.0 + 0.18 * jax.random.normal(key_list[2], (D,), jnp.float32), 0.1, 1.9),
        "in_weight": gaussian(key_list[3], (D, 3, CH), D ** -0.5, 0.0625, ((0, 4), (2, 4))),
        "conv_taps": gaussian(key_list[4], (3, TAPS, CH), 0.6, 3.0, ((2, 4),), jnp.float32),
        "modal_poles": draw_modal_poles(jax.random.fold_in(key_list[8], 71), 0),
        "residues": draw_residues(jax.random.fold_in(key_list[8], 71), 0),
        "skip_gain": gaussian(key_list[7], (CH,), 1.0, 4.0, ((0, 4),), jnp.float32),
    }


norm_eps = 1e-06

def modal_conv(product, modal_poles, residues):
    log_poles = jnp.log(modal_poles)
    steps = jnp.arange(BLOCK + 1).astype(jnp.float32)
    powers = jnp.exp(steps[:, None, None] * log_poles[None])
    kernel = lax.optimization_barrier(jnp.sum(powers[:BLOCK] * residues[None], axis=1))
    offsets = jnp.arange(BLOCK)[:, None] - jnp.arange(BLOCK)[None, :]
    toeplitz = jnp.where((offsets >= 0)[:, :, None], kernel[jnp.maximum(offsets, 0)], jnp.float32(0.0))
    backward_powers = powers[:BLOCK][::-1]
    lifted = powers[1:] * residues[None]
    decay = powers[BLOCK]
    u_blocks = product.reshape(SEQS, LENGTH // BLOCK, BLOCK, CH).transpose(1, 0, 2, 3)

    def advance(state, block_vals):
        inner = jnp.einsum('tsc,xsc->xtc', toeplitz, block_vals, precision=lax.Precision.HIGHEST)
        carried = jnp.einsum('tnc,xnc->xtc', lifted, state, precision=lax.Precision.HIGHEST)
        local = jnp.einsum('snc,xsc->xnc', backward_powers, block_vals, precision=lax.Precision.HIGHEST)
        return (decay[None] * state + local, inner + carried)
    start_state = jnp.zeros((SEQS, POLES, CH), jnp.float32)
    _, outputs = lax.scan(advance, start_state, u_blocks)
    return outputs.transpose(1, 0, 2, 3).reshape(SEQS, LENGTH, CH)

def reference(base_ids, embed_table, norm_gain, in_weight, conv_taps, modal_poles, residues, skip_gain):
    embedded = embed_table[base_ids]
    wide_embed = embedded.astype(jnp.float32)
    mean_square = lax.optimization_barrier(jnp.mean(wide_embed * wide_embed, axis=-1, keepdims=True))
    normed = (wide_embed * lax.rsqrt(mean_square + norm_eps) * norm_gain).astype(jnp.bfloat16)
    summed = jnp.dot(normed.reshape(SEQS * LENGTH, D), in_weight.reshape(D, 3 * CH), preferred_element_type=jnp.float32)
    proj = summed.astype(jnp.bfloat16).reshape(SEQS, LENGTH, 3, CH)
    padded = jnp.pad(proj.astype(jnp.float32), ((0, 0), (TAPS - 1, 0), (0, 0), (0, 0)))
    filtered = jnp.zeros((SEQS, LENGTH, 3, CH), jnp.float32)
    for lag_index in range(TAPS):
        first = TAPS - 1 - lag_index
        filtered = filtered + conv_taps[:, lag_index, :][None, None] * padded[:, first:first + LENGTH]
    query_f = filtered[:, :, 0, :]
    key_f = filtered[:, :, 1, :]
    value_f = filtered[:, :, 2, :]
    product = key_f * value_f
    convolved = modal_conv(product, modal_poles, residues)
    return (query_f * (convolved + skip_gain * product)).astype(jnp.bfloat16)
```

```python
import functools

import jax
import jax.numpy as jnp
from jax import lax
from jax.experimental import pallas as pl
from jax.experimental.pallas import tpu as pltpu
from jax.sharding import PartitionSpec as P

MESH = pl.DeviceIdType.MESH
F32 = jnp.float32
BF16 = jnp.bfloat16
norm_eps = 1e-06

CTX, FSDP, TP = 8, 4, 4
GROUP = CTX * FSDP
ROWS = 64
FEAT = 2048
CHAN = 1024
SLICE = CHAN // GROUP
STEPS = 256
POLES = 16
CHUNK = 256


def peers(i, y, t, fn):
    me = i * FSDP + y

    def one(k, carry):
        other = lax.rem(me + k, GROUP)
        fn(other, (lax.div(other, FSDP), lax.rem(other, FSDP), t))
        return carry

    lax.fori_loop(1, GROUP, one, 0)


def project_kernel(
    ids_ref, table_ref, gain_ref, weight_ref, parts_ref, all_ids_ref,
    weight_buf, own, rows, squares, send_buf,
    weight_sem, own_sem, rows_sem, rows_send, sq_send, sq_recv, ids_send, ids_recv, part_send, part_recv,
):
    i = lax.axis_index("ctx")
    y = lax.axis_index("fsdp")
    t = lax.axis_index("tp")
    me = i * FSDP + y
    hi = lax.div(t, 2)
    flip = i + 1 - 2 * lax.rem(i, 2)
    chunks = CHAN // CHUNK
    turn = lax.div(i, 2)

    def columns(step):
        return pl.ds(pl.multiple_of(lax.rem(turn + step, chunks) * CHUNK, CHUNK), CHUNK)

    def weight_copy(step):
        return pltpu.make_async_copy(
            weight_ref.at[:, :, columns(step)], weight_buf.at[step], weight_sem.at[step]
        )

    own_copy = pltpu.make_async_copy(table_ref.at[pl.ds(pl.multiple_of(i * ROWS, ROWS), ROWS), :], own, own_sem)
    own_copy.start()
    for step in range(chunks):
        weight_copy(step).start()

    barrier = pltpu.get_barrier_semaphore()

    def greet(device):
        pl.semaphore_signal(barrier, inc=1, device_id=device, device_id_type=MESH)

    for k in range(1, TP):
        greet((i, y, lax.rem(t + k, TP)))
    for core in range(2):
        greet((flip, y, (1 - hi) * 2 + core))
    peers(i, y, t, lambda other, device: greet(device))
    pl.semaphore_wait(barrier, TP - 1 + 2 + GROUP - 1)

    def table_rows(block):
        return table_ref.at[pl.ds(pl.multiple_of(block * ROWS, ROWS), ROWS), :]

    def rows_to(block, device, slot):
        return pltpu.make_async_remote_copy(
            src_ref=table_rows(block), dst_ref=rows, send_sem=rows_send.at[slot], recv_sem=rows_sem,
            device_id=device, device_id_type=MESH,
        )

    sibling = hi * 2 + 1 - lax.rem(t, 2)
    keep = pltpu.make_async_copy(table_rows(i), rows, rows_sem)

    @pl.when(t == y)
    def _():
        for core in range(2):
            rows_to(flip, (flip, y, (1 - hi) * 2 + core), core).start()
        rows_to(i, (i, y, sibling), 2).start()
        keep.start()

    def ids_to(other, device):
        return pltpu.make_async_remote_copy(
            src_ref=ids_ref, dst_ref=all_ids_ref.at[y, pl.ds(i, 1), :], send_sem=ids_send.at[other], recv_sem=ids_recv.at[me],
            device_id=device, device_id_type=MESH,
        )

    ids_keep = pltpu.make_async_copy(ids_ref, all_ids_ref.at[y, pl.ds(i, 1), :], ids_recv.at[me])
    ids_keep.start()

    def send_ids(other, device):
        ids_to(other, device).start()

    peers(i, y, t, send_ids)

    own_copy.wait()
    mine = own[...].astype(F32)
    sums = jnp.sum(mine * mine, axis=1, keepdims=True)
    diagonal = lax.broadcasted_iota(jnp.int32, (ROWS, 128), 0) == lax.broadcasted_iota(jnp.int32, (ROWS, 128), 1)
    flat = jnp.sum(jnp.where(diagonal, sums, 0.0), axis=0, keepdims=True)
    squares[t] = jnp.broadcast_to(flat, (8, 128))

    def squares_to(k):
        return pltpu.make_async_remote_copy(
            src_ref=squares.at[t], dst_ref=squares.at[t], send_sem=sq_send.at[k], recv_sem=sq_recv.at[t],
            device_id=(i, y, lax.rem(t + k, TP)), device_id_type=MESH,
        )

    for k in range(1, TP):
        squares_to(k).start()
    for k in range(1, TP):
        source = lax.rem(t + k, TP)
        pltpu.make_async_copy(squares.at[source], squares.at[source], sq_recv.at[source]).wait()
    total = squares[0] + squares[1] + squares[2] + squares[3]
    scale = lax.rsqrt(total[0:1, :] * (1.0 / (FEAT * FSDP)) + norm_eps)
    scale = jnp.sum(jnp.where(diagonal, scale, 0.0), axis=1, keepdims=True)

    keep.wait()
    gain = gain_ref[:, pl.ds(pl.multiple_of(y * FEAT, FEAT), FEAT)]
    normed = (rows[...].astype(F32) * scale * gain).astype(BF16)

    lane_block = lax.div(lax.broadcasted_iota(jnp.int32, (48, 128), 1), SLICE)

    def part_to(slot, device):
        return pltpu.make_async_remote_copy(
            src_ref=send_buf.at[slot], dst_ref=parts_ref.at[me], send_sem=part_send.at[slot], recv_sem=part_recv.at[me],
            device_id=device, device_id_type=MESH,
        )

    for step in range(chunks):
        weight_copy(step).wait()
        dots = [
            jnp.dot(normed, weight_buf[step, stream], preferred_element_type=F32) for stream in range(3)
        ]
        for half in range(CHUNK // 128):
            cols = [dot[:, half * 128 : half * 128 + 128] for dot in dots]
            for b in range(4):
                base = [pltpu.roll(c, (32 * (s - b)) % 128, 1) if (s - b) % 4 else c for s, c in enumerate(cols)]
                tail = jnp.concatenate(
                    [pltpu.roll(c[48:64], (32 * (3 - b)) % 128, 1) if (3 - b) % 4 else c[48:64] for c in cols], axis=0
                )
                piece = jnp.where(
                    lane_block == 0,
                    base[0][:48],
                    jnp.where(lane_block == 1, base[1][:48], jnp.where(lane_block == 2, base[2][:48], tail)),
                )
                send_buf[step * 8 + half * 4 + b] = piece.astype(BF16)
        first = lax.rem(turn + step, chunks) * 8
        for k in range(8):
            other = first + k
            slot = step * 8 + k

            @pl.when(other == me)
            def _():
                pltpu.make_async_copy(send_buf.at[slot], parts_ref.at[me], part_recv.at[me]).start()

            @pl.when(other != me)
            def _():
                part_to(slot, (lax.div(other, FSDP), lax.rem(other, FSDP), t)).start()

    def arrive(src, carry):
        pltpu.make_async_copy(parts_ref.at[src], parts_ref.at[src], part_recv.at[src]).wait()
        at = all_ids_ref.at[lax.rem(src, FSDP), pl.ds(lax.div(src, FSDP), 1), :]
        pltpu.make_async_copy(ids_ref, at, ids_recv.at[src]).wait()
        return carry

    lax.fori_loop(0, GROUP, arrive, 0)
    for k in range(1, TP):
        squares_to(k).wait_send()

    @pl.when(t == y)
    def _():
        for slot in range(3):
            rows_to(i, (i, y, sibling), slot).wait_send()

    def sent(other, device):
        ids_to(other, device).wait_send()

    peers(i, y, t, sent)
    for step in range(chunks):
        first = lax.rem(turn + step, chunks) * 8
        for k in range(8):

            @pl.when(first + k != me)
            def _():
                part_to(step * 8 + k, (i, y, t)).wait_send()


def project(base_ids, table, gain, weight):
    hbm = pl.BlockSpec(memory_space=pl.ANY)
    vmem = pl.BlockSpec(memory_space=pltpu.VMEM)
    dma = pltpu.SemaphoreType.DMA
    return pl.pallas_call(
        project_kernel,
        out_shape=(
            jax.ShapeDtypeStruct((GROUP, 48, 128), BF16),
            jax.ShapeDtypeStruct((FSDP, CTX, STEPS), jnp.int32),
        ),
        in_specs=[vmem, hbm, vmem, hbm],
        out_specs=(vmem, vmem),
        scratch_shapes=[
            pltpu.VMEM((CHAN // CHUNK, 3, FEAT, CHUNK), BF16),
            pltpu.VMEM((ROWS, FEAT), BF16),
            pltpu.VMEM((ROWS, FEAT), BF16),
            pltpu.VMEM((TP, 8, 128), F32),
            pltpu.VMEM((GROUP, 48, 128), BF16),
            dma((CHAN // CHUNK,)),
            dma,
            dma,
            dma((3,)),
            dma((TP,)),
            dma((TP,)),
            dma((GROUP,)),
            dma((GROUP,)),
            dma((GROUP,)),
            dma((GROUP,)),
        ],
        compiler_params=pltpu.CompilerParams(
            collective_id=0, has_side_effects=True, vmem_limit_bytes=40 * 2**20
        ),
        name="project",
    )(base_ids, table, gain, weight)


def tiled_lanes(x, b):
    block = lax.div(lax.broadcasted_iota(jnp.int32, x.shape, 1), SLICE)
    x = pltpu.roll(x, lax.rem(4 - b, 4) * SLICE, 1)
    out = x
    for k in range(1, 4):
        out = jnp.where(block == k, pltpu.roll(x, SLICE * k, 1), out)
    return out


def convolve_kernel(
    parts_ref, ids_ref, taps_ref, poles_ref, res_ref, skip_ref, out_ref, table, xq, xk, xv, product, mixed
):
    i = lax.axis_index("ctx")
    b = lax.axis_index("fsdp")
    here = pl.ds(pl.multiple_of(i * 128, 128), 128)
    block8 = lax.div(lax.broadcasted_iota(jnp.int32, (8, 128), 1), SLICE)

    for v in range(CTX):
        a = parts_ref[v * 4].astype(F32)
        for k in range(1, 4):
            a = a + parts_ref[v * 4 + k].astype(F32)
        tail = [pltpu.roll(a[16 * s : 16 * s + 16], SLICE * (s + 1), 1) for s in range(3)]
        block = lax.div(lax.broadcasted_iota(jnp.int32, (16, 128), 1), SLICE)
        last = jnp.where(block == 0, tail[0], jnp.where(block == 1, tail[1], tail[2]))
        a = jnp.concatenate([a, last], axis=0)
        for s in range(4):
            table[s, pl.ds(v * ROWS, ROWS), :] = (pltpu.roll(a, SLICE * s, 1) if s else a).astype(BF16)

    span = 32
    lane = lax.broadcasted_iota(jnp.int32, (span * 8, 128), 1)
    block = lax.div(lane, SLICE)

    def gather(at, carry):
        outs = []
        for s in range(4):
            ids = ids_ref[s, :, pl.ds(pl.multiple_of(lax.div(at, 4) * 128, 128), 128)]
            ids = pltpu.roll(ids, lax.rem(4 - lax.rem(at, 4), 4) * span, 1)
            col = jnp.concatenate([jnp.broadcast_to(ids[:, k : k + 1], (8, 128)) for k in range(span)], axis=0)
            onehot = jnp.concatenate(
                [jnp.where(col == lane + 128 * n, 1.0, 0.0).astype(BF16) for n in range(4)], axis=1
            )
            outs.append(jnp.dot(onehot, table[s], preferred_element_type=F32))

        def pick(shift):
            o = [outs[(n - shift) % 4] for n in range(4)]
            return jnp.where(block == 0, o[0], jnp.where(block == 1, o[1], jnp.where(block == 2, o[2], o[3])))

        to = pl.ds(pl.multiple_of(at * (span * 8) + 16, 8), span * 8)
        xq[to, :] = pick(0)
        xk[to, :] = pltpu.roll(pick(1), 128 - SLICE, 1)
        xv[to, :] = pltpu.roll(pick(2), 128 - 2 * SLICE, 1)
        return carry

    lax.fori_loop(0, STEPS // span, gather, 0)

    chunk = lax.broadcasted_iota(jnp.int32, (8, 128), 0)
    for x in (xq, xk, xv):
        for back in range(2):
            end = x[pl.ds((STEPS + back) * 8, 8), :]
            x[pl.ds(back * 8, 8), :] = jnp.where(chunk == 0, 0.0, pltpu.roll(end, 1, 0))

    def spread(row):
        return jnp.broadcast_to(tiled_lanes(jnp.broadcast_to(row, (8, 128)), b), (8, 128))

    taps = [[spread(taps_ref[s, n : n + 1, here]) for n in range(3)] for s in range(3)]
    poles = [spread(poles_ref[n : n + 1, here]) for n in range(POLES)]
    unroll = 4

    def rows(step):
        return pl.ds(pl.multiple_of(step * 8, 8), 8)

    def forward(at, carry):
        k1, k2, v1, v2, states = carry
        for n in range(unroll):
            step = at * unroll + n
            k0 = xk[rows(step + 2), :]
            v0 = xv[rows(step + 2), :]
            key = taps[1][0] * k0 + taps[1][1] * k1 + taps[1][2] * k2
            value = taps[2][0] * v0 + taps[2][1] * v1 + taps[2][2] * v2
            u = key * value
            product[rows(step), :] = u
            states = tuple(p * s + u for p, s in zip(poles, states))
            k1, k2, v1, v2 = k0, k1, v0, v1
        return k1, k2, v1, v2, states

    zero = jnp.zeros((8, 128), F32)
    states = lax.fori_loop(
        0,
        STEPS // unroll,
        forward,
        (xk[pl.ds(8, 8), :], xk[pl.ds(0, 8), :], xv[pl.ds(8, 8), :], xv[pl.ds(0, 8), :], (zero,) * POLES),
    )[4]

    entry = []
    for p, s in zip(poles, states):
        for _ in range(8):
            p = p * p
        s = jnp.where(chunk == 0, 0.0, pltpu.roll(s, 1, 0))
        for by in (1, 2, 4):
            s = s + p * jnp.where(chunk < by, 0.0, pltpu.roll(s, by, 0))
            p = p * p
        entry.append(s)

    res = [spread(res_ref[n : n + 1, here]) for n in range(POLES)]
    skip = spread(skip_ref[:, here])

    def backward(at, carry):
        q1, q2, states = carry
        for n in range(unroll):
            step = at * unroll + n
            q0 = xq[rows(step + 2), :]
            query = taps[0][0] * q0 + taps[0][1] * q1 + taps[0][2] * q2
            u = product[rows(step), :]
            states = tuple(p * s + u for p, s in zip(poles, states))
            terms = [r * s for r, s in zip(res, states)]
            while len(terms) > 1:
                terms = [a + c for a, c in zip(terms[::2], terms[1::2])]
            mixed[rows(step), :] = query * (terms[0] + skip * u)
            q1, q2 = q0, q1
        return q1, q2, states

    lax.fori_loop(0, STEPS // unroll, backward, (xq[pl.ds(8, 8), :], xq[pl.ds(0, 8), :], tuple(entry)))

    block = lax.div(lax.broadcasted_iota(jnp.int32, (64, 128), 1), SLICE)
    for j in range(CTX):
        quarters = [mixed[pl.ds(n * 512 + j, 64, stride=8), :] for n in range(4)]
        for s in range(4):
            moved = [pltpu.roll(x, (SLICE * (n - s)) % 128, 1) if n != s else x for n, x in enumerate(quarters)]
            piece = jnp.where(
                block == 0, moved[0], jnp.where(block == 1, moved[1], jnp.where(block == 2, moved[2], moved[3]))
            )
            out_ref[j * 4 + s] = piece.astype(BF16)


def convolve(parts, ids, taps, poles, residues, skip):
    vmem = pl.BlockSpec(memory_space=pltpu.VMEM)
    return pl.pallas_call(
        convolve_kernel,
        out_shape=jax.ShapeDtypeStruct((GROUP, 64, 128), BF16),
        in_specs=[vmem] * 6,
        out_specs=vmem,
        scratch_shapes=[
            pltpu.VMEM((4, 512, 128), BF16),
            pltpu.VMEM(((STEPS + 2) * 8, 128), F32),
            pltpu.VMEM(((STEPS + 2) * 8, 128), F32),
            pltpu.VMEM(((STEPS + 2) * 8, 128), F32),
            pltpu.VMEM((STEPS * 8, 128), F32),
            pltpu.VMEM((STEPS * 8, 128), F32),
        ],
        compiler_params=pltpu.CompilerParams(vmem_limit_bytes=32 * 2**20),
        name="convolve",
    )(parts, ids, taps, poles, residues, skip)


def deliver_kernel(pieces_ref, out_ref, landed, send_sem, recv_sem):
    i = lax.axis_index("ctx")
    y = lax.axis_index("fsdp")
    t = lax.axis_index("tp")
    me = i * FSDP + y
    barrier = pltpu.get_barrier_semaphore()

    def greet(other, device):
        pl.semaphore_signal(barrier, inc=1, device_id=device, device_id_type=MESH)

    peers(i, y, t, greet)
    pl.semaphore_wait(barrier, GROUP - 1)

    def copy(other, device):
        return pltpu.make_async_remote_copy(
            src_ref=pieces_ref.at[other], dst_ref=landed.at[me], send_sem=send_sem.at[other], recv_sem=recv_sem.at[me],
            device_id=device, device_id_type=MESH,
        )

    pltpu.make_async_copy(pieces_ref.at[me], landed.at[me], recv_sem.at[me]).start()
    peers(i, y, t, lambda other, device: copy(other, device).start())

    block = lax.div(lax.broadcasted_iota(jnp.int32, (64, 128), 1), SLICE)
    for g in range(CTX):
        for b in range(4):
            pltpu.make_async_copy(landed.at[g * 4 + b], landed.at[g * 4 + b], recv_sem.at[g * 4 + b]).wait()
        got = [landed[g * 4 + b].astype(F32) for b in range(4)]
        for n in range(4):
            moved = [pltpu.roll(x, (SLICE * (b - n)) % 128, 1) if b != n else x for b, x in enumerate(got)]
            tile = jnp.where(
                block == 0, moved[0], jnp.where(block == 1, moved[1], jnp.where(block == 2, moved[2], moved[3]))
            )
            out_ref[pl.ds(n * 64, 64), pl.ds(g * 128, 128)] = tile.astype(BF16)
    peers(i, y, t, lambda other, device: copy(other, device).wait_send())


def deliver(pieces):
    return pl.pallas_call(
        deliver_kernel,
        out_shape=jax.ShapeDtypeStruct((STEPS, CHAN), BF16),
        in_specs=[pl.BlockSpec(memory_space=pl.ANY)],
        out_specs=pl.BlockSpec(memory_space=pltpu.VMEM),
        scratch_shapes=[
            pltpu.VMEM((GROUP, 64, 128), BF16),
            pltpu.SemaphoreType.DMA((GROUP,)),
            pltpu.SemaphoreType.DMA((GROUP,)),
        ],
        compiler_params=pltpu.CompilerParams(collective_id=1, has_side_effects=True),
        name="deliver",
    )(pieces)


def shards(
    base_ids, embed_table, norm_gain, in_weight, conv_taps, modal_poles, residues, skip_gain
):
    weight = jnp.transpose(in_weight, (1, 0, 2))
    parts, ids = project(base_ids, embed_table, norm_gain.reshape(1, -1), weight)
    pieces = convolve(parts, ids, conv_taps, modal_poles, residues, skip_gain.reshape(1, -1))
    return deliver(pieces)[None]


def solution(mesh):
    in_specs = (
        P("fsdp", "ctx"),
        P(None, "tp"),
        P(),
        P("fsdp", None, "tp"),
        P(None, None, "tp"),
        P(None, "tp"),
        P(None, "tp"),
        P("tp"),
    )
    out_specs = P("fsdp", "ctx", "tp")
    return jax.shard_map(shards, mesh=mesh, in_specs=in_specs, out_specs=out_specs, check_vma=False)
```

```python
import jax
import jax.numpy as jnp
from jax import lax
from jax.experimental import pallas as pl
from jax.experimental.pallas import tpu as pltpu
from jax.sharding import PartitionSpec as P

MESH = pl.DeviceIdType.MESH
F32 = jnp.float32
BF16 = jnp.bfloat16
norm_eps = 1e-06

CTX, FSDP, TP = 8, 4, 4
GROUP = CTX * FSDP
VOCAB = 512
ROWS = VOCAB // CTX
FEAT = 2048
CHAN = 1024
SLICE = CHAN // GROUP
STEPS = 256
POLES = 16
CHUNK = 256
CHUNKS = CHAN // CHUNK
SUB = 8


def iota(shape, dim):
    return lax.broadcasted_iota(jnp.int32, shape, dim)


OFFSETS = sorted(
    [(x, z, y) for x in range(4) for z in range(2) for y in range(4) if (x, z, y) != (0, 0, 0)],
    key=lambda o: -(min(o[0], 4 - o[0]) + o[1] + min(o[2], 4 - o[2])),
)


def block_kernel(
    ids_ref, table_ref, gain_ref, weight_ref, taps_ref, poles_ref, res_ref, skip_ref, out_ref,
    weight_buf, own, rows, squares, send_buf, parts, all_ids, gain_buf, taps_buf, poles_buf, res_buf, skip_buf,
    params, kern, kmat, vmat, gmat, onehot, table, product, query, mixed,
    weight_sem, own_sem, small_sem, rows_sem, rows_send, sq_send, sq_recv, ids_send, ids_recv, part_send, part_recv,
    out_send, out_recv,
):
    i = lax.axis_index("ctx")
    y = lax.axis_index("fsdp")
    t = lax.axis_index("tp")
    me = i * FSDP + y
    hi = lax.div(t, 2)
    flip = i + 1 - 2 * lax.rem(i, 2)
    turn = lax.div(i, 2)
    here = pl.ds(pl.multiple_of(i * 128, 128), 128)

    others = []
    for dx, dz, dy in OFFSETS:
        oi = lax.rem(lax.div(i, 2) + dx, 4) * 2 + lax.rem(lax.rem(i, 2) + dz, 2)
        oy = lax.rem(y + dy, FSDP)
        others.append((oi * FSDP + oy, (oi, oy, t)))

    def table_rows(block):
        return table_ref.at[pl.ds(pl.multiple_of(block * ROWS, ROWS), ROWS), :]

    def columns(step):
        return pl.ds(pl.multiple_of(lax.rem(turn + step, CHUNKS) * CHUNK, CHUNK), CHUNK)

    def weight_copy(step):
        return pltpu.make_async_copy(weight_ref.at[:, :, columns(step)], weight_buf.at[step], weight_sem.at[step])

    own_copy = pltpu.make_async_copy(table_rows(i), own, own_sem)
    own_copy.start()
    small = [
        pltpu.make_async_copy(poles_ref, poles_buf, small_sem.at[0]),
        pltpu.make_async_copy(res_ref, res_buf, small_sem.at[1]),
        pltpu.make_async_copy(taps_ref, taps_buf, small_sem.at[2]),
        pltpu.make_async_copy(skip_ref, skip_buf, small_sem.at[3]),
        pltpu.make_async_copy(gain_ref, gain_buf, small_sem.at[4]),
    ]
    for copy in small:
        copy.start()
    for step in range(CHUNKS):
        weight_copy(step).start()

    barrier = pltpu.get_barrier_semaphore()

    def greet(device):
        pl.semaphore_signal(barrier, inc=1, device_id=device, device_id_type=MESH)

    for k in range(1, TP):
        greet((i, y, lax.rem(t + k, TP)))
    for core in range(2):
        greet((flip, y, (1 - hi) * 2 + core))
    for _, device in others:
        greet(device)

    own_copy.wait()
    mine = own[...].astype(F32)
    sums = jnp.sum(mine * mine, axis=1, keepdims=True)
    diagonal = iota((ROWS, 128), 0) == iota((ROWS, 128), 1)
    flat = jnp.sum(jnp.where(diagonal, sums, 0.0), axis=0, keepdims=True)
    squares[t] = jnp.broadcast_to(flat, (8, 128))

    for copy in small:
        copy.wait()
    stacked = jnp.concatenate(
        [poles_buf[:, here], res_buf[:, here]]
        + [taps_buf[s, n : n + 1, here] for s in range(3) for n in range(3)]
        + [skip_buf[:, here], jnp.zeros((128 - 2 * POLES - 10, 128), F32)],
        axis=0,
    )
    params[...] = stacked.T

    lag = iota((SUB, STEPS), 1).astype(F32)
    for g in range(SLICE // SUB):
        block = params[pl.ds(pl.multiple_of(y * SLICE + g * SUB, SUB), SUB), :]
        total = jnp.zeros((SUB, STEPS), F32)
        for n in range(POLES):
            pole = block[:, n : n + 1]
            rate = jnp.log(pole)
            lifted = block[:, POLES + n : POLES + n + 1] * jnp.exp(lag * rate)
            total = total + lifted
            at = pl.ds(n * SUB, SUB)
            gmat[g, at, :] = (lifted * pole).astype(BF16)
            vmat[g, at, :] = jnp.exp((STEPS - 1 - lag) * rate).astype(BF16)
        kern[0, pl.ds(g * SUB, SUB), :] = total[:, :128]
        kern[1, pl.ds(g * SUB, SUB), :] = total[:, 128:]

    row8 = iota((8, 128), 0)
    above = iota((128, 128), 1) >= iota((128, 128), 0)

    def fill(c, carry):
        shifted = []
        for half in range(2):
            x = jnp.broadcast_to(kern[half, pl.ds(c, 1), :], (8, 128))
            for bit in range(3):
                x = jnp.where(lax.rem(lax.div(row8, 2**bit), 2) == 1, pltpu.roll(x, 2**bit, 1), x)
            shifted.append(jnp.concatenate([pltpu.roll(x, 8 * m, 1) if m else x for m in range(16)], axis=0))
        near = jnp.where(above, shifted[0], 0.0).astype(BF16)
        far = jnp.where(above, shifted[1], shifted[0]).astype(BF16)
        kmat[c, pl.ds(0, 128), pl.ds(0, 128)] = near
        kmat[c, pl.ds(0, 128), pl.ds(128, 128)] = far
        kmat[c, pl.ds(128, 128), pl.ds(0, 128)] = jnp.zeros((128, 128), BF16)
        kmat[c, pl.ds(128, 128), pl.ds(128, 128)] = near
        return carry

    lax.fori_loop(0, SLICE, fill, 0)

    pl.semaphore_wait(barrier, TP - 1 + 2 + GROUP - 1)

    def rows_to(block, device, slot):
        return pltpu.make_async_remote_copy(
            src_ref=table_rows(block), dst_ref=rows, send_sem=rows_send.at[slot], recv_sem=rows_sem,
            device_id=device, device_id_type=MESH,
        )

    sibling = hi * 2 + 1 - lax.rem(t, 2)
    keep = pltpu.make_async_copy(table_rows(i), rows, rows_sem)

    @pl.when(t == y)
    def _():
        for core in range(2):
            rows_to(flip, (flip, y, (1 - hi) * 2 + core), core).start()
        rows_to(i, (i, y, sibling), 2).start()
        keep.start()

    def squares_to(k):
        return pltpu.make_async_remote_copy(
            src_ref=squares.at[t], dst_ref=squares.at[t], send_sem=sq_send.at[k], recv_sem=sq_recv.at[t],
            device_id=(i, y, lax.rem(t + k, TP)), device_id_type=MESH,
        )

    for k in range(1, TP):
        squares_to(k).start()

    def ids_to(other, device):
        return pltpu.make_async_remote_copy(
            src_ref=ids_ref, dst_ref=all_ids.at[y, pl.ds(i, 1), :], send_sem=ids_send.at[other],
            recv_sem=ids_recv.at[me], device_id=device, device_id_type=MESH,
        )

    pltpu.make_async_copy(ids_ref, all_ids.at[y, pl.ds(i, 1), :], ids_recv.at[me]).start()
    for other, device in others:
        ids_to(other, device).start()

    for k in range(1, TP):
        source = lax.rem(t + k, TP)
        pltpu.make_async_copy(squares.at[source], squares.at[source], sq_recv.at[source]).wait()
    total = squares[0] + squares[1] + squares[2] + squares[3]
    scale = lax.rsqrt(total[0:1, :] * (1.0 / (FEAT * FSDP)) + norm_eps)
    scale = jnp.sum(jnp.where(diagonal, scale, 0.0), axis=1, keepdims=True)

    keep.wait()
    gain = gain_buf[:, pl.ds(pl.multiple_of(y * FEAT, FEAT), FEAT)]
    normed = (rows[...].astype(F32) * scale * gain).astype(BF16)

    lane_block = lax.div(iota((48, 128), 1), SLICE)

    def part_to(slot, device):
        return pltpu.make_async_remote_copy(
            src_ref=send_buf.at[slot], dst_ref=parts.at[me], send_sem=part_send.at[slot], recv_sem=part_recv.at[me],
            device_id=device, device_id_type=MESH,
        )

    for step in range(CHUNKS):
        weight_copy(step).wait()
        dots = [jnp.dot(normed, weight_buf[step, stream], preferred_element_type=F32) for stream in range(3)]
        for half in range(CHUNK // 128):
            cols = [dot[:, half * 128 : half * 128 + 128] for dot in dots]
            for b in range(4):
                base = [pltpu.roll(c, (32 * (s - b)) % 128, 1) if (s - b) % 4 else c for s, c in enumerate(cols)]
                tail = jnp.concatenate(
                    [pltpu.roll(c[48:64], (32 * (3 - b)) % 128, 1) if (3 - b) % 4 else c[48:64] for c in cols], axis=0
                )
                piece = jnp.where(
                    lane_block == 0,
                    base[0][:48],
                    jnp.where(lane_block == 1, base[1][:48], jnp.where(lane_block == 2, base[2][:48], tail)),
                )
                send_buf[step * 8 + half * 4 + b] = piece.astype(BF16)
        first = lax.rem(turn + step, CHUNKS) * 8
        for k in range(8):
            other = first + k
            slot = step * 8 + k

            @pl.when(other == me)
            def _():
                pltpu.make_async_copy(send_buf.at[slot], parts.at[me], part_recv.at[me]).start()

            @pl.when(other != me)
            def _():
                part_to(slot, (lax.div(other, FSDP), lax.rem(other, FSDP), t)).start()

    vocab_row = iota((VOCAB, STEPS), 0)

    def hot(s, carry):
        for j in range(CTX):
            landed = all_ids.at[s, pl.ds(j, 1), :]
            pltpu.make_async_copy(ids_ref, landed, ids_recv.at[j * FSDP + s]).wait()
            row = all_ids[s, pl.ds(j, 1), :]
            onehot[s * CTX + j] = jnp.where(vocab_row == row, 1.0, 0.0).astype(BF16)
        return carry

    lax.fori_loop(0, FSDP, hot, 0)

    block16 = lax.div(iota((16, 128), 1), SLICE)
    for v in range(CTX):
        for k in range(4):
            pltpu.make_async_copy(parts.at[v * 4 + k], parts.at[v * 4 + k], part_recv.at[v * 4 + k]).wait()
        a = parts[v * 4].astype(F32)
        for k in range(1, 4):
            a = a + parts[v * 4 + k].astype(F32)
        tail = [pltpu.roll(a[16 * s : 16 * s + 16], SLICE * (s + 1), 1) for s in range(3)]
        last = jnp.where(block16 == 0, tail[0], jnp.where(block16 == 1, tail[1], tail[2]))
        mixed[0, pl.ds(v * ROWS, 48), :] = a
        mixed[0, pl.ds(v * ROWS + 48, 16), :] = last
    for v in range(VOCAB // 128):
        turned = mixed[0, pl.ds(v * 128, 128), :].T
        table[:, pl.ds(v * 128, 128)] = turned[: 3 * SLICE].astype(BF16)

    mine_params = params[pl.ds(pl.multiple_of(y * SLICE, SLICE), SLICE), :]
    taps = [
        jnp.concatenate(
            [
                jnp.broadcast_to(mine_params[:, 2 * POLES + 3 * s + n : 2 * POLES + 3 * s + n + 1], (SLICE, 128))
                for s in range(3)
            ],
            axis=0,
        )
        for n in range(3)
    ]
    lane = iota((3 * SLICE, 128), 1)

    def sequence(s, carry):
        before = jnp.zeros((3 * SLICE, 128), F32)
        for j in range(CTX):
            at = s * CTX + j
            proj = jnp.dot(table[...], onehot[at], preferred_element_type=F32)
            for half in range(2):
                now = proj[:, half * 128 : half * 128 + 128]
                done = taps[0] * now
                for n in range(1, 3):
                    done = done + taps[n] * jnp.where(lane < n, pltpu.roll(before, n, 1), pltpu.roll(now, n, 1))
                before = now
                to = pl.ds(pl.multiple_of(at * SLICE, SLICE), SLICE)
                query[half, to, :] = done[:SLICE]
                product[half, to, :] = done[SLICE : 2 * SLICE] * done[2 * SLICE :]
        return carry

    lax.fori_loop(0, FSDP, sequence, 0)

    same = lax.div(iota((SUB * GROUP, 128), 0), GROUP) == lax.rem(iota((SUB * GROUP, 128), 1), SUB)
    chunk = lax.rem(iota((SUB * GROUP, 128), 0), CTX)
    diagonal128 = iota((128, 128), 0) == iota((128, 128), 1)

    def convolve(g, carry):
        inputs, inner = [], []
        for k in range(SUB):
            every = pl.ds(g * SUB + k, GROUP, stride=SLICE)
            x = jnp.concatenate([product[half, every, :] for half in range(2)], axis=1).astype(BF16)
            inputs.append(x)
            inner.append(jnp.dot(x, kmat[g * SUB + k], preferred_element_type=F32))
        states = lax.dot_general(
            jnp.concatenate(inputs, axis=0), vmat[g], (((1,), (1,)), ((), ())), preferred_element_type=F32
        )
        states = jnp.where(same, states, 0.0)
        block = params[pl.ds(pl.multiple_of(y * SLICE + g * SUB, SUB), SUB), :]
        decay = jnp.concatenate(
            [jnp.broadcast_to(block[:, n : n + 1], (SUB, 128)) for n in range(POLES)], axis=0
        )
        decay = jnp.sum(jnp.where(diagonal128, decay, 0.0), axis=0, keepdims=True)
        for _ in range(8):
            decay = decay * decay
        states = jnp.where(chunk < 1, 0.0, pltpu.roll(states, 1, 0))
        for by in (1, 2, 4):
            states = states + decay * jnp.where(chunk < by, 0.0, pltpu.roll(states, by, 0))
            decay = decay * decay
        carried = jnp.dot(states.astype(BF16), gmat[g], preferred_element_type=F32)
        for k in range(SUB):
            every = pl.ds(g * SUB + k, GROUP, stride=SLICE)
            x = inner[k] + carried[k * GROUP : (k + 1) * GROUP]
            for half in range(2):
                mixed[half, every, :] = x[:, half * 128 : half * 128 + 128]
        return carry

    lax.fori_loop(0, SLICE // SUB, convolve, 0)

    skip = mine_params[:, 2 * POLES + 9 : 2 * POLES + 10]
    pieces = onehot

    def out_to(other, device):
        return pltpu.make_async_remote_copy(
            src_ref=pieces.at[other, pl.ds(0, SLICE), :], dst_ref=out_ref.at[me], send_sem=out_send.at[other],
            recv_sem=out_recv.at[me], device_id=device, device_id_type=MESH,
        )

    def gate(other):
        s = lax.rem(other, FSDP)
        j = lax.div(other, FSDP)
        at = pl.ds(pl.multiple_of((s * CTX + j) * SLICE, SLICE), SLICE)
        for half in range(2):
            x = query[half, at, :] * (mixed[half, at, :] + skip * product[half, at, :])
            pieces[other, pl.ds(0, SLICE), pl.ds(half * 128, 128)] = x.astype(BF16)

    for other, device in others:
        gate(other)
        out_to(other, device).start()
    gate(me)
    pltpu.make_async_copy(pieces.at[me, pl.ds(0, SLICE), :], out_ref.at[me], out_recv.at[me]).start()

    for k in range(1, TP):
        squares_to(k).wait_send()

    @pl.when(t == y)
    def _():
        for slot in range(3):
            rows_to(i, (i, y, sibling), slot).wait_send()

    for step in range(CHUNKS):
        first = lax.rem(turn + step, CHUNKS) * 8
        for k in range(8):

            @pl.when(first + k != me)
            def _():
                part_to(step * 8 + k, (i, y, t)).wait_send()

    for other, device in others:
        ids_to(other, device).wait_send()
        out_to(other, device).wait_send()

    def arrive(src, carry):
        pltpu.make_async_copy(out_ref.at[src], out_ref.at[src], out_recv.at[src]).wait()
        return carry

    lax.fori_loop(0, GROUP, arrive, 0)


def block(*args):
    hbm = pl.BlockSpec(memory_space=pltpu.HBM)
    dma = pltpu.SemaphoreType.DMA
    groups = SLICE // SUB
    return pl.pallas_call(
        block_kernel,
        out_shape=jax.ShapeDtypeStruct((GROUP, SLICE, STEPS), BF16),
        in_specs=[hbm] * 8,
        out_specs=hbm,
        scratch_shapes=[
            pltpu.VMEM((CHUNKS, 3, FEAT, CHUNK), BF16),
            pltpu.VMEM((ROWS, FEAT), BF16),
            pltpu.VMEM((ROWS, FEAT), BF16),
            pltpu.VMEM((TP, 8, 128), F32),
            pltpu.VMEM((GROUP, 48, 128), BF16),
            pltpu.VMEM((GROUP, 48, 128), BF16),
            pltpu.VMEM((FSDP, CTX, STEPS), jnp.int32),
            pltpu.VMEM((1, FEAT * FSDP), F32),
            pltpu.VMEM((3, 3, CHAN), F32),
            pltpu.VMEM((POLES, CHAN), F32),
            pltpu.VMEM((POLES, CHAN), F32),
            pltpu.VMEM((1, CHAN), F32),
            pltpu.VMEM((128, 128), F32),
            pltpu.VMEM((2, SLICE, 128), F32),
            pltpu.VMEM((SLICE, STEPS, STEPS), BF16),
            pltpu.VMEM((groups, POLES * SUB, STEPS), BF16),
            pltpu.VMEM((groups, POLES * SUB, STEPS), BF16),
            pltpu.VMEM((GROUP, VOCAB, STEPS), BF16),
            pltpu.VMEM((3 * SLICE, VOCAB), BF16),
            pltpu.VMEM((2, GROUP * SLICE, 128), F32),
            pltpu.VMEM((2, GROUP * SLICE, 128), F32),
            pltpu.VMEM((2, GROUP * SLICE, 128), F32),
            dma((CHUNKS,)),
            dma,
            dma((5,)),
            dma,
            dma((3,)),
            dma((TP,)),
            dma((TP,)),
            dma((GROUP,)),
            dma((GROUP,)),
            dma((GROUP,)),
            dma((GROUP,)),
            dma((GROUP,)),
            dma((GROUP,)),
        ],
        compiler_params=pltpu.CompilerParams(
            collective_id=0, has_side_effects=True, vmem_limit_bytes=56 * 2**20
        ),
        name="hyena_block",
    )(*args)


def shards(
    base_ids, embed_table, norm_gain, in_weight, conv_taps, modal_poles, residues, skip_gain
):
    landed = block(
        base_ids, embed_table, norm_gain.reshape(1, -1), jnp.transpose(in_weight, (1, 0, 2)),
        conv_taps, modal_poles, residues, skip_gain.reshape(1, -1),
    )
    return landed.reshape(CHAN, STEPS).T[None]


def solution(mesh):
    in_specs = (
        P("fsdp", "ctx"),
        P(None, "tp"),
        P(),
        P("fsdp", None, "tp"),
        P(None, None, "tp"),
        P(None, "tp"),
        P(None, "tp"),
        P("tp"),
    )
    out_specs = P("fsdp", "ctx", "tp")
    return jax.shard_map(shards, mesh=mesh, in_specs=in_specs, out_specs=out_specs, check_vma=False)
```

```python
import jax
import jax.numpy as jnp
from jax import lax
from jax.experimental import pallas as pl
from jax.experimental.pallas import tpu as pltpu
from jax.sharding import PartitionSpec as P

MESH = pl.DeviceIdType.MESH
F32 = jnp.float32
BF16 = jnp.bfloat16
norm_eps = 1e-06

CTX, FSDP, TP = 8, 4, 4
GROUP = CTX * FSDP
VOCAB = 512
ROWS = VOCAB // CTX
FEAT = 2048
CHAN = 1024
SLICE = CHAN // GROUP
STEPS = 256
POLES = 16
CHUNK = 256
CHUNKS = CHAN // CHUNK
SUB = 8


def iota(shape, dim):
    return lax.broadcasted_iota(jnp.int32, shape, dim)


OFFSETS = sorted(
    [(x, z, y) for x in range(4) for z in range(2) for y in range(4) if (x, z, y) != (0, 0, 0)],
    key=lambda o: -(min(o[0], 4 - o[0]) + o[1] + min(o[2], 4 - o[2])),
)


def block_kernel(
    ids_ref, table_ref, gain_ref, weight_ref, taps_ref, poles_ref, res_ref, skip_ref, out_ref,
    weight_buf, own, rows, squares, send_buf, parts, all_ids, gain_buf, taps_buf, poles_buf, res_buf, skip_buf,
    params, kern, kmat, vmat, gmat, onehot, table, product, query, mixed,
    weight_sem, own_sem, small_sem, rows_sem, rows_send, sq_send, sq_recv, ids_send, ids_recv, part_send, part_recv,
    out_send, out_recv,
):
    i = lax.axis_index("ctx")
    y = lax.axis_index("fsdp")
    t = lax.axis_index("tp")
    me = i * FSDP + y
    hi = lax.div(t, 2)
    flip = i + 1 - 2 * lax.rem(i, 2)
    turn = lax.div(i, 2)
    here = pl.ds(pl.multiple_of(i * 128, 128), 128)

    others = []
    for dx, dz, dy in OFFSETS:
        oi = lax.rem(lax.div(i, 2) + dx, 4) * 2 + lax.rem(lax.rem(i, 2) + dz, 2)
        oy = lax.rem(y + dy, FSDP)
        others.append((oi * FSDP + oy, (oi, oy, t)))

    def table_rows(block):
        return table_ref.at[pl.ds(pl.multiple_of(block * ROWS, ROWS), ROWS), :]

    def columns(step):
        return pl.ds(pl.multiple_of(lax.rem(turn + step, CHUNKS) * CHUNK, CHUNK), CHUNK)

    def weight_copy(step):
        return pltpu.make_async_copy(weight_ref.at[:, :, columns(step)], weight_buf.at[step], weight_sem.at[step])

    own_copy = pltpu.make_async_copy(table_rows(i), own, own_sem)
    own_copy.start()
    small = [
        pltpu.make_async_copy(poles_ref, poles_buf, small_sem.at[0]),
        pltpu.make_async_copy(res_ref, res_buf, small_sem.at[1]),
        pltpu.make_async_copy(taps_ref, taps_buf, small_sem.at[2]),
        pltpu.make_async_copy(skip_ref, skip_buf, small_sem.at[3]),
        pltpu.make_async_copy(gain_ref, gain_buf, small_sem.at[4]),
    ]
    for copy in small:
        copy.start()
    for step in range(CHUNKS):
        weight_copy(step).start()

    barrier = pltpu.get_barrier_semaphore()

    def greet(device):
        pl.semaphore_signal(barrier, inc=1, device_id=device, device_id_type=MESH)

    for k in range(1, TP):
        greet((i, y, lax.rem(t + k, TP)))
    for core in range(2):
        greet((flip, y, (1 - hi) * 2 + core))
    for _, device in others:
        greet(device)

    own_copy.wait()
    mine = own[...].astype(F32)
    sums = jnp.sum(mine * mine, axis=1, keepdims=True)
    diagonal = iota((ROWS, 128), 0) == iota((ROWS, 128), 1)
    flat = jnp.sum(jnp.where(diagonal, sums, 0.0), axis=0, keepdims=True)
    squares[t] = jnp.broadcast_to(flat, (8, 128))

    for copy in small:
        copy.wait()
    stacked = jnp.concatenate(
        [poles_buf[:, here], res_buf[:, here]]
        + [taps_buf[s, n : n + 1, here] for s in range(3) for n in range(3)]
        + [skip_buf[:, here], jnp.zeros((128 - 2 * POLES - 10, 128), F32)],
        axis=0,
    )
    params[...] = stacked.T

    pl.semaphore_wait(barrier, TP - 1 + 2 + GROUP - 1)

    half_rows = ROWS // 2
    core = lax.rem(t, 2)
    sibling = hi * 2 + 1 - core
    home = lax.div(y, 2)

    def table_half(block, half):
        return table_ref.at[pl.ds(pl.multiple_of(block * ROWS + half * half_rows, half_rows), half_rows), :]

    def rows_half(half):
        return rows.at[pl.ds(pl.multiple_of(half * half_rows, half_rows), half_rows), :]

    def half_to(source, half, device, slot):
        return pltpu.make_async_remote_copy(
            src_ref=source, dst_ref=rows_half(half), send_sem=rows_send.at[slot], recv_sem=rows_sem.at[half],
            device_id=device, device_id_type=MESH,
        )

    def arrived(half):
        return pltpu.make_async_copy(rows_half(half), rows_half(half), rows_sem.at[half])

    handed = [
        half_to(table_half(flip, half), half, (flip, y, (1 - hi) * 2 + half), half) for half in range(2)
    ] + [half_to(table_half(i, half), half, (i, y, sibling), 2 + half) for half in range(2)]
    forward = half_to(rows_half(core), core, (i, y, sibling), 0)

    @pl.when(t == y)
    def _():
        for copy in handed:
            copy.start()
        for half in range(2):
            pltpu.make_async_copy(table_half(i, half), rows_half(half), rows_sem.at[half]).start()

    def squares_to(k):
        return pltpu.make_async_remote_copy(
            src_ref=squares.at[t], dst_ref=squares.at[t], send_sem=sq_send.at[k], recv_sem=sq_recv.at[t],
            device_id=(i, y, lax.rem(t + k, TP)), device_id_type=MESH,
        )

    for k in range(1, TP):
        squares_to(k).start()

    def ids_to(other, device):
        return pltpu.make_async_remote_copy(
            src_ref=ids_ref, dst_ref=all_ids.at[y, pl.ds(i, 1), :], send_sem=ids_send.at[other],
            recv_sem=ids_recv.at[me], device_id=device, device_id_type=MESH,
        )

    pltpu.make_async_copy(ids_ref, all_ids.at[y, pl.ds(i, 1), :], ids_recv.at[me]).start()
    for other, device in others:
        ids_to(other, device).start()

    lag = iota((SUB, STEPS), 1).astype(F32)
    for g in range(SLICE // SUB):
        block = params[pl.ds(pl.multiple_of(y * SLICE + g * SUB, SUB), SUB), :]
        rates = jnp.log(block)
        total = jnp.zeros((SUB, STEPS), F32)
        for n in range(POLES):
            rate = rates[:, n : n + 1]
            lifted = block[:, POLES + n : POLES + n + 1] * jnp.exp(lag * rate)
            total = total + lifted
            at = pl.ds(n * SUB, SUB)
            gmat[g, at, :] = (lifted * block[:, n : n + 1]).astype(BF16)
            vmat[g, at, :] = jnp.exp((STEPS - 1 - lag) * rate).astype(BF16)
        kern[0, pl.ds(g * SUB, SUB), :] = total[:, :128]
        kern[1, pl.ds(g * SUB, SUB), :] = total[:, 128:]

    odd = [lax.rem(lax.div(iota((8, 128), 0), 2**bit), 2) == 1 for bit in range(3)]
    above = iota((128, 128), 1) >= iota((128, 128), 0)

    def fill(g, carry):
        block = pl.ds(pl.multiple_of(g * SUB, SUB), SUB)
        lags = [kern[half, block, :] for half in range(2)]
        bases = [[jnp.broadcast_to(x[k : k + 1], (8, 128)) for x in lags] for k in range(SUB)]
        for bit in range(3):
            bases = [[jnp.where(odd[bit], pltpu.roll(x, 2**bit, 1), x) for x in pair] for pair in bases]
        for k in range(SUB):
            shifted = [
                jnp.concatenate([pltpu.roll(x, 8 * m, 1) if m else x for m in range(16)], axis=0) for x in bases[k]
            ]
            kmat[g * SUB + k, :, pl.ds(0, 128)] = jnp.where(above, shifted[0], 0.0).astype(BF16)
            kmat[g * SUB + k, :, pl.ds(128, 128)] = jnp.where(above, shifted[1], shifted[0]).astype(BF16)
        return carry

    lax.fori_loop(0, SLICE // SUB // 2, fill, 0)

    @pl.when(hi != home)
    def _():
        arrived(core).wait()
        forward.start()

    for k in range(1, TP):
        source = lax.rem(t + k, TP)
        pltpu.make_async_copy(squares.at[source], squares.at[source], sq_recv.at[source]).wait()
    total = squares[0] + squares[1] + squares[2] + squares[3]
    scale = lax.rsqrt(total[0:1, :] * (1.0 / (FEAT * FSDP)) + norm_eps)
    scale = jnp.sum(jnp.where(diagonal, scale, 0.0), axis=1, keepdims=True)

    @pl.when(hi == home)
    def _():
        arrived(core).wait()

    arrived(1 - core).wait()
    gain = gain_buf[:, pl.ds(pl.multiple_of(y * FEAT, FEAT), FEAT)]
    normed = (rows[...].astype(F32) * scale * gain).astype(BF16)

    lane_block = lax.div(iota((48, 128), 1), SLICE)

    def part_to(slot, device):
        return pltpu.make_async_remote_copy(
            src_ref=send_buf.at[slot], dst_ref=parts.at[me], send_sem=part_send.at[slot], recv_sem=part_recv.at[me],
            device_id=device, device_id_type=MESH,
        )

    for step in range(CHUNKS):
        weight_copy(step).wait()
        dots = [jnp.dot(normed, weight_buf[step, stream], preferred_element_type=F32) for stream in range(3)]
        for half in range(CHUNK // 128):
            cols = [dot[:, half * 128 : half * 128 + 128] for dot in dots]
            for b in range(4):
                base = [pltpu.roll(c, (32 * (s - b)) % 128, 1) if (s - b) % 4 else c for s, c in enumerate(cols)]
                tail = jnp.concatenate(
                    [pltpu.roll(c[48:64], (32 * (3 - b)) % 128, 1) if (3 - b) % 4 else c[48:64] for c in cols], axis=0
                )
                piece = jnp.where(
                    lane_block == 0,
                    base[0][:48],
                    jnp.where(lane_block == 1, base[1][:48], jnp.where(lane_block == 2, base[2][:48], tail)),
                )
                send_buf[step * 8 + half * 4 + b] = piece.astype(BF16)
        first = lax.rem(turn + step, CHUNKS) * 8
        for k in range(8):
            other = first + k
            slot = step * 8 + k

            @pl.when(other == me)
            def _():
                pltpu.make_async_copy(send_buf.at[slot], parts.at[me], part_recv.at[me]).start()

            @pl.when(other != me)
            def _():
                part_to(slot, (lax.div(other, FSDP), lax.rem(other, FSDP), t)).start()

    vocab_row = iota((VOCAB // 2, STEPS), 0)

    def hot(s, carry):
        for j in range(CTX):
            landed = all_ids.at[s, pl.ds(j, 1), :]
            pltpu.make_async_copy(ids_ref, landed, ids_recv.at[j * FSDP + s]).wait()
            row = all_ids[s, pl.ds(j, 1), :]
            low = jnp.where(row >= VOCAB // 2, row - VOCAB // 2, row)
            onehot[s * CTX + j] = jnp.where(vocab_row == low, 1.0, 0.0).astype(BF16)
        return carry

    lax.fori_loop(SLICE // SUB // 2, SLICE // SUB, fill, 0)
    lax.fori_loop(0, FSDP, hot, 0)

    block16 = lax.div(iota((16, 128), 1), SLICE)
    for v in range(CTX):
        for k in range(4):
            pltpu.make_async_copy(parts.at[v * 4 + k], parts.at[v * 4 + k], part_recv.at[v * 4 + k]).wait()
        a = parts[v * 4].astype(F32)
        for k in range(1, 4):
            a = a + parts[v * 4 + k].astype(F32)
        tail = [pltpu.roll(a[16 * s : 16 * s + 16], SLICE * (s + 1), 1) for s in range(3)]
        last = jnp.where(block16 == 0, tail[0], jnp.where(block16 == 1, tail[1], tail[2]))
        mixed[0, pl.ds(v * ROWS, 48), :] = a
        mixed[0, pl.ds(v * ROWS + 48, 16), :] = last
    for v in range(VOCAB // 128):
        turned = mixed[0, pl.ds(v * 128, 128), :].T
        to = pl.ds(v // 2 * 3 * SLICE, 3 * SLICE)
        table[to, pl.ds(v % 2 * 128, 128)] = turned[: 3 * SLICE].astype(BF16)

    mine_params = params[pl.ds(pl.multiple_of(y * SLICE, SLICE), SLICE), :]
    taps = [
        jnp.concatenate(
            [
                jnp.broadcast_to(mine_params[:, 2 * POLES + 3 * s + n : 2 * POLES + 3 * s + n + 1], (SLICE, 128))
                for s in range(3)
            ],
            axis=0,
        )
        for n in range(3)
    ]
    lane = iota((3 * SLICE, 128), 1)

    def sequence(s, carry):
        before = jnp.zeros((3 * SLICE, 128), F32)
        for j in range(CTX):
            at = s * CTX + j
            both = jnp.dot(table[...], onehot[at], preferred_element_type=F32)
            upper = all_ids[s, pl.ds(j, 1), :] >= VOCAB // 2
            for half in range(2):
                cols = slice(half * 128, half * 128 + 128)
                now = jnp.where(upper[:, cols], both[3 * SLICE :, cols], both[: 3 * SLICE, cols])
                done = taps[0] * now
                for n in range(1, 3):
                    done = done + taps[n] * jnp.where(lane < n, pltpu.roll(before, n, 1), pltpu.roll(now, n, 1))
                before = now
                to = pl.ds(pl.multiple_of(at * SLICE, SLICE), SLICE)
                query[half, to, :] = done[:SLICE]
                product[half, to, :] = done[SLICE : 2 * SLICE] * done[2 * SLICE :]
        return carry

    lax.fori_loop(0, FSDP, sequence, 0)

    same = lax.div(iota((SUB * GROUP, 128), 0), GROUP) == lax.rem(iota((SUB * GROUP, 128), 1), SUB)
    chunk = lax.rem(iota((SUB * GROUP, 128), 0), CTX)
    diagonal128 = iota((128, 128), 0) == iota((128, 128), 1)

    def convolve(g, carry):
        inputs, inner = [], []
        for k in range(SUB):
            every = pl.ds(g * SUB + k, GROUP, stride=SLICE)
            x = [product[half, every, :].astype(BF16) for half in range(2)]
            inputs.append(jnp.concatenate(x, axis=1))
            both = jnp.dot(jnp.concatenate(x, axis=0), kmat[g * SUB + k], preferred_element_type=F32)
            inner.append([both[:GROUP, :128], both[:GROUP, 128:] + both[GROUP:, :128]])
        states = lax.dot_general(
            jnp.concatenate(inputs, axis=0), vmat[g], (((1,), (1,)), ((), ())), preferred_element_type=F32
        )
        states = jnp.where(same, states, 0.0)
        block = params[pl.ds(pl.multiple_of(y * SLICE + g * SUB, SUB), SUB), :]
        decay = jnp.concatenate(
            [jnp.broadcast_to(block[:, n : n + 1], (SUB, 128)) for n in range(POLES)], axis=0
        )
        decay = jnp.sum(jnp.where(diagonal128, decay, 0.0), axis=0, keepdims=True)
        for _ in range(8):
            decay = decay * decay
        states = jnp.where(chunk < 1, 0.0, pltpu.roll(states, 1, 0))
        for by in (1, 2, 4):
            states = states + decay * jnp.where(chunk < by, 0.0, pltpu.roll(states, by, 0))
            decay = decay * decay
        carried = jnp.dot(states.astype(BF16), gmat[g], preferred_element_type=F32)
        for k in range(SUB):
            every = pl.ds(g * SUB + k, GROUP, stride=SLICE)
            for half in range(2):
                mixed[half, every, :] = (
                    inner[k][half] + carried[k * GROUP : (k + 1) * GROUP, half * 128 : half * 128 + 128]
                )
        return carry

    lax.fori_loop(0, SLICE // SUB, convolve, 0)

    skip = mine_params[:, 2 * POLES + 9 : 2 * POLES + 10]
    pieces = onehot

    def out_to(other, device):
        return pltpu.make_async_remote_copy(
            src_ref=pieces.at[other, pl.ds(0, SLICE), :], dst_ref=out_ref.at[me], send_sem=out_send.at[other],
            recv_sem=out_recv.at[me], device_id=device, device_id_type=MESH,
        )

    def gate(other):
        s = lax.rem(other, FSDP)
        j = lax.div(other, FSDP)
        at = pl.ds(pl.multiple_of((s * CTX + j) * SLICE, SLICE), SLICE)
        for half in range(2):
            x = query[half, at, :] * (mixed[half, at, :] + skip * product[half, at, :])
            pieces[other, pl.ds(0, SLICE), pl.ds(half * 128, 128)] = x.astype(BF16)

    for other, device in others:
        gate(other)
        out_to(other, device).start()
    gate(me)
    pltpu.make_async_copy(pieces.at[me, pl.ds(0, SLICE), :], out_ref.at[me], out_recv.at[me]).start()

    for k in range(1, TP):
        squares_to(k).wait_send()

    @pl.when(t == y)
    def _():
        for copy in handed:
            copy.wait_send()

    @pl.when(hi != home)
    def _():
        forward.wait_send()

    for step in range(CHUNKS):
        first = lax.rem(turn + step, CHUNKS) * 8
        for k in range(8):

            @pl.when(first + k != me)
            def _():
                part_to(step * 8 + k, (i, y, t)).wait_send()

    for other, device in others:
        ids_to(other, device).wait_send()
        out_to(other, device).wait_send()

    def arrive(src, carry):
        pltpu.make_async_copy(out_ref.at[src], out_ref.at[src], out_recv.at[src]).wait()
        return carry

    lax.fori_loop(0, GROUP, arrive, 0)


def block(*args):
    hbm = pl.BlockSpec(memory_space=pltpu.HBM)
    dma = pltpu.SemaphoreType.DMA
    groups = SLICE // SUB
    return pl.pallas_call(
        block_kernel,
        out_shape=jax.ShapeDtypeStruct((GROUP, SLICE, STEPS), BF16),
        in_specs=[hbm] * 8,
        out_specs=hbm,
        scratch_shapes=[
            pltpu.VMEM((CHUNKS, 3, FEAT, CHUNK), BF16),
            pltpu.VMEM((ROWS, FEAT), BF16),
            pltpu.VMEM((ROWS, FEAT), BF16),
            pltpu.VMEM((TP, 8, 128), F32),
            pltpu.VMEM((GROUP, 48, 128), BF16),
            pltpu.VMEM((GROUP, 48, 128), BF16),
            pltpu.VMEM((FSDP, CTX, STEPS), jnp.int32),
            pltpu.VMEM((1, FEAT * FSDP), F32),
            pltpu.VMEM((3, 3, CHAN), F32),
            pltpu.VMEM((POLES, CHAN), F32),
            pltpu.VMEM((POLES, CHAN), F32),
            pltpu.VMEM((1, CHAN), F32),
            pltpu.VMEM((128, 128), F32),
            pltpu.VMEM((2, SLICE, 128), F32),
            pltpu.VMEM((SLICE, STEPS // 2, STEPS), BF16),
            pltpu.VMEM((groups, POLES * SUB, STEPS), BF16),
            pltpu.VMEM((groups, POLES * SUB, STEPS), BF16),
            pltpu.VMEM((GROUP, VOCAB // 2, STEPS), BF16),
            pltpu.VMEM((6 * SLICE, VOCAB // 2), BF16),
            pltpu.VMEM((2, GROUP * SLICE, 128), F32),
            pltpu.VMEM((2, GROUP * SLICE, 128), F32),
            pltpu.VMEM((2, GROUP * SLICE, 128), F32),
            dma((CHUNKS,)),
            dma,
            dma((5,)),
            dma((2,)),
            dma((4,)),
            dma((TP,)),
            dma((TP,)),
            dma((GROUP,)),
            dma((GROUP,)),
            dma((GROUP,)),
            dma((GROUP,)),
            dma((GROUP,)),
            dma((GROUP,)),
        ],
        compiler_params=pltpu.CompilerParams(
            collective_id=0, has_side_effects=True, vmem_limit_bytes=56 * 2**20
        ),
        name="hyena_block",
    )(*args)


def shards(
    base_ids, embed_table, norm_gain, in_weight, conv_taps, modal_poles, residues, skip_gain
):
    landed = block(
        base_ids, embed_table, norm_gain.reshape(1, -1), jnp.transpose(in_weight, (1, 0, 2)),
        conv_taps, modal_poles, residues, skip_gain.reshape(1, -1),
    )
    return landed.reshape(CHAN, STEPS).T[None]


def solution(mesh):
    in_specs = (
        P("fsdp", "ctx"),
        P(None, "tp"),
        P(),
        P("fsdp", None, "tp"),
        P(None, None, "tp"),
        P(None, "tp"),
        P(None, "tp"),
        P("tp"),
    )
    out_specs = P("fsdp", "ctx", "tp")
    return jax.shard_map(shards, mesh=mesh, in_specs=in_specs, out_specs=out_specs, check_vma=False)
```

```python
import jax
import jax.numpy as jnp
from jax import lax
from jax.experimental import pallas as pl
from jax.experimental.pallas import tpu as pltpu
from jax.sharding import PartitionSpec as P

MESH = pl.DeviceIdType.MESH
F32 = jnp.float32
BF16 = jnp.bfloat16
norm_eps = 1e-06

CTX, FSDP, TP = 8, 4, 4
GROUP = CTX * FSDP
VOCAB = 512
ROWS = VOCAB // CTX
FEAT = 2048
CHAN = 1024
SLICE = CHAN // GROUP
STEPS = 256
POLES = 16
CHUNK = 256
CHUNKS = CHAN // CHUNK
SUB = 8


def iota(shape, dim):
    return lax.broadcasted_iota(jnp.int32, shape, dim)


OFFSETS = sorted(
    [(x, z, y) for x in range(4) for z in range(2) for y in range(4) if (x, z, y) != (0, 0, 0)],
    key=lambda o: -(min(o[0], 4 - o[0]) + o[1] + min(o[2], 4 - o[2])),
)


def block_kernel(
    ids_ref, table_ref, gain_ref, weight_ref, taps_ref, poles_ref, res_ref, skip_ref, out_ref,
    weight_buf, own, rows, squares, send_buf, parts, all_ids, gain_buf, taps_buf, poles_buf, res_buf, skip_buf,
    params, kern, kmat, vmat, gmat, onehot, table, whole, raw, product, query, mixed,
    weight_sem, own_sem, small_sem, rows_sem, rows_send, sq_send, sq_recv, ids_send, ids_recv, part_send, part_recv,
    out_send, out_recv,
):
    i = lax.axis_index("ctx")
    y = lax.axis_index("fsdp")
    t = lax.axis_index("tp")
    me = i * FSDP + y
    hi = lax.div(t, 2)
    flip = i + 1 - 2 * lax.rem(i, 2)
    turn = [lax.rem(lax.div(i, 2) + x, CHUNKS) for x in (2, 1, 3, 0)]
    here = pl.ds(pl.multiple_of(i * 128, 128), 128)

    others = []
    for dx, dz, dy in OFFSETS:
        oi = lax.rem(lax.div(i, 2) + dx, 4) * 2 + lax.rem(lax.rem(i, 2) + dz, 2)
        oy = lax.rem(y + dy, FSDP)
        others.append((oi * FSDP + oy, (oi, oy, t)))

    barrier = pltpu.get_barrier_semaphore()

    def greet(device):
        pl.semaphore_signal(barrier, inc=1, device_id=device, device_id_type=MESH)

    for k in range(1, TP):
        greet((i, y, lax.rem(t + k, TP)))
    for core in range(2):
        greet((flip, y, (1 - hi) * 2 + core))
    for _, device in others:
        greet(device)

    def table_rows(block):
        return table_ref.at[pl.ds(pl.multiple_of(block * ROWS, ROWS), ROWS), :]

    def columns(step):
        return pl.ds(pl.multiple_of(turn[step] * CHUNK, CHUNK), CHUNK)

    def weight_copy(step):
        return pltpu.make_async_copy(weight_ref.at[:, :, columns(step)], weight_buf.at[step], weight_sem.at[step])

    own_copy = pltpu.make_async_copy(table_rows(i), own, own_sem)
    own_copy.start()
    small = [
        pltpu.make_async_copy(poles_ref, poles_buf, small_sem.at[0]),
        pltpu.make_async_copy(res_ref, res_buf, small_sem.at[1]),
        pltpu.make_async_copy(taps_ref, taps_buf, small_sem.at[2]),
        pltpu.make_async_copy(skip_ref, skip_buf, small_sem.at[3]),
        pltpu.make_async_copy(gain_ref, gain_buf, small_sem.at[4]),
    ]
    for copy in small:
        copy.start()
    for step in range(CHUNKS):
        weight_copy(step).start()

    pl.semaphore_wait(barrier, TP - 1 + 2 + GROUP - 1)

    half_rows = ROWS // 2
    core = lax.rem(t, 2)
    sibling = hi * 2 + 1 - core
    home = lax.div(y, 2)

    def table_half(block, half):
        return table_ref.at[pl.ds(pl.multiple_of(block * ROWS + half * half_rows, half_rows), half_rows), :]

    def rows_half(half):
        return rows.at[pl.ds(pl.multiple_of(half * half_rows, half_rows), half_rows), :]

    def half_to(source, half, device, slot):
        return pltpu.make_async_remote_copy(
            src_ref=source, dst_ref=rows_half(half), send_sem=rows_send.at[slot], recv_sem=rows_sem.at[half],
            device_id=device, device_id_type=MESH,
        )

    def arrived(half):
        return pltpu.make_async_copy(rows_half(half), rows_half(half), rows_sem.at[half])

    handed = [
        half_to(table_half(flip, half), half, (flip, y, (1 - hi) * 2 + half), half) for half in range(2)
    ] + [half_to(table_half(i, half), half, (i, y, sibling), 2 + half) for half in range(2)]
    forward = half_to(rows_half(core), core, (i, y, sibling), 0)

    @pl.when(t == y)
    def _():
        for copy in handed:
            copy.start()
        for half in range(2):
            pltpu.make_async_copy(table_half(i, half), rows_half(half), rows_sem.at[half]).start()

    own_copy.wait()
    mine = own[...].astype(F32)
    sums = jnp.sum(mine * mine, axis=1, keepdims=True)
    diagonal = iota((ROWS, 128), 0) == iota((ROWS, 128), 1)
    flat = jnp.sum(jnp.where(diagonal, sums, 0.0), axis=0, keepdims=True)
    squares[t] = jnp.broadcast_to(flat, (8, 128))

    def squares_to(k):
        return pltpu.make_async_remote_copy(
            src_ref=squares.at[t], dst_ref=squares.at[t], send_sem=sq_send.at[k], recv_sem=sq_recv.at[t],
            device_id=(i, y, lax.rem(t + k, TP)), device_id_type=MESH,
        )

    for k in range(1, TP):
        squares_to(k).start()

    def ids_to(other, device):
        return pltpu.make_async_remote_copy(
            src_ref=ids_ref, dst_ref=all_ids.at[y, pl.ds(i, 1), :], send_sem=ids_send.at[other],
            recv_sem=ids_recv.at[me], device_id=device, device_id_type=MESH,
        )

    pltpu.make_async_copy(ids_ref, all_ids.at[y, pl.ds(i, 1), :], ids_recv.at[me]).start()
    for other, device in others:
        ids_to(other, device).start()

    for copy in small:
        copy.wait()
    stacked = jnp.concatenate(
        [poles_buf[:, here], res_buf[:, here]]
        + [taps_buf[s, n : n + 1, here] for s in range(3) for n in range(3)]
        + [skip_buf[:, here], jnp.zeros((128 - 2 * POLES - 10, 128), F32)],
        axis=0,
    )
    params[...] = stacked.T

    lag = iota((SUB, STEPS), 1).astype(F32)
    for g in range(SLICE // SUB):
        block = params[pl.ds(pl.multiple_of(y * SLICE + g * SUB, SUB), SUB), :]
        rates = jnp.log(block)
        total = jnp.zeros((SUB, STEPS), F32)
        for n in range(POLES):
            rate = rates[:, n : n + 1]
            lifted = block[:, POLES + n : POLES + n + 1] * jnp.exp(lag * rate)
            total = total + lifted
            at = pl.ds(n * SUB, SUB)
            gmat[g, at, :] = (lifted * block[:, n : n + 1]).astype(BF16)
            vmat[g, at, :] = jnp.exp((STEPS - 1 - lag) * rate).astype(BF16)
        kern[0, pl.ds(g * SUB, SUB), :] = total[:, :128]
        kern[1, pl.ds(g * SUB, SUB), :] = total[:, 128:]

    odd = [lax.rem(lax.div(iota((8, 128), 0), 2**bit), 2) == 1 for bit in range(3)]
    above = iota((128, 128), 1) >= iota((128, 128), 0)

    def fill(g, carry):
        block = pl.ds(pl.multiple_of(g * SUB, SUB), SUB)
        lags = [kern[half, block, :] for half in range(2)]
        bases = [[jnp.broadcast_to(x[k : k + 1], (8, 128)) for x in lags] for k in range(SUB)]
        for bit in range(3):
            bases = [[jnp.where(odd[bit], pltpu.roll(x, 2**bit, 1), x) for x in pair] for pair in bases]
        for k in range(SUB):
            shifted = [
                jnp.concatenate([pltpu.roll(x, 8 * m, 1) if m else x for m in range(16)], axis=0) for x in bases[k]
            ]
            kmat[g * SUB + k, :, pl.ds(0, 128)] = jnp.where(above, shifted[0], 0.0).astype(BF16)
            kmat[g * SUB + k, :, pl.ds(128, 128)] = jnp.where(above, shifted[1], shifted[0]).astype(BF16)
        return carry

    lax.fori_loop(0, SLICE // SUB // 2, fill, 0)

    @pl.when(hi != home)
    def _():
        arrived(core).wait()
        forward.start()

    for k in range(1, TP):
        source = lax.rem(t + k, TP)
        pltpu.make_async_copy(squares.at[source], squares.at[source], sq_recv.at[source]).wait()
    total = squares[0] + squares[1] + squares[2] + squares[3]
    scale = lax.rsqrt(total[0:1, :] * (1.0 / (FEAT * FSDP)) + norm_eps)
    scale = jnp.sum(jnp.where(diagonal, scale, 0.0), axis=1, keepdims=True)

    @pl.when(hi == home)
    def _():
        arrived(core).wait()

    arrived(1 - core).wait()
    gain = gain_buf[:, pl.ds(pl.multiple_of(y * FEAT, FEAT), FEAT)]
    normed = (rows[...].astype(F32) * scale * gain).astype(BF16)

    lane_block = lax.div(iota((48, 128), 1), SLICE)

    def part_to(slot, device):
        return pltpu.make_async_remote_copy(
            src_ref=send_buf.at[slot], dst_ref=parts.at[me], send_sem=part_send.at[slot], recv_sem=part_recv.at[i],
            device_id=device, device_id_type=MESH,
        )

    for step in range(CHUNKS):
        weight_copy(step).wait()
        dots = [jnp.dot(normed, weight_buf[step, stream], preferred_element_type=F32) for stream in range(3)]
        for half in range(CHUNK // 128):
            cols = [dot[:, half * 128 : half * 128 + 128] for dot in dots]
            for b in range(4):
                base = [pltpu.roll(c, (32 * (s - b)) % 128, 1) if (s - b) % 4 else c for s, c in enumerate(cols)]
                tail = jnp.concatenate(
                    [pltpu.roll(c[48:64], (32 * (3 - b)) % 128, 1) if (3 - b) % 4 else c[48:64] for c in cols], axis=0
                )
                piece = jnp.where(
                    lane_block == 0,
                    base[0][:48],
                    jnp.where(lane_block == 1, base[1][:48], jnp.where(lane_block == 2, base[2][:48], tail)),
                )
                send_buf[step * 8 + half * 4 + b] = piece.astype(BF16)
        first = turn[step] * 8
        for k in range(8):
            other = first + k
            slot = step * 8 + k

            @pl.when(other == me)
            def _():
                pltpu.make_async_copy(send_buf.at[slot], parts.at[me], part_recv.at[i]).start()

            @pl.when(other != me)
            def _():
                part_to(slot, (lax.div(other, FSDP), lax.rem(other, FSDP), t)).start()

    vocab_row = iota((VOCAB // 2, STEPS), 0)

    def hot(s, carry):
        for j in range(CTX):
            landed = all_ids.at[s, pl.ds(j, 1), :]
            pltpu.make_async_copy(ids_ref, landed, ids_recv.at[j * FSDP + s]).wait()
            row = all_ids[s, pl.ds(j, 1), :]
            low = jnp.where(row >= VOCAB // 2, row - VOCAB // 2, row)
            onehot[s * CTX + j] = jnp.where(vocab_row == low, 1.0, 0.0).astype(BF16)
        return carry

    lax.fori_loop(SLICE // SUB // 2, SLICE // SUB, fill, 0)
    lax.fori_loop(0, FSDP, hot, 0)

    block16 = lax.div(iota((16, 128), 1), SLICE)
    for v in range(CTX):
        four = parts.at[pl.ds(v * 4, 4)]
        pltpu.make_async_copy(four, four, part_recv.at[v]).wait()
        a = parts[v * 4].astype(F32)
        for k in range(1, 4):
            a = a + parts[v * 4 + k].astype(F32)
        tail = [pltpu.roll(a[16 * s : 16 * s + 16], SLICE * (s + 1), 1) for s in range(3)]
        last = jnp.where(block16 == 0, tail[0], jnp.where(block16 == 1, tail[1], tail[2]))
        whole[pl.ds(v * ROWS, 48), :] = a
        whole[pl.ds(v * ROWS + 48, 16), :] = last
    for v in range(VOCAB // 128):
        turned = whole[pl.ds(v * 128, 128), :].T
        to = pl.ds(v // 2 * 3 * SLICE, 3 * SLICE)
        table[to, pl.ds(v % 2 * 128, 128)] = turned[: 3 * SLICE].astype(BF16)

    def gather(s, carry):
        for j in range(CTX):
            at = s * CTX + j
            both = jnp.dot(table[...], onehot[at], preferred_element_type=F32)
            upper = all_ids[s, pl.ds(j, 1), :] >= VOCAB // 2
            for half in range(2):
                cols = slice(half * 128, half * 128 + 128)
                raw[half, at] = jnp.where(upper[:, cols], both[3 * SLICE :, cols], both[: 3 * SLICE, cols])
        return carry

    lax.fori_loop(0, FSDP, gather, 0)

    lane = iota((SUB, 128), 1)

    def featurize(g):
        block = params[pl.ds(pl.multiple_of(y * SLICE + g * SUB, SUB), SUB), :]
        taps = [
            [
                jnp.broadcast_to(block[:, 2 * POLES + 3 * s + n : 2 * POLES + 3 * s + n + 1], (SUB, 128))
                for n in range(3)
            ]
            for s in range(3)
        ]
        for at in range(GROUP):
            if at % CTX == 0:
                before = [[jnp.zeros((SUB, 128), F32)] * 2] * 3
            for half in range(2):
                done = []
                for s in range(3):
                    now = raw[half, at, pl.ds(s * SLICE + g * SUB, SUB), :]
                    moved = [pltpu.roll(now, n, 1) for n in (1, 2)]
                    total = taps[s][0] * now
                    for n in (1, 2):
                        total = total + taps[s][n] * jnp.where(lane < n, before[s][n - 1], moved[n - 1])
                    before = before[:s] + [moved] + before[s + 1 :]
                    done.append(total)
                to = pl.ds(at * SUB, SUB)
                query[g][half, to, :] = done[0]
                product[g][half, to, :] = done[1] * done[2]

    same = lax.div(iota((SUB * GROUP, 128), 0), GROUP) == lax.rem(iota((SUB * GROUP, 128), 1), SUB)
    chunk = lax.rem(iota((SUB * GROUP, 128), 0), CTX)
    diagonal128 = iota((128, 128), 0) == iota((128, 128), 1)

    def convolve(g):
        block = params[pl.ds(pl.multiple_of(y * SLICE + g * SUB, SUB), SUB), :]
        decay = jnp.concatenate(
            [jnp.broadcast_to(block[:, n : n + 1], (SUB, 128)) for n in range(POLES)], axis=0
        )
        decay = jnp.sum(jnp.where(diagonal128, decay, 0.0), axis=0, keepdims=True)
        for _ in range(8):
            decay = decay * decay
        halves = [
            [product[g][half, pl.ds(k, GROUP, stride=SUB), :].astype(BF16) for half in range(2)] for k in range(SUB)
        ]
        inputs = jnp.concatenate([jnp.concatenate(x, axis=1) for x in halves], axis=0)
        states = lax.dot_general(inputs, vmat[g], (((1,), (1,)), ((), ())), preferred_element_type=F32)
        inner = []
        for k in range(SUB):
            both = jnp.dot(jnp.concatenate(halves[k], axis=0), kmat[g * SUB + k], preferred_element_type=F32)
            inner.append([both[:GROUP, :128], both[:GROUP, 128:] + both[GROUP:, :128]])
        states = jnp.where(same, states, 0.0)
        states = jnp.where(chunk < 1, 0.0, pltpu.roll(states, 1, 0))
        for by in (1, 2, 4):
            states = states + decay * jnp.where(chunk < by, 0.0, pltpu.roll(states, by, 0))
            decay = decay * decay
        carried = jnp.dot(states.astype(BF16), gmat[g], preferred_element_type=F32)
        for k in range(SUB):
            for half in range(2):
                mixed[g][half, pl.ds(k, GROUP, stride=SUB), :] = (
                    inner[k][half] + carried[k * GROUP : (k + 1) * GROUP, half * 128 : half * 128 + 128]
                )

    groups = SLICE // SUB
    featurize(0)
    for g in range(groups):
        if g + 1 < groups:
            featurize(g + 1)
        convolve(g)

    mine_params = params[pl.ds(pl.multiple_of(y * SLICE, SLICE), SLICE), :]
    skip = jnp.broadcast_to(mine_params[:, 2 * POLES + 9 : 2 * POLES + 10], (SLICE, 128))
    pieces = onehot

    def out_to(other, device):
        return pltpu.make_async_remote_copy(
            src_ref=pieces.at[other, pl.ds(0, SLICE), :], dst_ref=out_ref.at[me], send_sem=out_send.at[other],
            recv_sem=out_recv, device_id=device, device_id_type=MESH,
        )

    def gate(other):
        s = lax.rem(other, FSDP)
        j = lax.div(other, FSDP)
        at = pl.ds(pl.multiple_of((s * CTX + j) * SUB, SUB), SUB)
        for half in range(2):
            q, u, c = [
                jnp.concatenate([x[g][half, at, :] for g in range(groups)], axis=0) for x in (query, product, mixed)
            ]
            pieces[other, pl.ds(0, SLICE), pl.ds(half * 128, 128)] = (q * (c + skip * u)).astype(BF16)

    for other, device in others:
        gate(other)
        out_to(other, device).start()
    gate(me)
    pltpu.make_async_copy(pieces.at[me, pl.ds(0, SLICE), :], out_ref.at[me], out_recv).start()

    for k in range(1, TP):
        squares_to(k).wait_send()

    @pl.when(t == y)
    def _():
        for copy in handed:
            copy.wait_send()

    @pl.when(hi != home)
    def _():
        forward.wait_send()

    for step in range(CHUNKS):
        first = turn[step] * 8
        for k in range(8):

            @pl.when(first + k != me)
            def _():
                part_to(step * 8 + k, (i, y, t)).wait_send()

    for other, device in others:
        ids_to(other, device).wait_send()
        out_to(other, device).wait_send()

    pltpu.make_async_copy(out_ref, out_ref, out_recv).wait()


def block(*args):
    hbm = pl.BlockSpec(memory_space=pltpu.HBM)
    dma = pltpu.SemaphoreType.DMA
    groups = SLICE // SUB
    return pl.pallas_call(
        block_kernel,
        out_shape=jax.ShapeDtypeStruct((GROUP, SLICE, STEPS), BF16),
        in_specs=[hbm] * 8,
        out_specs=hbm,
        scratch_shapes=[
            pltpu.VMEM((CHUNKS, 3, FEAT, CHUNK), BF16),
            pltpu.VMEM((ROWS, FEAT), BF16),
            pltpu.VMEM((ROWS, FEAT), BF16),
            pltpu.VMEM((TP, 8, 128), F32),
            pltpu.VMEM((GROUP, 48, 128), BF16),
            pltpu.VMEM((GROUP, 48, 128), BF16),
            pltpu.VMEM((FSDP, CTX, STEPS), jnp.int32),
            pltpu.VMEM((1, FEAT * FSDP), F32),
            pltpu.VMEM((3, 3, CHAN), F32),
            pltpu.VMEM((POLES, CHAN), F32),
            pltpu.VMEM((POLES, CHAN), F32),
            pltpu.VMEM((1, CHAN), F32),
            pltpu.VMEM((128, 128), F32),
            pltpu.VMEM((2, SLICE, 128), F32),
            pltpu.VMEM((SLICE, STEPS // 2, STEPS), BF16),
            pltpu.VMEM((groups, POLES * SUB, STEPS), BF16),
            pltpu.VMEM((groups, POLES * SUB, STEPS), BF16),
            pltpu.VMEM((GROUP, VOCAB // 2, STEPS), BF16),
            pltpu.VMEM((6 * SLICE, VOCAB // 2), BF16),
            pltpu.VMEM((VOCAB, 128), F32),
            pltpu.VMEM((2, GROUP, 3 * SLICE, 128), F32),
            [pltpu.VMEM((2, GROUP * SUB, 128), F32) for _ in range(groups)],
            [pltpu.VMEM((2, GROUP * SUB, 128), F32) for _ in range(groups)],
            [pltpu.VMEM((2, GROUP * SUB, 128), F32) for _ in range(groups)],
            dma((CHUNKS,)),
            dma,
            dma((5,)),
            dma((2,)),
            dma((4,)),
            dma((TP,)),
            dma((TP,)),
            dma((GROUP,)),
            dma((GROUP,)),
            dma((GROUP,)),
            dma((CTX,)),
            dma((GROUP,)),
            dma,
        ],
        compiler_params=pltpu.CompilerParams(
            collective_id=0, has_side_effects=True, vmem_limit_bytes=56 * 2**20
        ),
        name="hyena_block",
    )(*args)


def shards(
    base_ids, embed_table, norm_gain, in_weight, conv_taps, modal_poles, residues, skip_gain
):
    landed = block(
        base_ids, embed_table, norm_gain.reshape(1, -1), jnp.transpose(in_weight, (1, 0, 2)),
        conv_taps, modal_poles, residues, skip_gain.reshape(1, -1),
    )
    return landed.reshape(CHAN, STEPS).T[None]


def solution(mesh):
    in_specs = (
        P("fsdp", "ctx"),
        P(None, "tp"),
        P(),
        P("fsdp", None, "tp"),
        P(None, None, "tp"),
        P(None, "tp"),
        P(None, "tp"),
        P("tp"),
    )
    out_specs = P("fsdp", "ctx", "tp")
    return jax.shard_map(shards, mesh=mesh, in_specs=in_specs, out_specs=out_specs, check_vma=False)
```

```python
import jax
import jax.numpy as jnp
from jax import lax
from jax.experimental import pallas as pl
from jax.experimental.pallas import tpu as pltpu
from jax.sharding import PartitionSpec as P

MESH = pl.DeviceIdType.MESH
F32 = jnp.float32
BF16 = jnp.bfloat16
norm_eps = 1e-06

CTX, FSDP, TP = 8, 4, 4
GROUP = CTX * FSDP
VOCAB = 512
ROWS = VOCAB // CTX
FEAT = 2048
CHAN = 1024
SLICE = CHAN // GROUP
STEPS = 256
POLES = 16
CHUNK = 256
CHUNKS = CHAN // CHUNK
SUB = 8


def iota(shape, dim):
    return lax.broadcasted_iota(jnp.int32, shape, dim)


OFFSETS = sorted(
    [(x, z, y) for x in range(4) for z in range(2) for y in range(4) if (x, z, y) != (0, 0, 0)],
    key=lambda o: -(min(o[0], 4 - o[0]) + o[1] + min(o[2], 4 - o[2])),
)


FAR_X = (2, 1, 3, 0)


def block_kernel(
    ids_ref, table_ref, gain_ref, weight_ref, taps_ref, poles_ref, res_ref, skip_ref, out_ref,
    weight_buf, own, rows, squares, send_buf, parts, all_ids, gain_buf, taps_buf, poles_buf, res_buf, skip_buf,
    params, kern, kmat, vmat, gmat, onehot, table, whole, raw, product, query, mixed,
    weight_sem, own_sem, small_sem, rows_sem, rows_send, sq_send, sq_recv, ids_send, ids_recv, part_send, part_recv,
    out_send, out_recv, ready,
):
    i = lax.axis_index("ctx")
    y = lax.axis_index("fsdp")
    t = lax.axis_index("tp")
    me = i * FSDP + y
    hi = lax.div(t, 2)
    flip = i + 1 - 2 * lax.rem(i, 2)
    turn = [lax.rem(lax.div(i, 2) + x, CHUNKS) for x in FAR_X]
    here = pl.ds(pl.multiple_of(i * 128, 128), 128)

    others = []
    for dx, dz, dy in OFFSETS:
        oi = lax.rem(lax.div(i, 2) + dx, 4) * 2 + lax.rem(lax.rem(i, 2) + dz, 2)
        oy = lax.rem(y + dy, FSDP)
        others.append((oi * FSDP + oy, (oi, oy, t)))

    barrier = pltpu.get_barrier_semaphore()

    def greet(device):
        pl.semaphore_signal(barrier, inc=1, device_id=device, device_id_type=MESH)

    for k in range(1, TP):
        greet((i, y, lax.rem(t + k, TP)))
    for core in range(2):
        greet((flip, y, (1 - hi) * 2 + core))
    for k in range(1, FSDP):
        greet((i, lax.rem(y + k, FSDP), t))
    columns_of = [(lax.rem(i + k, CTX), y, t) for k in range(1, CTX)]
    for device in columns_of:
        greet(device)

    def table_rows(block):
        return table_ref.at[pl.ds(pl.multiple_of(block * ROWS, ROWS), ROWS), :]

    def columns(step):
        return pl.ds(pl.multiple_of(turn[step] * CHUNK, CHUNK), CHUNK)

    def weight_copy(step):
        return pltpu.make_async_copy(weight_ref.at[:, :, columns(step)], weight_buf.at[step], weight_sem.at[step])

    own_copy = pltpu.make_async_copy(table_rows(i), own, own_sem)
    own_copy.start()
    small = [
        pltpu.make_async_copy(poles_ref, poles_buf, small_sem.at[0]),
        pltpu.make_async_copy(res_ref, res_buf, small_sem.at[1]),
        pltpu.make_async_copy(taps_ref, taps_buf, small_sem.at[2]),
        pltpu.make_async_copy(skip_ref, skip_buf, small_sem.at[3]),
        pltpu.make_async_copy(gain_ref, gain_buf, small_sem.at[4]),
    ]
    for copy in small:
        copy.start()
    for step in range(CHUNKS):
        weight_copy(step).start()

    pl.semaphore_wait(barrier, TP - 1 + 2 + FSDP - 1 + CTX - 1)

    half_rows = ROWS // 2
    core = lax.rem(t, 2)
    sibling = hi * 2 + 1 - core
    home = lax.div(y, 2)

    def table_half(block, half):
        return table_ref.at[pl.ds(pl.multiple_of(block * ROWS + half * half_rows, half_rows), half_rows), :]

    def rows_half(half):
        return rows.at[pl.ds(pl.multiple_of(half * half_rows, half_rows), half_rows), :]

    def half_to(source, half, device, slot):
        return pltpu.make_async_remote_copy(
            src_ref=source, dst_ref=rows_half(half), send_sem=rows_send.at[slot], recv_sem=rows_sem.at[half],
            device_id=device, device_id_type=MESH,
        )

    def arrived(half):
        return pltpu.make_async_copy(rows_half(half), rows_half(half), rows_sem.at[half])

    handed = [
        half_to(table_half(flip, half), half, (flip, y, (1 - hi) * 2 + half), half) for half in range(2)
    ] + [half_to(table_half(i, half), half, (i, y, sibling), 2 + half) for half in range(2)]
    forward = half_to(rows_half(core), core, (i, y, sibling), 0)

    @pl.when(t == y)
    def _():
        for copy in handed:
            copy.start()
        for half in range(2):
            pltpu.make_async_copy(table_half(i, half), rows_half(half), rows_sem.at[half]).start()

    for device in columns_of:
        pl.semaphore_signal(ready, inc=1, device_id=device, device_id_type=MESH)

    own_copy.wait()
    mine = own[...].astype(F32)
    sums = jnp.sum(mine * mine, axis=1, keepdims=True)
    diagonal = iota((ROWS, 128), 0) == iota((ROWS, 128), 1)
    flat = jnp.sum(jnp.where(diagonal, sums, 0.0), axis=0, keepdims=True)
    squares[t] = jnp.broadcast_to(flat, (8, 128))

    def squares_to(k):
        return pltpu.make_async_remote_copy(
            src_ref=squares.at[t], dst_ref=squares.at[t], send_sem=sq_send.at[k], recv_sem=sq_recv.at[t],
            device_id=(i, y, lax.rem(t + k, TP)), device_id_type=MESH,
        )

    for k in range(1, TP):
        squares_to(k).start()

    def ids_to(other, device):
        return pltpu.make_async_remote_copy(
            src_ref=ids_ref, dst_ref=all_ids.at[y, pl.ds(i, 1), :], send_sem=ids_send.at[other],
            recv_sem=ids_recv.at[me], device_id=device, device_id_type=MESH,
        )

    pltpu.make_async_copy(ids_ref, all_ids.at[y, pl.ds(i, 1), :], ids_recv.at[me]).start()
    pl.semaphore_wait(ready, CTX - 1)
    for other, device in others:
        ids_to(other, device).start()

    for copy in small:
        copy.wait()
    stacked = jnp.concatenate(
        [poles_buf[:, here], res_buf[:, here]]
        + [taps_buf[s, n : n + 1, here] for s in range(3) for n in range(3)]
        + [skip_buf[:, here], jnp.zeros((128 - 2 * POLES - 10, 128), F32)],
        axis=0,
    )
    params[...] = stacked.T

    lag = iota((SUB, STEPS), 1).astype(F32)
    for g in range(SLICE // SUB):
        block = params[pl.ds(pl.multiple_of(y * SLICE + g * SUB, SUB), SUB), :]
        rates = jnp.log(block)
        total = jnp.zeros((SUB, STEPS), F32)
        for n in range(POLES):
            rate = rates[:, n : n + 1]
            lifted = block[:, POLES + n : POLES + n + 1] * jnp.exp(lag * rate)
            total = total + lifted
            at = pl.ds(n * SUB, SUB)
            gmat[g, at, :] = (lifted * block[:, n : n + 1]).astype(BF16)
            vmat[g, at, :] = jnp.exp((STEPS - 1 - lag) * rate).astype(BF16)
        kern[0, pl.ds(g * SUB, SUB), :] = total[:, :128]
        kern[1, pl.ds(g * SUB, SUB), :] = total[:, 128:]

    odd = [lax.rem(lax.div(iota((8, 128), 0), 2**bit), 2) == 1 for bit in range(3)]
    above = iota((128, 128), 1) >= iota((128, 128), 0)

    def fill(g, carry):
        block = pl.ds(pl.multiple_of(g * SUB, SUB), SUB)
        lags = [kern[half, block, :] for half in range(2)]
        bases = [[jnp.broadcast_to(x[k : k + 1], (8, 128)) for x in lags] for k in range(SUB)]
        for bit in range(3):
            bases = [[jnp.where(odd[bit], pltpu.roll(x, 2**bit, 1), x) for x in pair] for pair in bases]
        for k in range(SUB):
            shifted = [
                jnp.concatenate([pltpu.roll(x, 8 * m, 1) if m else x for m in range(16)], axis=0) for x in bases[k]
            ]
            kmat[g * SUB + k, :, pl.ds(0, 128)] = jnp.where(above, shifted[0], 0.0).astype(BF16)
            kmat[g * SUB + k, :, pl.ds(128, 128)] = jnp.where(above, shifted[1], shifted[0]).astype(BF16)
        return carry

    lax.fori_loop(0, SLICE // SUB // 2, fill, 0)

    @pl.when(hi != home)
    def _():
        arrived(core).wait()
        forward.start()

    for k in range(1, TP):
        source = lax.rem(t + k, TP)
        pltpu.make_async_copy(squares.at[source], squares.at[source], sq_recv.at[source]).wait()
    total = squares[0] + squares[1] + squares[2] + squares[3]
    scale = lax.rsqrt(total[0:1, :] * (1.0 / (FEAT * FSDP)) + norm_eps)
    scale = jnp.sum(jnp.where(diagonal, scale, 0.0), axis=1, keepdims=True)

    @pl.when(hi == home)
    def _():
        arrived(core).wait()

    arrived(1 - core).wait()
    gain = gain_buf[:, pl.ds(pl.multiple_of(y * FEAT, FEAT), FEAT)]
    normed = (rows[...].astype(F32) * scale * gain).astype(BF16)

    lane_block = lax.div(iota((48, 128), 1), SLICE)

    def part_to(slot, device):
        return pltpu.make_async_remote_copy(
            src_ref=send_buf.at[slot], dst_ref=parts.at[me], send_sem=part_send.at[slot], recv_sem=part_recv.at[i],
            device_id=device, device_id_type=MESH,
        )

    mine_at = lax.rem(me, 8)

    def receivers(step):
        for dx, dz, dy in OFFSETS:
            if dx == FAR_X[step]:
                oz, oy = lax.rem(lax.rem(i, 2) + dz, 2), lax.rem(y + dy, FSDP)
                yield oz * FSDP + oy, (turn[step] * 2 + oz, oy, t)

    for step in range(CHUNKS):
        weight_copy(step).wait()
        dots = [jnp.dot(normed, weight_buf[step, stream], preferred_element_type=F32) for stream in range(3)]
        for half in range(CHUNK // 128):
            cols = [dot[:, half * 128 : half * 128 + 128] for dot in dots]
            for b in range(4):
                base = [pltpu.roll(c, (32 * (s - b)) % 128, 1) if (s - b) % 4 else c for s, c in enumerate(cols)]
                tail = jnp.concatenate(
                    [pltpu.roll(c[48:64], (32 * (3 - b)) % 128, 1) if (3 - b) % 4 else c[48:64] for c in cols], axis=0
                )
                piece = jnp.where(
                    lane_block == 0,
                    base[0][:48],
                    jnp.where(lane_block == 1, base[1][:48], jnp.where(lane_block == 2, base[2][:48], tail)),
                )
                send_buf[step * 8 + half * 4 + b] = piece.astype(BF16)
        for slot, device in receivers(step):
            part_to(step * 8 + slot, device).start()
        if FAR_X[step] == 0:
            pltpu.make_async_copy(send_buf.at[step * 8 + mine_at], parts.at[me], part_recv.at[i]).start()

    vocab_row = iota((VOCAB // 2, STEPS), 0)

    def hot(s, carry):
        for j in range(CTX):
            landed = all_ids.at[s, pl.ds(j, 1), :]
            pltpu.make_async_copy(ids_ref, landed, ids_recv.at[j * FSDP + s]).wait()
            row = all_ids[s, pl.ds(j, 1), :]
            low = jnp.where(row >= VOCAB // 2, row - VOCAB // 2, row)
            onehot[s * CTX + j] = jnp.where(vocab_row == low, 1.0, 0.0).astype(BF16)
        return carry

    lax.fori_loop(SLICE // SUB // 2, SLICE // SUB, fill, 0)
    lax.fori_loop(0, FSDP, hot, 0)

    block16 = lax.div(iota((16, 128), 1), SLICE)
    for v in range(CTX):
        four = parts.at[pl.ds(v * 4, 4)]
        pltpu.make_async_copy(four, four, part_recv.at[v]).wait()
        a = parts[v * 4].astype(F32)
        for k in range(1, 4):
            a = a + parts[v * 4 + k].astype(F32)
        tail = [pltpu.roll(a[16 * s : 16 * s + 16], SLICE * (s + 1), 1) for s in range(3)]
        last = jnp.where(block16 == 0, tail[0], jnp.where(block16 == 1, tail[1], tail[2]))
        whole[pl.ds(v * ROWS, 48), :] = a
        whole[pl.ds(v * ROWS + 48, 16), :] = last
    for v in range(VOCAB // 128):
        turned = whole[pl.ds(v * 128, 128), :].T
        to = pl.ds(v // 2 * 3 * SLICE, 3 * SLICE)
        table[to, pl.ds(v % 2 * 128, 128)] = turned[: 3 * SLICE].astype(BF16)

    def gather(s, carry):
        for j in range(CTX):
            at = s * CTX + j
            both = jnp.dot(table[...], onehot[at], preferred_element_type=F32)
            upper = all_ids[s, pl.ds(j, 1), :] >= VOCAB // 2
            for half in range(2):
                cols = slice(half * 128, half * 128 + 128)
                raw[half, at] = jnp.where(upper[:, cols], both[3 * SLICE :, cols], both[: 3 * SLICE, cols])
        return carry

    lax.fori_loop(0, FSDP, gather, 0)

    lane = iota((SUB, 128), 1)

    def featurize(g):
        block = params[pl.ds(pl.multiple_of(y * SLICE + g * SUB, SUB), SUB), :]
        taps = [
            [
                jnp.broadcast_to(block[:, 2 * POLES + 3 * s + n : 2 * POLES + 3 * s + n + 1], (SUB, 128))
                for n in range(3)
            ]
            for s in range(3)
        ]
        for at in range(GROUP):
            if at % CTX == 0:
                before = [[jnp.zeros((SUB, 128), F32)] * 2] * 3
            for half in range(2):
                done = []
                for s in range(3):
                    now = raw[half, at, pl.ds(s * SLICE + g * SUB, SUB), :]
                    moved = [pltpu.roll(now, n, 1) for n in (1, 2)]
                    total = taps[s][0] * now
                    for n in (1, 2):
                        total = total + taps[s][n] * jnp.where(lane < n, before[s][n - 1], moved[n - 1])
                    before = before[:s] + [moved] + before[s + 1 :]
                    done.append(total)
                to = pl.ds(at * SUB, SUB)
                query[g][half, to, :] = done[0]
                product[g][half, to, :] = done[1] * done[2]

    same = lax.div(iota((SUB * GROUP, 128), 0), GROUP) == lax.rem(iota((SUB * GROUP, 128), 1), SUB)
    chunk = lax.rem(iota((SUB * GROUP, 128), 0), CTX)
    diagonal128 = iota((128, 128), 0) == iota((128, 128), 1)

    def convolve(g):
        block = params[pl.ds(pl.multiple_of(y * SLICE + g * SUB, SUB), SUB), :]
        decay = jnp.concatenate(
            [jnp.broadcast_to(block[:, n : n + 1], (SUB, 128)) for n in range(POLES)], axis=0
        )
        decay = jnp.sum(jnp.where(diagonal128, decay, 0.0), axis=0, keepdims=True)
        for _ in range(8):
            decay = decay * decay
        halves = [
            [product[g][half, pl.ds(k, GROUP, stride=SUB), :].astype(BF16) for half in range(2)] for k in range(SUB)
        ]
        inputs = jnp.concatenate([jnp.concatenate(x, axis=1) for x in halves], axis=0)
        states = lax.dot_general(inputs, vmat[g], (((1,), (1,)), ((), ())), preferred_element_type=F32)
        inner = []
        for k in range(SUB):
            both = jnp.dot(jnp.concatenate(halves[k], axis=0), kmat[g * SUB + k], preferred_element_type=F32)
            inner.append([both[:GROUP, :128], both[:GROUP, 128:] + both[GROUP:, :128]])
        states = jnp.where(same, states, 0.0)
        states = jnp.where(chunk < 1, 0.0, pltpu.roll(states, 1, 0))
        for by in (1, 2, 4):
            states = states + decay * jnp.where(chunk < by, 0.0, pltpu.roll(states, by, 0))
            decay = decay * decay
        carried = jnp.dot(states.astype(BF16), gmat[g], preferred_element_type=F32)
        for k in range(SUB):
            for half in range(2):
                mixed[g][half, pl.ds(k, GROUP, stride=SUB), :] = (
                    inner[k][half] + carried[k * GROUP : (k + 1) * GROUP, half * 128 : half * 128 + 128]
                )

    groups = SLICE // SUB
    featurize(0)
    for g in range(groups):
        if g + 1 < groups:
            featurize(g + 1)
        convolve(g)

    mine_params = params[pl.ds(pl.multiple_of(y * SLICE, SLICE), SLICE), :]
    skip = jnp.broadcast_to(mine_params[:, 2 * POLES + 9 : 2 * POLES + 10], (SLICE, 128))
    pieces = onehot

    def out_to(other, device):
        return pltpu.make_async_remote_copy(
            src_ref=pieces.at[other, pl.ds(0, SLICE), :], dst_ref=out_ref.at[me], send_sem=out_send.at[other],
            recv_sem=out_recv, device_id=device, device_id_type=MESH,
        )

    def gate(other):
        s = lax.rem(other, FSDP)
        j = lax.div(other, FSDP)
        at = pl.ds(pl.multiple_of((s * CTX + j) * SUB, SUB), SUB)
        for half in range(2):
            q, u, c = [
                jnp.concatenate([x[g][half, at, :] for g in range(groups)], axis=0) for x in (query, product, mixed)
            ]
            pieces[other, pl.ds(0, SLICE), pl.ds(half * 128, 128)] = (q * (c + skip * u)).astype(BF16)

    for other, device in others:
        gate(other)
        out_to(other, device).start()
    gate(me)
    pltpu.make_async_copy(pieces.at[me, pl.ds(0, SLICE), :], out_ref.at[me], out_recv).start()

    for k in range(1, TP):
        squares_to(k).wait_send()

    @pl.when(t == y)
    def _():
        for copy in handed:
            copy.wait_send()

    @pl.when(hi != home)
    def _():
        forward.wait_send()

    for step in range(CHUNKS):
        for slot, device in receivers(step):
            part_to(step * 8 + slot, device).wait_send()

    for other, device in others:
        ids_to(other, device).wait_send()
        out_to(other, device).wait_send()

    pltpu.make_async_copy(out_ref, out_ref, out_recv).wait()


def block(*args):
    hbm = pl.BlockSpec(memory_space=pltpu.HBM)
    dma = pltpu.SemaphoreType.DMA
    groups = SLICE // SUB
    return pl.pallas_call(
        block_kernel,
        out_shape=jax.ShapeDtypeStruct((GROUP, SLICE, STEPS), BF16),
        in_specs=[hbm] * 8,
        out_specs=hbm,
        scratch_shapes=[
            pltpu.VMEM((CHUNKS, 3, FEAT, CHUNK), BF16),
            pltpu.VMEM((ROWS, FEAT), BF16),
            pltpu.VMEM((ROWS, FEAT), BF16),
            pltpu.VMEM((TP, 8, 128), F32),
            pltpu.VMEM((GROUP, 48, 128), BF16),
            pltpu.VMEM((GROUP, 48, 128), BF16),
            pltpu.VMEM((FSDP, CTX, STEPS), jnp.int32),
            pltpu.VMEM((1, FEAT * FSDP), F32),
            pltpu.VMEM((3, 3, CHAN), F32),
            pltpu.VMEM((POLES, CHAN), F32),
            pltpu.VMEM((POLES, CHAN), F32),
            pltpu.VMEM((1, CHAN), F32),
            pltpu.VMEM((128, 128), F32),
            pltpu.VMEM((2, SLICE, 128), F32),
            pltpu.VMEM((SLICE, STEPS // 2, STEPS), BF16),
            pltpu.VMEM((groups, POLES * SUB, STEPS), BF16),
            pltpu.VMEM((groups, POLES * SUB, STEPS), BF16),
            pltpu.VMEM((GROUP, VOCAB // 2, STEPS), BF16),
            pltpu.VMEM((6 * SLICE, VOCAB // 2), BF16),
            pltpu.VMEM((VOCAB, 128), F32),
            pltpu.VMEM((2, GROUP, 3 * SLICE, 128), F32),
            [pltpu.VMEM((2, GROUP * SUB, 128), F32) for _ in range(groups)],
            [pltpu.VMEM((2, GROUP * SUB, 128), F32) for _ in range(groups)],
            [pltpu.VMEM((2, GROUP * SUB, 128), F32) for _ in range(groups)],
            dma((CHUNKS,)),
            dma,
            dma((5,)),
            dma((2,)),
            dma((4,)),
            dma((TP,)),
            dma((TP,)),
            dma((GROUP,)),
            dma((GROUP,)),
            dma((GROUP,)),
            dma((CTX,)),
            dma((GROUP,)),
            dma,
            pltpu.SemaphoreType.REGULAR,
        ],
        compiler_params=pltpu.CompilerParams(
            collective_id=0, has_side_effects=True, vmem_limit_bytes=56 * 2**20
        ),
        name="hyena_block",
    )(*args)


def shards(
    base_ids, embed_table, norm_gain, in_weight, conv_taps, modal_poles, residues, skip_gain
):
    landed = block(
        base_ids, embed_table, norm_gain.reshape(1, -1), jnp.transpose(in_weight, (1, 0, 2)),
        conv_taps, modal_poles, residues, skip_gain.reshape(1, -1),
    )
    return landed.reshape(CHAN, STEPS).T[None]


def solution(mesh):
    in_specs = (
        P("fsdp", "ctx"),
        P(None, "tp"),
        P(),
        P("fsdp", None, "tp"),
        P(None, None, "tp"),
        P(None, "tp"),
        P(None, "tp"),
        P("tp"),
    )
    out_specs = P("fsdp", "ctx", "tp")
    return jax.shard_map(shards, mesh=mesh, in_specs=in_specs, out_specs=out_specs, check_vma=False)
```

```python
import jax
import jax.numpy as jnp
from jax import lax
from jax.experimental import pallas as pl
from jax.experimental.pallas import tpu as pltpu
from jax.sharding import PartitionSpec as P

MESH = pl.DeviceIdType.MESH
F32 = jnp.float32
BF16 = jnp.bfloat16
norm_eps = 1e-06

CTX, FSDP, TP = 8, 4, 4
GROUP = CTX * FSDP
VOCAB = 512
ROWS = VOCAB // CTX
FEAT = 2048
CHAN = 1024
SLICE = CHAN // GROUP
STEPS = 256
POLES = 16
CHUNK = 256
CHUNKS = CHAN // CHUNK
SUB = 8


def iota(shape, dim):
    return lax.broadcasted_iota(jnp.int32, shape, dim)


OFFSETS = sorted(
    [(x, z, y) for x in range(4) for z in range(2) for y in range(4) if (x, z, y) != (0, 0, 0)],
    key=lambda o: -(min(o[0], 4 - o[0]) + o[1] + min(o[2], 4 - o[2])),
)


FAR_X = (2, 1, 3, 0)


def block_kernel(
    ids_ref, table_ref, gain_ref, weight_ref, taps_ref, poles_ref, res_ref, skip_ref, out_ref,
    weight_buf, own, next_rows, rows, squares, send_buf, parts, all_ids, gain_buf, taps_buf, poles_buf, res_buf, skip_buf,
    params, kern, kmat, vmat, gmat, onehot, table, whole, raw, product, query, mixed,
    weight_sem, own_sem, next_sem, small_sem, rows_sem, rows_send, sq_send, sq_recv, ids_send, ids_recv, part_send, part_recv,
    out_send, out_recv, ready,
):
    i = lax.axis_index("ctx")
    y = lax.axis_index("fsdp")
    t = lax.axis_index("tp")
    me = i * FSDP + y
    hi = lax.div(t, 2)
    flip = i + 1 - 2 * lax.rem(i, 2)
    turn = [lax.rem(lax.div(i, 2) + x, CHUNKS) for x in FAR_X]
    here = pl.ds(pl.multiple_of(i * 128, 128), 128)

    others = []
    for dx, dz, dy in OFFSETS:
        oi = lax.rem(lax.div(i, 2) + dx, 4) * 2 + lax.rem(lax.rem(i, 2) + dz, 2)
        oy = lax.rem(y + dy, FSDP)
        others.append((oi * FSDP + oy, (oi, oy, t)))

    barrier = pltpu.get_barrier_semaphore()

    def greet(device):
        pl.semaphore_signal(barrier, inc=1, device_id=device, device_id_type=MESH)

    for k in range(1, TP):
        greet((i, y, lax.rem(t + k, TP)))
    for core in range(2):
        greet((flip, y, (1 - hi) * 2 + core))
    for k in range(1, FSDP):
        greet((i, lax.rem(y + k, FSDP), t))
    along_x = [(lax.rem(i + 2 * k, CTX), y, t) for k in range(1, 4)]
    for device in along_x + [(flip, y, t)]:
        greet(device)

    def table_rows(block):
        return table_ref.at[pl.ds(pl.multiple_of(block * ROWS, ROWS), ROWS), :]

    def columns(step):
        return pl.ds(pl.multiple_of(turn[step] * CHUNK, CHUNK), CHUNK)

    def weight_copy(step):
        return pltpu.make_async_copy(weight_ref.at[:, :, columns(step)], weight_buf.at[step], weight_sem.at[step])

    own_copy = pltpu.make_async_copy(table_rows(i), own, own_sem)
    own_copy.start()
    next_copy = pltpu.make_async_copy(table_rows(flip), next_rows, next_sem)
    next_copy.start()
    small = [
        pltpu.make_async_copy(poles_ref, poles_buf, small_sem.at[0]),
        pltpu.make_async_copy(res_ref, res_buf, small_sem.at[1]),
        pltpu.make_async_copy(taps_ref, taps_buf, small_sem.at[2]),
        pltpu.make_async_copy(skip_ref, skip_buf, small_sem.at[3]),
        pltpu.make_async_copy(gain_ref, gain_buf, small_sem.at[4]),
    ]
    for copy in small:
        copy.start()
    for step in range(CHUNKS):
        weight_copy(step).start()

    pl.semaphore_wait(barrier, TP - 1 + 2 + FSDP - 1 + 3 + 1)

    piece_rows = ROWS // 4
    core = lax.rem(t, 2)
    sibling = hi * 2 + 1 - core
    home = lax.div(y, 2)

    def piece(ref, at):
        return ref.at[pl.ds(pl.multiple_of(at * piece_rows, piece_rows), piece_rows), :]

    def piece_to(source, at, device, slot):
        return pltpu.make_async_remote_copy(
            src_ref=piece(source, at), dst_ref=piece(rows, at), send_sem=rows_send.at[slot], recv_sem=rows_sem.at[at],
            device_id=device, device_id_type=MESH,
        )

    def arrived(at):
        return pltpu.make_async_copy(piece(rows, at), piece(rows, at), rows_sem.at[at])

    order = (0, 2, 1, 3)
    handed = [piece_to(next_rows, at, (flip, y, (1 - hi) * 2 + at // 2), at) for at in order] + [
        piece_to(own, at, (i, y, sibling), 4 + at) for at in order
    ]
    forward = [piece_to(rows, core * 2 + k, (i, y, sibling), k) for k in range(2)]

    own_copy.wait()
    next_copy.wait()

    @pl.when(t == y)
    def _():
        for copy in handed:
            copy.start()
        for at in range(4):
            pltpu.make_async_copy(piece(own, at), piece(rows, at), rows_sem.at[at]).start()

    for device in along_x:
        pl.semaphore_signal(ready.at[0], inc=1, device_id=device, device_id_type=MESH)

    mine = own[...].astype(F32)
    sums = jnp.sum(mine * mine, axis=1, keepdims=True)
    diagonal = iota((ROWS, 128), 0) == iota((ROWS, 128), 1)
    flat = jnp.sum(jnp.where(diagonal, sums, 0.0), axis=0, keepdims=True)
    squares[t] = jnp.broadcast_to(flat, (8, 128))

    def squares_to(k):
        return pltpu.make_async_remote_copy(
            src_ref=squares.at[t], dst_ref=squares.at[t], send_sem=sq_send.at[k], recv_sem=sq_recv.at[t],
            device_id=(i, y, lax.rem(t + k, TP)), device_id_type=MESH,
        )

    for k in range(1, TP):
        squares_to(k).start()

    for copy in small:
        copy.wait()
    stacked = jnp.concatenate(
        [poles_buf[:, here], res_buf[:, here]]
        + [taps_buf[s, n : n + 1, here] for s in range(3) for n in range(3)]
        + [skip_buf[:, here], jnp.zeros((128 - 2 * POLES - 10, 128), F32)],
        axis=0,
    )
    params[...] = stacked.T

    lag = iota((SUB, STEPS), 1).astype(F32)
    for g in range(SLICE // SUB):
        block = params[pl.ds(pl.multiple_of(y * SLICE + g * SUB, SUB), SUB), :]
        rates = jnp.log(block)
        total = jnp.zeros((SUB, STEPS), F32)
        for n in range(POLES):
            rate = rates[:, n : n + 1]
            lifted = block[:, POLES + n : POLES + n + 1] * jnp.exp(lag * rate)
            total = total + lifted
            at = pl.ds(n * SUB, SUB)
            gmat[g, at, :] = (lifted * block[:, n : n + 1]).astype(BF16)
            vmat[g, at, :] = jnp.exp((STEPS - 1 - lag) * rate).astype(BF16)
        kern[0, pl.ds(g * SUB, SUB), :] = total[:, :128]
        kern[1, pl.ds(g * SUB, SUB), :] = total[:, 128:]

    pl.semaphore_wait(ready.at[0], 3)
    pl.semaphore_signal(ready.at[1], inc=1, device_id=(flip, y, t), device_id_type=MESH)

    @pl.when(hi != home)
    def _():
        for k in range(2):
            arrived(core * 2 + k).wait()
            forward[k].start()

    def ids_to(other, device):
        return pltpu.make_async_remote_copy(
            src_ref=ids_ref, dst_ref=all_ids.at[y, pl.ds(i, 1), :], send_sem=ids_send.at[other],
            recv_sem=ids_recv.at[me], device_id=device, device_id_type=MESH,
        )

    pltpu.make_async_copy(ids_ref, all_ids.at[y, pl.ds(i, 1), :], ids_recv.at[me]).start()
    pl.semaphore_wait(ready.at[1], 1)
    for other, device in others:
        ids_to(other, device).start()

    for k in range(1, TP):
        source = lax.rem(t + k, TP)
        pltpu.make_async_copy(squares.at[source], squares.at[source], sq_recv.at[source]).wait()
    total = squares[0] + squares[1] + squares[2] + squares[3]
    scale = lax.rsqrt(total[0:1, :] * (1.0 / (FEAT * FSDP)) + norm_eps)
    scale = jnp.sum(jnp.where(diagonal, scale, 0.0), axis=1, keepdims=True)

    @pl.when(hi == home)
    def _():
        for k in range(2):
            arrived(core * 2 + k).wait()

    for k in range(2):
        arrived((1 - core) * 2 + k).wait()
    gain = gain_buf[:, pl.ds(pl.multiple_of(y * FEAT, FEAT), FEAT)]
    normed = (rows[...].astype(F32) * scale * gain).astype(BF16)

    lane_block = lax.div(iota((48, 128), 1), SLICE)

    def part_to(slot, device):
        return pltpu.make_async_remote_copy(
            src_ref=send_buf.at[slot], dst_ref=parts.at[me], send_sem=part_send.at[slot], recv_sem=part_recv.at[i],
            device_id=device, device_id_type=MESH,
        )

    mine_at = lax.rem(me, 8)

    def receivers(step):
        for dx, dz, dy in OFFSETS:
            if dx == FAR_X[step]:
                oz, oy = lax.rem(lax.rem(i, 2) + dz, 2), lax.rem(y + dy, FSDP)
                yield oz * FSDP + oy, (turn[step] * 2 + oz, oy, t)

    for step in range(CHUNKS):
        weight_copy(step).wait()
        dots = [jnp.dot(normed, weight_buf[step, stream], preferred_element_type=F32) for stream in range(3)]
        for half in range(CHUNK // 128):
            cols = [dot[:, half * 128 : half * 128 + 128] for dot in dots]
            for b in range(4):
                base = [pltpu.roll(c, (32 * (s - b)) % 128, 1) if (s - b) % 4 else c for s, c in enumerate(cols)]
                tail = jnp.concatenate(
                    [pltpu.roll(c[48:64], (32 * (3 - b)) % 128, 1) if (3 - b) % 4 else c[48:64] for c in cols], axis=0
                )
                piece = jnp.where(
                    lane_block == 0,
                    base[0][:48],
                    jnp.where(lane_block == 1, base[1][:48], jnp.where(lane_block == 2, base[2][:48], tail)),
                )
                send_buf[step * 8 + half * 4 + b] = piece.astype(BF16)
        for slot, device in receivers(step):
            part_to(step * 8 + slot, device).start()
        if FAR_X[step] == 0:
            pltpu.make_async_copy(send_buf.at[step * 8 + mine_at], parts.at[me], part_recv.at[i]).start()

    odd = [lax.rem(lax.div(iota((8, 128), 0), 2**bit), 2) == 1 for bit in range(3)]
    above = iota((128, 128), 1) >= iota((128, 128), 0)

    def fill(g, carry):
        block = pl.ds(pl.multiple_of(g * SUB, SUB), SUB)
        lags = [kern[half, block, :] for half in range(2)]
        bases = [[jnp.broadcast_to(x[k : k + 1], (8, 128)) for x in lags] for k in range(SUB)]
        for bit in range(3):
            bases = [[jnp.where(odd[bit], pltpu.roll(x, 2**bit, 1), x) for x in pair] for pair in bases]
        for k in range(SUB):
            shifted = [
                jnp.concatenate([pltpu.roll(x, 8 * m, 1) if m else x for m in range(16)], axis=0) for x in bases[k]
            ]
            kmat[g * SUB + k, :, pl.ds(0, 128)] = jnp.where(above, shifted[0], 0.0).astype(BF16)
            kmat[g * SUB + k, :, pl.ds(128, 128)] = jnp.where(above, shifted[1], shifted[0]).astype(BF16)
        return carry

    vocab_row = iota((VOCAB // 2, STEPS), 0)

    def hot(s, carry):
        for j in range(CTX):
            landed = all_ids.at[s, pl.ds(j, 1), :]
            pltpu.make_async_copy(ids_ref, landed, ids_recv.at[j * FSDP + s]).wait()
            row = all_ids[s, pl.ds(j, 1), :]
            low = jnp.where(row >= VOCAB // 2, row - VOCAB // 2, row)
            onehot[s * CTX + j] = jnp.where(vocab_row == low, 1.0, 0.0).astype(BF16)
        return carry

    lax.fori_loop(0, SLICE // SUB, fill, 0)
    lax.fori_loop(0, FSDP, hot, 0)

    block16 = lax.div(iota((16, 128), 1), SLICE)
    for v in range(CTX):
        four = parts.at[pl.ds(v * 4, 4)]
        pltpu.make_async_copy(four, four, part_recv.at[v]).wait()
        a = parts[v * 4].astype(F32)
        for k in range(1, 4):
            a = a + parts[v * 4 + k].astype(F32)
        tail = [pltpu.roll(a[16 * s : 16 * s + 16], SLICE * (s + 1), 1) for s in range(3)]
        last = jnp.where(block16 == 0, tail[0], jnp.where(block16 == 1, tail[1], tail[2]))
        whole[pl.ds(v * ROWS, 48), :] = a
        whole[pl.ds(v * ROWS + 48, 16), :] = last
    for v in range(VOCAB // 128):
        turned = whole[pl.ds(v * 128, 128), :].T
        to = pl.ds(v // 2 * 3 * SLICE, 3 * SLICE)
        table[to, pl.ds(v % 2 * 128, 128)] = turned[: 3 * SLICE].astype(BF16)

    def gather(s, carry):
        for j in range(CTX):
            at = s * CTX + j
            both = jnp.dot(table[...], onehot[at], preferred_element_type=F32)
            upper = all_ids[s, pl.ds(j, 1), :] >= VOCAB // 2
            for half in range(2):
                cols = slice(half * 128, half * 128 + 128)
                raw[half, at] = jnp.where(upper[:, cols], both[3 * SLICE :, cols], both[: 3 * SLICE, cols])
        return carry

    lax.fori_loop(0, FSDP, gather, 0)

    lane = iota((SUB, 128), 1)

    def featurize(g):
        block = params[pl.ds(pl.multiple_of(y * SLICE + g * SUB, SUB), SUB), :]
        taps = [
            [
                jnp.broadcast_to(block[:, 2 * POLES + 3 * s + n : 2 * POLES + 3 * s + n + 1], (SUB, 128))
                for n in range(3)
            ]
            for s in range(3)
        ]
        for at in range(GROUP):
            if at % CTX == 0:
                before = [[jnp.zeros((SUB, 128), F32)] * 2] * 3
            for half in range(2):
                done = []
                for s in range(3):
                    now = raw[half, at, pl.ds(s * SLICE + g * SUB, SUB), :]
                    moved = [pltpu.roll(now, n, 1) for n in (1, 2)]
                    total = taps[s][0] * now
                    for n in (1, 2):
                        total = total + taps[s][n] * jnp.where(lane < n, before[s][n - 1], moved[n - 1])
                    before = before[:s] + [moved] + before[s + 1 :]
                    done.append(total)
                to = pl.ds(at * SUB, SUB)
                query[g][half, to, :] = done[0]
                product[g][half, to, :] = done[1] * done[2]

    same = lax.div(iota((SUB * GROUP, 128), 0), GROUP) == lax.rem(iota((SUB * GROUP, 128), 1), SUB)
    chunk = lax.rem(iota((SUB * GROUP, 128), 0), CTX)
    diagonal128 = iota((128, 128), 0) == iota((128, 128), 1)

    def convolve(g):
        block = params[pl.ds(pl.multiple_of(y * SLICE + g * SUB, SUB), SUB), :]
        decay = jnp.concatenate(
            [jnp.broadcast_to(block[:, n : n + 1], (SUB, 128)) for n in range(POLES)], axis=0
        )
        decay = jnp.sum(jnp.where(diagonal128, decay, 0.0), axis=0, keepdims=True)
        for _ in range(8):
            decay = decay * decay
        halves = [
            [product[g][half, pl.ds(k, GROUP, stride=SUB), :].astype(BF16) for half in range(2)] for k in range(SUB)
        ]
        inputs = jnp.concatenate([jnp.concatenate(x, axis=1) for x in halves], axis=0)
        states = lax.dot_general(inputs, vmat[g], (((1,), (1,)), ((), ())), preferred_element_type=F32)
        inner = []
        for k in range(SUB):
            both = jnp.dot(jnp.concatenate(halves[k], axis=0), kmat[g * SUB + k], preferred_element_type=F32)
            inner.append([both[:GROUP, :128], both[:GROUP, 128:] + both[GROUP:, :128]])
        states = jnp.where(same, states, 0.0)
        states = jnp.where(chunk < 1, 0.0, pltpu.roll(states, 1, 0))
        for by in (1, 2, 4):
            states = states + decay * jnp.where(chunk < by, 0.0, pltpu.roll(states, by, 0))
            decay = decay * decay
        carried = jnp.dot(states.astype(BF16), gmat[g], preferred_element_type=F32)
        for k in range(SUB):
            for half in range(2):
                mixed[g][half, pl.ds(k, GROUP, stride=SUB), :] = (
                    inner[k][half] + carried[k * GROUP : (k + 1) * GROUP, half * 128 : half * 128 + 128]
                )

    groups = SLICE // SUB
    featurize(0)
    for g in range(groups):
        if g + 1 < groups:
            featurize(g + 1)
        convolve(g)

    mine_params = params[pl.ds(pl.multiple_of(y * SLICE, SLICE), SLICE), :]
    skip = jnp.broadcast_to(mine_params[:, 2 * POLES + 9 : 2 * POLES + 10], (SLICE, 128))
    pieces = onehot

    def out_to(other, device):
        return pltpu.make_async_remote_copy(
            src_ref=pieces.at[other, pl.ds(0, SLICE), :], dst_ref=out_ref.at[me], send_sem=out_send.at[other],
            recv_sem=out_recv, device_id=device, device_id_type=MESH,
        )

    def gate(other):
        s = lax.rem(other, FSDP)
        j = lax.div(other, FSDP)
        at = pl.ds(pl.multiple_of((s * CTX + j) * SUB, SUB), SUB)
        for half in range(2):
            q, u, c = [
                jnp.concatenate([x[g][half, at, :] for g in range(groups)], axis=0) for x in (query, product, mixed)
            ]
            pieces[other, pl.ds(0, SLICE), pl.ds(half * 128, 128)] = (q * (c + skip * u)).astype(BF16)

    for other, device in others:
        gate(other)
        out_to(other, device).start()
    gate(me)
    pltpu.make_async_copy(pieces.at[me, pl.ds(0, SLICE), :], out_ref.at[me], out_recv).start()

    for k in range(1, TP):
        squares_to(k).wait_send()

    @pl.when(t == y)
    def _():
        for copy in handed:
            copy.wait_send()

    @pl.when(hi != home)
    def _():
        for copy in forward:
            copy.wait_send()

    for step in range(CHUNKS):
        for slot, device in receivers(step):
            part_to(step * 8 + slot, device).wait_send()

    for other, device in others:
        ids_to(other, device).wait_send()
        out_to(other, device).wait_send()

    pltpu.make_async_copy(out_ref, out_ref, out_recv).wait()


def block(*args):
    hbm = pl.BlockSpec(memory_space=pltpu.HBM)
    dma = pltpu.SemaphoreType.DMA
    groups = SLICE // SUB
    return pl.pallas_call(
        block_kernel,
        out_shape=jax.ShapeDtypeStruct((GROUP, SLICE, STEPS), BF16),
        in_specs=[hbm] * 8,
        out_specs=hbm,
        scratch_shapes=[
            pltpu.VMEM((CHUNKS, 3, FEAT, CHUNK), BF16),
            pltpu.VMEM((ROWS, FEAT), BF16),
            pltpu.VMEM((ROWS, FEAT), BF16),
            pltpu.VMEM((ROWS, FEAT), BF16),
            pltpu.VMEM((TP, 8, 128), F32),
            pltpu.VMEM((GROUP, 48, 128), BF16),
            pltpu.VMEM((GROUP, 48, 128), BF16),
            pltpu.VMEM((FSDP, CTX, STEPS), jnp.int32),
            pltpu.VMEM((1, FEAT * FSDP), F32),
            pltpu.VMEM((3, 3, CHAN), F32),
            pltpu.VMEM((POLES, CHAN), F32),
            pltpu.VMEM((POLES, CHAN), F32),
            pltpu.VMEM((1, CHAN), F32),
            pltpu.VMEM((128, 128), F32),
            pltpu.VMEM((2, SLICE, 128), F32),
            pltpu.VMEM((SLICE, STEPS // 2, STEPS), BF16),
            pltpu.VMEM((groups, POLES * SUB, STEPS), BF16),
            pltpu.VMEM((groups, POLES * SUB, STEPS), BF16),
            pltpu.VMEM((GROUP, VOCAB // 2, STEPS), BF16),
            pltpu.VMEM((6 * SLICE, VOCAB // 2), BF16),
            pltpu.VMEM((VOCAB, 128), F32),
            pltpu.VMEM((2, GROUP, 3 * SLICE, 128), F32),
            [pltpu.VMEM((2, GROUP * SUB, 128), F32) for _ in range(groups)],
            [pltpu.VMEM((2, GROUP * SUB, 128), F32) for _ in range(groups)],
            [pltpu.VMEM((2, GROUP * SUB, 128), F32) for _ in range(groups)],
            dma((CHUNKS,)),
            dma,
            dma,
            dma((5,)),
            dma((4,)),
            dma((8,)),
            dma((TP,)),
            dma((TP,)),
            dma((GROUP,)),
            dma((GROUP,)),
            dma((GROUP,)),
            dma((CTX,)),
            dma((GROUP,)),
            dma,
            pltpu.SemaphoreType.REGULAR((2,)),
        ],
        compiler_params=pltpu.CompilerParams(
            collective_id=0, has_side_effects=True, vmem_limit_bytes=56 * 2**20
        ),
        name="hyena_block",
    )(*args)


def shards(
    base_ids, embed_table, norm_gain, in_weight, conv_taps, modal_poles, residues, skip_gain
):
    landed = block(
        base_ids, embed_table, norm_gain.reshape(1, -1), jnp.transpose(in_weight, (1, 0, 2)),
        conv_taps, modal_poles, residues, skip_gain.reshape(1, -1),
    )
    return landed.reshape(CHAN, STEPS).T[None]


def solution(mesh):
    in_specs = (
        P("fsdp", "ctx"),
        P(None, "tp"),
        P(),
        P("fsdp", None, "tp"),
        P(None, None, "tp"),
        P(None, "tp"),
        P(None, "tp"),
        P("tp"),
    )
    out_specs = P("fsdp", "ctx", "tp")
    return jax.shard_map(shards, mesh=mesh, in_specs=in_specs, out_specs=out_specs, check_vma=False)
```

```python
import jax
import jax.numpy as jnp
from jax import lax
from jax.experimental import pallas as pl
from jax.experimental.pallas import tpu as pltpu
from jax.sharding import PartitionSpec as P

MESH = pl.DeviceIdType.MESH
F32 = jnp.float32
BF16 = jnp.bfloat16
norm_eps = 1e-06

CTX, FSDP, TP = 8, 4, 4
GROUP = CTX * FSDP
VOCAB = 512
ROWS = VOCAB // CTX
FEAT = 2048
CHAN = 1024
SLICE = CHAN // GROUP
STEPS = 256
POLES = 16
CHUNK = 256
CHUNKS = CHAN // CHUNK
SUB = 8


def iota(shape, dim):
    return lax.broadcasted_iota(jnp.int32, shape, dim)


OFFSETS = sorted(
    [(x, z, y) for x in range(4) for z in range(2) for y in range(4) if (x, z, y) != (0, 0, 0)],
    key=lambda o: -(min(o[0], 4 - o[0]) + o[1] + min(o[2], 4 - o[2])),
)


FAR_X = (2, 1, 3, 0)


def block_kernel(
    ids_ref, table_ref, gain_ref, weight_ref, taps_ref, poles_ref, res_ref, skip_ref, out_ref,
    weight_buf, own, rows, squares, send_buf, parts, all_ids, gain_buf, taps_buf, poles_buf, res_buf, skip_buf,
    params, kern, kmat, vmat, gmat, onehot, table, whole, raw, product, query, mixed,
    weight_sem, own_sem, small_sem, rows_sem, rows_send, sq_send, sq_recv, ids_send, ids_recv, part_send, part_recv,
    out_send, out_recv, ready,
):
    i = lax.axis_index("ctx")
    y = lax.axis_index("fsdp")
    t = lax.axis_index("tp")
    me = i * FSDP + y
    hi = lax.div(t, 2)
    flip = i + 1 - 2 * lax.rem(i, 2)
    turn = [lax.rem(lax.div(i, 2) + x, CHUNKS) for x in FAR_X]
    here = pl.ds(pl.multiple_of(i * 128, 128), 128)

    others = []
    for dx, dz, dy in OFFSETS:
        oi = lax.rem(lax.div(i, 2) + dx, 4) * 2 + lax.rem(lax.rem(i, 2) + dz, 2)
        oy = lax.rem(y + dy, FSDP)
        others.append((oi * FSDP + oy, (oi, oy, t)))

    barrier = pltpu.get_barrier_semaphore()

    def greet(device):
        pl.semaphore_signal(barrier, inc=1, device_id=device, device_id_type=MESH)

    for k in range(1, TP):
        greet((i, y, lax.rem(t + k, TP)))
    for core in range(2):
        greet((flip, y, (1 - hi) * 2 + core))
    for k in range(1, FSDP):
        greet((i, lax.rem(y + k, FSDP), t))
    columns_of = [(lax.rem(i + k, CTX), y, t) for k in range(1, CTX)]
    for device in columns_of:
        greet(device)

    def table_rows(block):
        return table_ref.at[pl.ds(pl.multiple_of(block * ROWS, ROWS), ROWS), :]

    def columns(step):
        return pl.ds(pl.multiple_of(turn[step] * CHUNK, CHUNK), CHUNK)

    def weight_copy(step):
        return pltpu.make_async_copy(weight_ref.at[:, :, columns(step)], weight_buf.at[step], weight_sem.at[step])

    own_copy = pltpu.make_async_copy(table_rows(i), own, own_sem)
    own_copy.start()
    small = [
        pltpu.make_async_copy(poles_ref, poles_buf, small_sem.at[0]),
        pltpu.make_async_copy(res_ref, res_buf, small_sem.at[1]),
        pltpu.make_async_copy(taps_ref, taps_buf, small_sem.at[2]),
        pltpu.make_async_copy(skip_ref, skip_buf, small_sem.at[3]),
        pltpu.make_async_copy(gain_ref, gain_buf, small_sem.at[4]),
    ]
    for copy in small:
        copy.start()
    for step in range(CHUNKS):
        weight_copy(step).start()

    pl.semaphore_wait(barrier, TP - 1 + 2 + FSDP - 1 + CTX - 1)

    piece_rows = ROWS // 4
    core = lax.rem(t, 2)
    sibling = hi * 2 + 1 - core
    home = lax.div(y, 2)

    def piece(ref, at):
        return ref.at[pl.ds(pl.multiple_of(at * piece_rows, piece_rows), piece_rows), :]

    def piece_to(source, at, device, slot):
        return pltpu.make_async_remote_copy(
            src_ref=piece(source, at), dst_ref=piece(rows, at), send_sem=rows_send.at[slot], recv_sem=rows_sem.at[at],
            device_id=device, device_id_type=MESH,
        )

    def arrived(at):
        return pltpu.make_async_copy(piece(rows, at), piece(rows, at), rows_sem.at[at])

    order = (0, 2, 1, 3)
    handed = [piece_to(table_rows(flip), at, (flip, y, (1 - hi) * 2 + at // 2), at) for at in order] + [
        piece_to(table_rows(i), at, (i, y, sibling), 4 + at) for at in order
    ]
    forward = [piece_to(rows, core * 2 + k, (i, y, sibling), k) for k in range(2)]

    @pl.when(t == y)
    def _():
        for copy in handed:
            copy.start()
        for at in range(4):
            pltpu.make_async_copy(piece(table_rows(i), at), piece(rows, at), rows_sem.at[at]).start()

    for device in columns_of:
        pl.semaphore_signal(ready, inc=1, device_id=device, device_id_type=MESH)

    own_copy.wait()
    mine = own[...].astype(F32)
    sums = jnp.sum(mine * mine, axis=1, keepdims=True)
    diagonal = iota((ROWS, 128), 0) == iota((ROWS, 128), 1)
    flat = jnp.sum(jnp.where(diagonal, sums, 0.0), axis=0, keepdims=True)
    squares[t] = jnp.broadcast_to(flat, (8, 128))

    def squares_to(k):
        return pltpu.make_async_remote_copy(
            src_ref=squares.at[t], dst_ref=squares.at[t], send_sem=sq_send.at[k], recv_sem=sq_recv.at[t],
            device_id=(i, y, lax.rem(t + k, TP)), device_id_type=MESH,
        )

    for k in range(1, TP):
        squares_to(k).start()

    for copy in small:
        copy.wait()
    stacked = jnp.concatenate(
        [poles_buf[:, here], res_buf[:, here]]
        + [taps_buf[s, n : n + 1, here] for s in range(3) for n in range(3)]
        + [skip_buf[:, here], jnp.zeros((128 - 2 * POLES - 10, 128), F32)],
        axis=0,
    )
    params[...] = stacked.T

    lag = iota((SUB, STEPS), 1).astype(F32)
    for g in range(SLICE // SUB):
        block = params[pl.ds(pl.multiple_of(y * SLICE + g * SUB, SUB), SUB), :]
        rates = jnp.log(block)
        total = jnp.zeros((SUB, STEPS), F32)
        for n in range(POLES):
            rate = rates[:, n : n + 1]
            lifted = block[:, POLES + n : POLES + n + 1] * jnp.exp(lag * rate)
            total = total + lifted
            at = pl.ds(n * SUB, SUB)
            gmat[g, at, :] = (lifted * block[:, n : n + 1]).astype(BF16)
            vmat[g, at, :] = jnp.exp((STEPS - 1 - lag) * rate).astype(BF16)
        kern[0, pl.ds(g * SUB, SUB), :] = total[:, :128]
        kern[1, pl.ds(g * SUB, SUB), :] = total[:, 128:]

    @pl.when(hi != home)
    def _():
        for k in range(2):
            arrived(core * 2 + k).wait()
            forward[k].start()

    def ids_to(other, device):
        return pltpu.make_async_remote_copy(
            src_ref=ids_ref, dst_ref=all_ids.at[y, pl.ds(i, 1), :], send_sem=ids_send.at[other],
            recv_sem=ids_recv.at[me], device_id=device, device_id_type=MESH,
        )

    pltpu.make_async_copy(ids_ref, all_ids.at[y, pl.ds(i, 1), :], ids_recv.at[me]).start()
    pl.semaphore_wait(ready, CTX - 1)
    for other, device in others:
        ids_to(other, device).start()

    for k in range(1, TP):
        source = lax.rem(t + k, TP)
        pltpu.make_async_copy(squares.at[source], squares.at[source], sq_recv.at[source]).wait()
    total = squares[0] + squares[1] + squares[2] + squares[3]
    scale = lax.rsqrt(total[0:1, :] * (1.0 / (FEAT * FSDP)) + norm_eps)
    scale = jnp.sum(jnp.where(diagonal, scale, 0.0), axis=1, keepdims=True)

    @pl.when(hi == home)
    def _():
        for k in range(2):
            arrived(core * 2 + k).wait()

    for k in range(2):
        arrived((1 - core) * 2 + k).wait()
    gain = gain_buf[:, pl.ds(pl.multiple_of(y * FEAT, FEAT), FEAT)]
    normed = (rows[...].astype(F32) * scale * gain).astype(BF16)

    lane_block = lax.div(iota((48, 128), 1), SLICE)

    def part_to(slot, device):
        return pltpu.make_async_remote_copy(
            src_ref=send_buf.at[slot], dst_ref=parts.at[me], send_sem=part_send.at[slot], recv_sem=part_recv.at[i],
            device_id=device, device_id_type=MESH,
        )

    mine_at = lax.rem(me, 8)

    def receivers(step):
        for dx, dz, dy in OFFSETS:
            if dx == FAR_X[step]:
                oz, oy = lax.rem(lax.rem(i, 2) + dz, 2), lax.rem(y + dy, FSDP)
                yield oz * FSDP + oy, (turn[step] * 2 + oz, oy, t)

    for step in range(CHUNKS):
        weight_copy(step).wait()
        dots = [jnp.dot(normed, weight_buf[step, stream], preferred_element_type=F32) for stream in range(3)]
        for half in range(CHUNK // 128):
            cols = [dot[:, half * 128 : half * 128 + 128] for dot in dots]
            for b in range(4):
                base = [pltpu.roll(c, (32 * (s - b)) % 128, 1) if (s - b) % 4 else c for s, c in enumerate(cols)]
                tail = jnp.concatenate(
                    [pltpu.roll(c[48:64], (32 * (3 - b)) % 128, 1) if (3 - b) % 4 else c[48:64] for c in cols], axis=0
                )
                piece = jnp.where(
                    lane_block == 0,
                    base[0][:48],
                    jnp.where(lane_block == 1, base[1][:48], jnp.where(lane_block == 2, base[2][:48], tail)),
                )
                send_buf[step * 8 + half * 4 + b] = piece.astype(BF16)
        for slot, device in receivers(step):
            part_to(step * 8 + slot, device).start()
        if FAR_X[step] == 0:
            pltpu.make_async_copy(send_buf.at[step * 8 + mine_at], parts.at[me], part_recv.at[i]).start()

    odd = [lax.rem(lax.div(iota((8, 128), 0), 2**bit), 2) == 1 for bit in range(3)]
    above = iota((128, 128), 1) >= iota((128, 128), 0)

    def fill(g, carry):
        block = pl.ds(pl.multiple_of(g * SUB, SUB), SUB)
        lags = [kern[half, block, :] for half in range(2)]
        bases = [[jnp.broadcast_to(x[k : k + 1], (8, 128)) for x in lags] for k in range(SUB)]
        for bit in range(3):
            bases = [[jnp.where(odd[bit], pltpu.roll(x, 2**bit, 1), x) for x in pair] for pair in bases]
        for k in range(SUB):
            shifted = [
                jnp.concatenate([pltpu.roll(x, 8 * m, 1) if m else x for m in range(16)], axis=0) for x in bases[k]
            ]
            kmat[g * SUB + k, :, pl.ds(0, 128)] = jnp.where(above, shifted[0], 0.0).astype(BF16)
            kmat[g * SUB + k, :, pl.ds(128, 128)] = jnp.where(above, shifted[1], shifted[0]).astype(BF16)
        return carry

    vocab_row = iota((VOCAB // 2, STEPS), 0)

    def hot(s, carry):
        for j in range(CTX):
            landed = all_ids.at[s, pl.ds(j, 1), :]
            pltpu.make_async_copy(ids_ref, landed, ids_recv.at[j * FSDP + s]).wait()
            row = all_ids[s, pl.ds(j, 1), :]
            low = jnp.where(row >= VOCAB // 2, row - VOCAB // 2, row)
            onehot[s * CTX + j] = jnp.where(vocab_row == low, 1.0, 0.0).astype(BF16)
        return carry

    lax.fori_loop(0, SLICE // SUB, fill, 0)
    lax.fori_loop(0, FSDP, hot, 0)

    block16 = lax.div(iota((16, 128), 1), SLICE)
    for step in range(CHUNKS):
        pair = lax.rem(lax.div(i, 2) + 4 - FAR_X[step], CHUNKS)
        for z in range(2):
            four = parts.at[pl.ds((pair * 2 + z) * 4, 4)]
            pltpu.make_async_copy(four, four, part_recv.at[pair * 2 + z]).wait()
            a = parts[(pair * 2 + z) * 4].astype(F32)
            for k in range(1, 4):
                a = a + parts[(pair * 2 + z) * 4 + k].astype(F32)
            tail = [pltpu.roll(a[16 * s : 16 * s + 16], SLICE * (s + 1), 1) for s in range(3)]
            whole[pl.ds(z * ROWS, 48), :] = a
            whole[pl.ds(z * ROWS + 48, 16), :] = jnp.where(
                block16 == 0, tail[0], jnp.where(block16 == 1, tail[1], tail[2])
            )
        to = pl.ds(pl.multiple_of(lax.div(pair, 2) * (3 * SLICE), 3 * SLICE), 3 * SLICE)
        cols = pl.ds(pl.multiple_of(lax.rem(pair, 2) * 128, 128), 128)
        table[to, cols] = whole[...].T[: 3 * SLICE].astype(BF16)

    def gather(s, carry):
        for j in range(CTX):
            at = s * CTX + j
            both = jnp.dot(table[...], onehot[at], preferred_element_type=F32)
            upper = all_ids[s, pl.ds(j, 1), :] >= VOCAB // 2
            for half in range(2):
                cols = slice(half * 128, half * 128 + 128)
                raw[half, at] = jnp.where(upper[:, cols], both[3 * SLICE :, cols], both[: 3 * SLICE, cols])
        return carry

    lax.fori_loop(0, FSDP, gather, 0)

    lane = iota((SUB, 128), 1)

    def featurize(g):
        block = params[pl.ds(pl.multiple_of(y * SLICE + g * SUB, SUB), SUB), :]
        taps = [
            [
                jnp.broadcast_to(block[:, 2 * POLES + 3 * s + n : 2 * POLES + 3 * s + n + 1], (SUB, 128))
                for n in range(3)
            ]
            for s in range(3)
        ]
        for at in range(GROUP):
            if at % CTX == 0:
                before = [[jnp.zeros((SUB, 128), F32)] * 2] * 3
            for half in range(2):
                done = []
                for s in range(3):
                    now = raw[half, at, pl.ds(s * SLICE + g * SUB, SUB), :]
                    moved = [pltpu.roll(now, n, 1) for n in (1, 2)]
                    total = taps[s][0] * now
                    for n in (1, 2):
                        total = total + taps[s][n] * jnp.where(lane < n, before[s][n - 1], moved[n - 1])
                    before = before[:s] + [moved] + before[s + 1 :]
                    done.append(total)
                to = pl.ds(at * SUB, SUB)
                query[g][half, to, :] = done[0]
                product[g][half, to, :] = done[1] * done[2]

    same = lax.div(iota((SUB * GROUP, 128), 0), GROUP) == lax.rem(iota((SUB * GROUP, 128), 1), SUB)
    chunk = lax.rem(iota((SUB * GROUP, 128), 0), CTX)
    diagonal128 = iota((128, 128), 0) == iota((128, 128), 1)

    def convolve(g):
        block = params[pl.ds(pl.multiple_of(y * SLICE + g * SUB, SUB), SUB), :]
        decay = jnp.concatenate(
            [jnp.broadcast_to(block[:, n : n + 1], (SUB, 128)) for n in range(POLES)], axis=0
        )
        decay = jnp.sum(jnp.where(diagonal128, decay, 0.0), axis=0, keepdims=True)
        for _ in range(8):
            decay = decay * decay
        halves = [
            [product[g][half, pl.ds(k, GROUP, stride=SUB), :].astype(BF16) for half in range(2)] for k in range(SUB)
        ]
        inputs = jnp.concatenate([jnp.concatenate(x, axis=1) for x in halves], axis=0)
        states = lax.dot_general(inputs, vmat[g], (((1,), (1,)), ((), ())), preferred_element_type=F32)
        inner = []
        for k in range(SUB):
            both = jnp.dot(jnp.concatenate(halves[k], axis=0), kmat[g * SUB + k], preferred_element_type=F32)
            inner.append([both[:GROUP, :128], both[:GROUP, 128:] + both[GROUP:, :128]])
        states = jnp.where(same, states, 0.0)
        states = jnp.where(chunk < 1, 0.0, pltpu.roll(states, 1, 0))
        for by in (1, 2, 4):
            states = states + decay * jnp.where(chunk < by, 0.0, pltpu.roll(states, by, 0))
            decay = decay * decay
        carried = jnp.dot(states.astype(BF16), gmat[g], preferred_element_type=F32)
        for k in range(SUB):
            for half in range(2):
                mixed[g][half, pl.ds(k, GROUP, stride=SUB), :] = (
                    inner[k][half] + carried[k * GROUP : (k + 1) * GROUP, half * 128 : half * 128 + 128]
                )

    mine_params = params[pl.ds(pl.multiple_of(y * SLICE, SLICE), SLICE), :]
    skip = jnp.broadcast_to(mine_params[:, 2 * POLES + 9 : 2 * POLES + 10], (SLICE, 128))
    pieces = onehot

    def share(part):
        return pl.ds(part * 2 * SUB, 2 * SUB)

    def out_to(part, other, device):
        return pltpu.make_async_remote_copy(
            src_ref=pieces.at[other, share(part), :], dst_ref=out_ref.at[me, share(part), :],
            send_sem=out_send.at[part, other], recv_sem=out_recv, device_id=device, device_id_type=MESH,
        )

    def gate(part, other):
        s = lax.rem(other, FSDP)
        j = lax.div(other, FSDP)
        at = pl.ds(pl.multiple_of((s * CTX + j) * SUB, SUB), SUB)
        for half in range(2):
            q, u, c = [
                jnp.concatenate([x[2 * part + g][half, at, :] for g in range(2)], axis=0)
                for x in (query, product, mixed)
            ]
            gated = q * (c + skip[part * 2 * SUB : (part + 1) * 2 * SUB] * u)
            pieces[other, share(part), pl.ds(half * 128, 128)] = gated.astype(BF16)

    for part in range(2):
        featurize(2 * part)
        featurize(2 * part + 1)
        convolve(2 * part)
        convolve(2 * part + 1)
        for other, device in others:
            gate(part, other)
            out_to(part, other, device).start()
        gate(part, me)
        pltpu.make_async_copy(pieces.at[me, share(part), :], out_ref.at[me, share(part), :], out_recv).start()

    for k in range(1, TP):
        squares_to(k).wait_send()

    @pl.when(t == y)
    def _():
        for copy in handed:
            copy.wait_send()

    @pl.when(hi != home)
    def _():
        for copy in forward:
            copy.wait_send()

    for step in range(CHUNKS):
        for slot, device in receivers(step):
            part_to(step * 8 + slot, device).wait_send()

    for other, device in others:
        ids_to(other, device).wait_send()
        for part in range(2):
            out_to(part, other, device).wait_send()

    pltpu.make_async_copy(out_ref, out_ref, out_recv).wait()


def block(*args):
    hbm = pl.BlockSpec(memory_space=pltpu.HBM)
    dma = pltpu.SemaphoreType.DMA
    groups = SLICE // SUB
    return pl.pallas_call(
        block_kernel,
        out_shape=jax.ShapeDtypeStruct((GROUP, SLICE, STEPS), BF16),
        in_specs=[hbm] * 8,
        out_specs=hbm,
        scratch_shapes=[
            pltpu.VMEM((CHUNKS, 3, FEAT, CHUNK), BF16),
            pltpu.VMEM((ROWS, FEAT), BF16),
            pltpu.VMEM((ROWS, FEAT), BF16),
            pltpu.VMEM((TP, 8, 128), F32),
            pltpu.VMEM((GROUP, 48, 128), BF16),
            pltpu.VMEM((GROUP, 48, 128), BF16),
            pltpu.VMEM((FSDP, CTX, STEPS), jnp.int32),
            pltpu.VMEM((1, FEAT * FSDP), F32),
            pltpu.VMEM((3, 3, CHAN), F32),
            pltpu.VMEM((POLES, CHAN), F32),
            pltpu.VMEM((POLES, CHAN), F32),
            pltpu.VMEM((1, CHAN), F32),
            pltpu.VMEM((128, 128), F32),
            pltpu.VMEM((2, SLICE, 128), F32),
            pltpu.VMEM((SLICE, STEPS // 2, STEPS), BF16),
            pltpu.VMEM((groups, POLES * SUB, STEPS), BF16),
            pltpu.VMEM((groups, POLES * SUB, STEPS), BF16),
            pltpu.VMEM((GROUP, VOCAB // 2, STEPS), BF16),
            pltpu.VMEM((6 * SLICE, VOCAB // 2), BF16),
            pltpu.VMEM((2 * ROWS, 128), F32),
            pltpu.VMEM((2, GROUP, 3 * SLICE, 128), F32),
            [pltpu.VMEM((2, GROUP * SUB, 128), F32) for _ in range(groups)],
            [pltpu.VMEM((2, GROUP * SUB, 128), F32) for _ in range(groups)],
            [pltpu.VMEM((2, GROUP * SUB, 128), F32) for _ in range(groups)],
            dma((CHUNKS,)),
            dma,
            dma((5,)),
            dma((4,)),
            dma((8,)),
            dma((TP,)),
            dma((TP,)),
            dma((GROUP,)),
            dma((GROUP,)),
            dma((GROUP,)),
            dma((CTX,)),
            dma((2, GROUP)),
            dma,
            pltpu.SemaphoreType.REGULAR,
        ],
        compiler_params=pltpu.CompilerParams(
            collective_id=0, has_side_effects=True, vmem_limit_bytes=56 * 2**20
        ),
        name="hyena_block",
    )(*args)


def shards(
    base_ids, embed_table, norm_gain, in_weight, conv_taps, modal_poles, residues, skip_gain
):
    landed = block(
        base_ids, embed_table, norm_gain.reshape(1, -1), jnp.transpose(in_weight, (1, 0, 2)),
        conv_taps, modal_poles, residues, skip_gain.reshape(1, -1),
    )
    return landed.reshape(CHAN, STEPS).T[None]


def solution(mesh):
    in_specs = (
        P("fsdp", "ctx"),
        P(None, "tp"),
        P(),
        P("fsdp", None, "tp"),
        P(None, None, "tp"),
        P(None, "tp"),
        P(None, "tp"),
        P("tp"),
    )
    out_specs = P("fsdp", "ctx", "tp")
    return jax.shard_map(shards, mesh=mesh, in_specs=in_specs, out_specs=out_specs, check_vma=False)
```

```python
import jax
import jax.numpy as jnp
from jax import lax
from jax.experimental import pallas as pl
from jax.experimental.pallas import tpu as pltpu
from jax.sharding import PartitionSpec as P

MESH = pl.DeviceIdType.MESH
F32 = jnp.float32
BF16 = jnp.bfloat16
norm_eps = 1e-06

CTX, FSDP, TP = 8, 4, 4
GROUP = CTX * FSDP
VOCAB = 512
ROWS = VOCAB // CTX
FEAT = 2048
CHAN = 1024
SLICE = CHAN // GROUP
STEPS = 256
POLES = 16
CHUNK = 256
CHUNKS = CHAN // CHUNK
SUB = 8


def iota(shape, dim):
    return lax.broadcasted_iota(jnp.int32, shape, dim)


OFFSETS = sorted(
    [(x, z, y) for x in range(4) for z in range(2) for y in range(4) if (x, z, y) != (0, 0, 0)],
    key=lambda o: -(min(o[0], 4 - o[0]) + o[1] + min(o[2], 4 - o[2])),
)


FAR_X = (2, 1, 3, 0)


def block_kernel(
    ids_ref, table_ref, gain_ref, weight_ref, taps_ref, poles_ref, res_ref, skip_ref, out_ref,
    weight_buf, own, rows, squares, send_buf, parts, all_ids, gain_buf, taps_buf, poles_buf, res_buf, skip_buf,
    params, decays, kern, kmat, vmat, gmat, onehot, table, whole, raw, product, query, mixed,
    weight_sem, own_sem, small_sem, rows_sem, rows_send, sq_send, sq_recv, ids_send, ids_recv, part_send, part_recv,
    out_send, out_recv, ready,
):
    i = lax.axis_index("ctx")
    y = lax.axis_index("fsdp")
    t = lax.axis_index("tp")
    me = i * FSDP + y
    hi = lax.div(t, 2)
    flip = i + 1 - 2 * lax.rem(i, 2)
    turn = [lax.rem(lax.div(i, 2) + x, CHUNKS) for x in FAR_X]
    here = pl.ds(pl.multiple_of(i * 128, 128), 128)

    others = []
    for dx, dz, dy in OFFSETS:
        oi = lax.rem(lax.div(i, 2) + dx, 4) * 2 + lax.rem(lax.rem(i, 2) + dz, 2)
        oy = lax.rem(y + dy, FSDP)
        others.append((oi * FSDP + oy, (oi, oy, t)))

    barrier = pltpu.get_barrier_semaphore()

    def greet(device):
        pl.semaphore_signal(barrier, inc=1, device_id=device, device_id_type=MESH)

    for k in range(1, TP):
        greet((i, y, lax.rem(t + k, TP)))
    for core in range(2):
        greet((flip, y, (1 - hi) * 2 + core))
    for k in range(1, FSDP):
        greet((i, lax.rem(y + k, FSDP), t))
    columns_of = [(lax.rem(i + k, CTX), y, t) for k in range(1, CTX)]
    for device in columns_of:
        greet(device)

    def table_rows(block):
        return table_ref.at[pl.ds(pl.multiple_of(block * ROWS, ROWS), ROWS), :]

    def columns(step):
        return pl.ds(pl.multiple_of(turn[step] * CHUNK, CHUNK), CHUNK)

    def weight_copy(step):
        return pltpu.make_async_copy(weight_ref.at[:, :, columns(step)], weight_buf.at[step], weight_sem.at[step])

    own_copy = pltpu.make_async_copy(table_rows(i), own, own_sem)
    own_copy.start()
    small = [
        pltpu.make_async_copy(poles_ref, poles_buf, small_sem.at[0]),
        pltpu.make_async_copy(res_ref, res_buf, small_sem.at[1]),
        pltpu.make_async_copy(taps_ref, taps_buf, small_sem.at[2]),
        pltpu.make_async_copy(skip_ref, skip_buf, small_sem.at[3]),
        pltpu.make_async_copy(gain_ref, gain_buf, small_sem.at[4]),
    ]
    for copy in small:
        copy.start()
    for step in range(CHUNKS):
        weight_copy(step).start()

    pl.semaphore_wait(barrier, TP - 1 + 2 + FSDP - 1 + CTX - 1)

    piece_rows = ROWS // 4
    core = lax.rem(t, 2)
    sibling = hi * 2 + 1 - core
    home = lax.div(y, 2)

    def piece(ref, at):
        return ref.at[pl.ds(pl.multiple_of(at * piece_rows, piece_rows), piece_rows), :]

    def piece_to(source, at, device, slot):
        return pltpu.make_async_remote_copy(
            src_ref=piece(source, at), dst_ref=piece(rows, at), send_sem=rows_send.at[slot], recv_sem=rows_sem.at[at],
            device_id=device, device_id_type=MESH,
        )

    def arrived(at):
        return pltpu.make_async_copy(piece(rows, at), piece(rows, at), rows_sem.at[at])

    order = (0, 2, 1, 3)
    handed = [piece_to(table_rows(flip), at, (flip, y, (1 - hi) * 2 + at // 2), at) for at in order] + [
        piece_to(table_rows(i), at, (i, y, sibling), 4 + at) for at in order
    ]
    forward = [piece_to(rows, core * 2 + k, (i, y, sibling), k) for k in range(2)]

    @pl.when(t == y)
    def _():
        for copy in handed:
            copy.start()
        for at in range(4):
            pltpu.make_async_copy(piece(table_rows(i), at), piece(rows, at), rows_sem.at[at]).start()

    for device in columns_of:
        pl.semaphore_signal(ready, inc=1, device_id=device, device_id_type=MESH)

    own_copy.wait()
    mine = own[...].astype(F32)
    sums = jnp.sum(mine * mine, axis=1, keepdims=True)
    diagonal = iota((ROWS, 128), 0) == iota((ROWS, 128), 1)
    flat = jnp.sum(jnp.where(diagonal, sums, 0.0), axis=0, keepdims=True)
    squares[t] = jnp.broadcast_to(flat, (8, 128))

    def squares_to(k):
        return pltpu.make_async_remote_copy(
            src_ref=squares.at[t], dst_ref=squares.at[t], send_sem=sq_send.at[k], recv_sem=sq_recv.at[t],
            device_id=(i, y, lax.rem(t + k, TP)), device_id_type=MESH,
        )

    for k in range(1, TP):
        squares_to(k).start()

    for copy in small:
        copy.wait()
    stacked = jnp.concatenate(
        [poles_buf[:, here], res_buf[:, here]]
        + [taps_buf[s, n : n + 1, here] for s in range(3) for n in range(3)]
        + [skip_buf[:, here], jnp.zeros((128 - 2 * POLES - 10, 128), F32)],
        axis=0,
    )
    params[...] = stacked.T

    lag = iota((SUB, STEPS), 1).astype(F32)
    for g in range(SLICE // SUB):
        block = params[pl.ds(pl.multiple_of(y * SLICE + g * SUB, SUB), SUB), :]
        rates = jnp.log(block)
        total = jnp.zeros((SUB, STEPS), F32)
        for n in range(POLES):
            rate = rates[:, n : n + 1]
            lifted = block[:, POLES + n : POLES + n + 1] * jnp.exp(lag * rate)
            total = total + lifted
            at = pl.ds(n * SUB, SUB)
            gmat[g, at, :] = (lifted * block[:, n : n + 1]).astype(BF16)
            vmat[g, at, :] = jnp.exp((STEPS - 1 - lag) * rate).astype(BF16)
        kern[0, pl.ds(g * SUB, SUB), :] = total[:, :128]
        kern[1, pl.ds(g * SUB, SUB), :] = total[:, 128:]

    @pl.when(hi != home)
    def _():
        for k in range(2):
            arrived(core * 2 + k).wait()
            forward[k].start()

    def ids_to(other, device):
        return pltpu.make_async_remote_copy(
            src_ref=ids_ref, dst_ref=all_ids.at[y, pl.ds(i, 1), :], send_sem=ids_send.at[other],
            recv_sem=ids_recv.at[me], device_id=device, device_id_type=MESH,
        )

    pltpu.make_async_copy(ids_ref, all_ids.at[y, pl.ds(i, 1), :], ids_recv.at[me]).start()
    pl.semaphore_wait(ready, CTX - 1)
    for other, device in others:
        ids_to(other, device).start()

    for k in range(1, TP):
        source = lax.rem(t + k, TP)
        pltpu.make_async_copy(squares.at[source], squares.at[source], sq_recv.at[source]).wait()
    total = squares[0] + squares[1] + squares[2] + squares[3]
    scale = lax.rsqrt(total[0:1, :] * (1.0 / (FEAT * FSDP)) + norm_eps)
    scale = jnp.sum(jnp.where(diagonal, scale, 0.0), axis=1, keepdims=True)

    @pl.when(hi == home)
    def _():
        for k in range(2):
            arrived(core * 2 + k).wait()

    for k in range(2):
        arrived((1 - core) * 2 + k).wait()
    gain = gain_buf[:, pl.ds(pl.multiple_of(y * FEAT, FEAT), FEAT)]
    normed = (rows[...].astype(F32) * scale * gain).astype(BF16)

    lane_block = lax.div(iota((48, 128), 1), SLICE)

    def part_to(slot, device):
        return pltpu.make_async_remote_copy(
            src_ref=send_buf.at[slot], dst_ref=parts.at[me], send_sem=part_send.at[slot], recv_sem=part_recv.at[i],
            device_id=device, device_id_type=MESH,
        )

    mine_at = lax.rem(me, 8)

    def receivers(step):
        for dx, dz, dy in OFFSETS:
            if dx == FAR_X[step]:
                oz, oy = lax.rem(lax.rem(i, 2) + dz, 2), lax.rem(y + dy, FSDP)
                yield oz * FSDP + oy, (turn[step] * 2 + oz, oy, t)

    def multiply(step):
        weight_copy(step).wait()
        return [jnp.dot(normed, weight_buf[step, stream], preferred_element_type=F32) for stream in range(3)]

    following = multiply(0)
    for step in range(CHUNKS):
        dots = following
        if step + 1 < CHUNKS:
            following = multiply(step + 1)
        for half in range(CHUNK // 128):
            cols = [dot[:, half * 128 : half * 128 + 128] for dot in dots]
            for b in range(4):
                base = [pltpu.roll(c, (32 * (s - b)) % 128, 1) if (s - b) % 4 else c for s, c in enumerate(cols)]
                tail = jnp.concatenate(
                    [pltpu.roll(c[48:64], (32 * (3 - b)) % 128, 1) if (3 - b) % 4 else c[48:64] for c in cols], axis=0
                )
                piece = jnp.where(
                    lane_block == 0,
                    base[0][:48],
                    jnp.where(lane_block == 1, base[1][:48], jnp.where(lane_block == 2, base[2][:48], tail)),
                )
                send_buf[step * 8 + half * 4 + b] = piece.astype(BF16)
        for slot, device in receivers(step):
            part_to(step * 8 + slot, device).start()
        if FAR_X[step] == 0:
            pltpu.make_async_copy(send_buf.at[step * 8 + mine_at], parts.at[me], part_recv.at[i]).start()

    odd = [lax.rem(lax.div(iota((8, 128), 0), 2**bit), 2) == 1 for bit in range(3)]
    above = iota((128, 128), 1) >= iota((128, 128), 0)

    def fill(g, carry):
        block = pl.ds(pl.multiple_of(g * SUB, SUB), SUB)
        lags = [kern[half, block, :] for half in range(2)]
        bases = [[jnp.broadcast_to(x[k : k + 1], (8, 128)) for x in lags] for k in range(SUB)]
        for bit in range(3):
            bases = [[jnp.where(odd[bit], pltpu.roll(x, 2**bit, 1), x) for x in pair] for pair in bases]
        for k in range(SUB):
            shifted = [
                jnp.concatenate([pltpu.roll(x, 8 * m, 1) if m else x for m in range(16)], axis=0) for x in bases[k]
            ]
            kmat[g * SUB + k, :, pl.ds(0, 128)] = jnp.where(above, shifted[0], 0.0).astype(BF16)
            kmat[g * SUB + k, :, pl.ds(128, 128)] = jnp.where(above, shifted[1], shifted[0]).astype(BF16)
        return carry

    vocab_row = iota((VOCAB // 2, STEPS), 0)

    def hot(s, carry):
        for j in range(CTX):
            landed = all_ids.at[s, pl.ds(j, 1), :]
            pltpu.make_async_copy(ids_ref, landed, ids_recv.at[j * FSDP + s]).wait()
            row = all_ids[s, pl.ds(j, 1), :]
            low = jnp.where(row >= VOCAB // 2, row - VOCAB // 2, row)
            onehot[s * CTX + j] = jnp.where(vocab_row == low, 1.0, 0.0).astype(BF16)
        return carry

    lax.fori_loop(0, SLICE // SUB, fill, 0)
    diagonal128 = iota((128, 128), 0) == iota((128, 128), 1)
    for g in range(SLICE // SUB):
        block = params[pl.ds(pl.multiple_of(y * SLICE + g * SUB, SUB), SUB), :]
        decay = jnp.concatenate(
            [jnp.broadcast_to(block[:, n : n + 1], (SUB, 128)) for n in range(POLES)], axis=0
        )
        decay = jnp.sum(jnp.where(diagonal128, decay, 0.0), axis=0, keepdims=True)
        for _ in range(8):
            decay = decay * decay
        decays[g] = jnp.broadcast_to(decay, (8, 128))

    lax.fori_loop(0, FSDP, hot, 0)

    block16 = lax.div(iota((16, 128), 1), SLICE)
    for step in range(CHUNKS):
        pair = lax.rem(lax.div(i, 2) + 4 - FAR_X[step], CHUNKS)
        for z in range(2):
            four = parts.at[pl.ds((pair * 2 + z) * 4, 4)]
            pltpu.make_async_copy(four, four, part_recv.at[pair * 2 + z]).wait()
            a = parts[(pair * 2 + z) * 4].astype(F32)
            for k in range(1, 4):
                a = a + parts[(pair * 2 + z) * 4 + k].astype(F32)
            tail = [pltpu.roll(a[16 * s : 16 * s + 16], SLICE * (s + 1), 1) for s in range(3)]
            whole[pl.ds(z * ROWS, 48), :] = a
            whole[pl.ds(z * ROWS + 48, 16), :] = jnp.where(
                block16 == 0, tail[0], jnp.where(block16 == 1, tail[1], tail[2])
            )
        to = pl.ds(pl.multiple_of(lax.div(pair, 2) * (3 * SLICE), 3 * SLICE), 3 * SLICE)
        cols = pl.ds(pl.multiple_of(lax.rem(pair, 2) * 128, 128), 128)
        table[to, cols] = whole[...].T[: 3 * SLICE].astype(BF16)

    def gather(s, carry):
        for j in range(CTX):
            at = s * CTX + j
            both = jnp.dot(table[...], onehot[at], preferred_element_type=F32)
            upper = all_ids[s, pl.ds(j, 1), :] >= VOCAB // 2
            for half in range(2):
                cols = slice(half * 128, half * 128 + 128)
                raw[half, at] = jnp.where(upper[:, cols], both[3 * SLICE :, cols], both[: 3 * SLICE, cols])
        return carry

    lax.fori_loop(0, FSDP, gather, 0)

    lane = iota((SUB, 128), 1)

    def featurize(g):
        block = params[pl.ds(pl.multiple_of(y * SLICE + g * SUB, SUB), SUB), :]
        taps = [
            [
                jnp.broadcast_to(block[:, 2 * POLES + 3 * s + n : 2 * POLES + 3 * s + n + 1], (SUB, 128))
                for n in range(3)
            ]
            for s in range(3)
        ]
        for at in range(GROUP):
            if at % CTX == 0:
                before = [[jnp.zeros((SUB, 128), F32)] * 2] * 3
            for half in range(2):
                done = []
                for s in range(3):
                    now = raw[half, at, pl.ds(s * SLICE + g * SUB, SUB), :]
                    moved = [pltpu.roll(now, n, 1) for n in (1, 2)]
                    total = taps[s][0] * now
                    for n in (1, 2):
                        total = total + taps[s][n] * jnp.where(lane < n, before[s][n - 1], moved[n - 1])
                    before = before[:s] + [moved] + before[s + 1 :]
                    done.append(total)
                to = pl.ds(at * SUB, SUB)
                query[g][half, to, :] = done[0]
                product[g][half, to, :] = done[1] * done[2]

    channel = lax.rem(iota((GROUP, 128), 1), SUB)
    chunk = lax.rem(iota((GROUP, 128), 0), CTX)

    def convolve(g):
        decay = decays[g, 0:1, :]
        halves = [
            [product[g][half, pl.ds(k, GROUP, stride=SUB), :].astype(BF16) for half in range(2)] for k in range(SUB)
        ]
        inputs = jnp.concatenate([jnp.concatenate(x, axis=1) for x in halves], axis=0)
        states = lax.dot_general(inputs, vmat[g], (((1,), (1,)), ((), ())), preferred_element_type=F32)
        inner = []
        for k in range(SUB):
            both = jnp.dot(jnp.concatenate(halves[k], axis=0), kmat[g * SUB + k], preferred_element_type=F32)
            inner.append([both[:GROUP, :128], both[:GROUP, 128:] + both[GROUP:, :128]])
        stacked = states[:GROUP]
        for k in range(1, SUB):
            stacked = jnp.where(channel == k, states[k * GROUP : (k + 1) * GROUP], stacked)
        states = stacked
        states = jnp.where(chunk < 1, 0.0, pltpu.roll(states, 1, 0))
        for by in (1, 2, 4):
            states = states + decay * jnp.where(chunk < by, 0.0, pltpu.roll(states, by, 0))
            decay = decay * decay
        states = jnp.concatenate([jnp.where(channel == k, states, 0.0) for k in range(SUB)], axis=0)
        carried = jnp.dot(states.astype(BF16), gmat[g], preferred_element_type=F32)
        for k in range(SUB):
            for half in range(2):
                mixed[g][half, pl.ds(k, GROUP, stride=SUB), :] = (
                    inner[k][half] + carried[k * GROUP : (k + 1) * GROUP, half * 128 : half * 128 + 128]
                )

    mine_params = params[pl.ds(pl.multiple_of(y * SLICE, SLICE), SLICE), :]
    skip = jnp.broadcast_to(mine_params[:, 2 * POLES + 9 : 2 * POLES + 10], (SLICE, 128))
    pieces = onehot

    def share(part):
        return pl.ds(part * 2 * SUB, 2 * SUB)

    def out_to(part, other, device):
        return pltpu.make_async_remote_copy(
            src_ref=pieces.at[other, share(part), :], dst_ref=out_ref.at[me, share(part), :],
            send_sem=out_send.at[part, other], recv_sem=out_recv, device_id=device, device_id_type=MESH,
        )

    def gate(part, other):
        s = lax.rem(other, FSDP)
        j = lax.div(other, FSDP)
        at = pl.ds(pl.multiple_of((s * CTX + j) * SUB, SUB), SUB)
        for half in range(2):
            q, u, c = [
                jnp.concatenate([x[2 * part + g][half, at, :] for g in range(2)], axis=0)
                for x in (query, product, mixed)
            ]
            gated = q * (c + skip[part * 2 * SUB : (part + 1) * 2 * SUB] * u)
            pieces[other, share(part), pl.ds(half * 128, 128)] = gated.astype(BF16)

    for part in range(2):
        featurize(2 * part)
        featurize(2 * part + 1)
        convolve(2 * part)
        convolve(2 * part + 1)
        for other, device in others:
            gate(part, other)
            out_to(part, other, device).start()
        gate(part, me)
        pltpu.make_async_copy(pieces.at[me, share(part), :], out_ref.at[me, share(part), :], out_recv).start()

    for k in range(1, TP):
        squares_to(k).wait_send()

    @pl.when(t == y)
    def _():
        for copy in handed:
            copy.wait_send()

    @pl.when(hi != home)
    def _():
        for copy in forward:
            copy.wait_send()

    for step in range(CHUNKS):
        for slot, device in receivers(step):
            part_to(step * 8 + slot, device).wait_send()

    for other, device in others:
        ids_to(other, device).wait_send()
        for part in range(2):
            out_to(part, other, device).wait_send()

    pltpu.make_async_copy(out_ref, out_ref, out_recv).wait()


def block(*args):
    hbm = pl.BlockSpec(memory_space=pltpu.HBM)
    dma = pltpu.SemaphoreType.DMA
    groups = SLICE // SUB
    return pl.pallas_call(
        block_kernel,
        out_shape=jax.ShapeDtypeStruct((GROUP, SLICE, STEPS), BF16),
        in_specs=[hbm] * 8,
        out_specs=hbm,
        scratch_shapes=[
            pltpu.VMEM((CHUNKS, 3, FEAT, CHUNK), BF16),
            pltpu.VMEM((ROWS, FEAT), BF16),
            pltpu.VMEM((ROWS, FEAT), BF16),
            pltpu.VMEM((TP, 8, 128), F32),
            pltpu.VMEM((GROUP, 48, 128), BF16),
            pltpu.VMEM((GROUP, 48, 128), BF16),
            pltpu.VMEM((FSDP, CTX, STEPS), jnp.int32),
            pltpu.VMEM((1, FEAT * FSDP), F32),
            pltpu.VMEM((3, 3, CHAN), F32),
            pltpu.VMEM((POLES, CHAN), F32),
            pltpu.VMEM((POLES, CHAN), F32),
            pltpu.VMEM((1, CHAN), F32),
            pltpu.VMEM((128, 128), F32),
            pltpu.VMEM((groups, 8, 128), F32),
            pltpu.VMEM((2, SLICE, 128), F32),
            pltpu.VMEM((SLICE, STEPS // 2, STEPS), BF16),
            pltpu.VMEM((groups, POLES * SUB, STEPS), BF16),
            pltpu.VMEM((groups, POLES * SUB, STEPS), BF16),
            pltpu.VMEM((GROUP, VOCAB // 2, STEPS), BF16),
            pltpu.VMEM((6 * SLICE, VOCAB // 2), BF16),
            pltpu.VMEM((2 * ROWS, 128), F32),
            pltpu.VMEM((2, GROUP, 3 * SLICE, 128), F32),
            [pltpu.VMEM((2, GROUP * SUB, 128), F32) for _ in range(groups)],
            [pltpu.VMEM((2, GROUP * SUB, 128), F32) for _ in range(groups)],
            [pltpu.VMEM((2, GROUP * SUB, 128), F32) for _ in range(groups)],
            dma((CHUNKS,)),
            dma,
            dma((5,)),
            dma((4,)),
            dma((8,)),
            dma((TP,)),
            dma((TP,)),
            dma((GROUP,)),
            dma((GROUP,)),
            dma((GROUP,)),
            dma((CTX,)),
            dma((2, GROUP)),
            dma,
            pltpu.SemaphoreType.REGULAR,
        ],
        compiler_params=pltpu.CompilerParams(
            collective_id=0, has_side_effects=True, vmem_limit_bytes=56 * 2**20
        ),
        name="hyena_block",
    )(*args)


def shards(
    base_ids, embed_table, norm_gain, in_weight, conv_taps, modal_poles, residues, skip_gain
):
    landed = block(
        base_ids, embed_table, norm_gain.reshape(1, -1), jnp.transpose(in_weight, (1, 0, 2)),
        conv_taps, modal_poles, residues, skip_gain.reshape(1, -1),
    )
    return landed.reshape(CHAN, STEPS).T[None]


def solution(mesh):
    in_specs = (
        P("fsdp", "ctx"),
        P(None, "tp"),
        P(),
        P("fsdp", None, "tp"),
        P(None, None, "tp"),
        P(None, "tp"),
        P(None, "tp"),
        P("tp"),
    )
    out_specs = P("fsdp", "ctx", "tp")
    return jax.shard_map(shards, mesh=mesh, in_specs=in_specs, out_specs=out_specs, check_vma=False)
```

```python
import jax
import jax.numpy as jnp
from jax import lax
from jax.experimental import pallas as pl
from jax.experimental.pallas import tpu as pltpu
from jax.sharding import PartitionSpec as P

MESH = pl.DeviceIdType.MESH
F32 = jnp.float32
BF16 = jnp.bfloat16
norm_eps = 1e-06

CTX, FSDP, TP = 8, 4, 4
GROUP = CTX * FSDP
VOCAB = 512
ROWS = VOCAB // CTX
FEAT = 2048
CHAN = 1024
SLICE = CHAN // GROUP
STEPS = 256
POLES = 16
CHUNK = 256
CHUNKS = CHAN // CHUNK
SUB = 8


def iota(shape, dim):
    return lax.broadcasted_iota(jnp.int32, shape, dim)


OFFSETS = sorted(
    [(x, z, y) for x in range(4) for z in range(2) for y in range(4) if (x, z, y) != (0, 0, 0)],
    key=lambda o: -(min(o[0], 4 - o[0]) + o[1] + min(o[2], 4 - o[2])),
)


FAR_X = (2, 1, 3, 0)


def block_kernel(
    ids_ref, table_ref, gain_ref, weight_ref, taps_ref, poles_ref, res_ref, skip_ref, out_ref,
    weight_buf, own, rows, squares, send_buf, parts, all_ids, gain_buf, taps_buf, poles_buf, res_buf, skip_buf,
    params, decays, kern, kmat, vmat, gmat, onehot, table, whole, raw, product, query, mixed,
    weight_sem, own_sem, small_sem, rows_sem, rows_send, sq_send, sq_recv, ids_send, ids_recv, part_send, part_recv,
    out_send, out_recv, ready,
):
    i = lax.axis_index("ctx")
    y = lax.axis_index("fsdp")
    t = lax.axis_index("tp")
    me = i * FSDP + y
    hi = lax.div(t, 2)
    flip = i + 1 - 2 * lax.rem(i, 2)
    turn = [lax.rem(lax.div(i, 2) + x, CHUNKS) for x in FAR_X]
    here = pl.ds(pl.multiple_of(i * 128, 128), 128)

    others = []
    for dx, dz, dy in OFFSETS:
        oi = lax.rem(lax.div(i, 2) + dx, 4) * 2 + lax.rem(lax.rem(i, 2) + dz, 2)
        oy = lax.rem(y + dy, FSDP)
        others.append((oi * FSDP + oy, (oi, oy, t)))

    barrier = pltpu.get_barrier_semaphore()

    def greet(device):
        pl.semaphore_signal(barrier, inc=1, device_id=device, device_id_type=MESH)

    for k in range(1, TP):
        greet((i, y, lax.rem(t + k, TP)))
    for core in range(2):
        greet((flip, y, (1 - hi) * 2 + core))
    for k in range(1, FSDP):
        greet((i, lax.rem(y + k, FSDP), t))
    columns_of = [(lax.rem(i + k, CTX), y, t) for k in range(1, CTX)]
    for device in columns_of:
        greet(device)

    def table_rows(block):
        return table_ref.at[pl.ds(pl.multiple_of(block * ROWS, ROWS), ROWS), :]

    def columns(step):
        return pl.ds(pl.multiple_of(turn[step] * CHUNK, CHUNK), CHUNK)

    def weight_copy(step):
        return pltpu.make_async_copy(weight_ref.at[:, :, columns(step)], weight_buf.at[step], weight_sem.at[step])

    own_copy = pltpu.make_async_copy(table_rows(i), own, own_sem)
    own_copy.start()
    small = [
        pltpu.make_async_copy(poles_ref, poles_buf, small_sem.at[0]),
        pltpu.make_async_copy(res_ref, res_buf, small_sem.at[1]),
        pltpu.make_async_copy(taps_ref, taps_buf, small_sem.at[2]),
        pltpu.make_async_copy(skip_ref, skip_buf, small_sem.at[3]),
        pltpu.make_async_copy(gain_ref, gain_buf, small_sem.at[4]),
    ]
    for copy in small:
        copy.start()
    for step in range(CHUNKS):
        weight_copy(step).start()

    pl.semaphore_wait(barrier, TP - 1 + 2 + FSDP - 1 + CTX - 1)

    piece_rows = ROWS // 4
    core = lax.rem(t, 2)
    sibling = hi * 2 + 1 - core
    home = lax.div(y, 2)

    def piece(ref, at):
        return ref.at[pl.ds(pl.multiple_of(at * piece_rows, piece_rows), piece_rows), :]

    def piece_to(source, at, device, slot):
        return pltpu.make_async_remote_copy(
            src_ref=piece(source, at), dst_ref=piece(rows, at), send_sem=rows_send.at[slot], recv_sem=rows_sem.at[at],
            device_id=device, device_id_type=MESH,
        )

    def arrived(at):
        return pltpu.make_async_copy(piece(rows, at), piece(rows, at), rows_sem.at[at])

    order = (0, 2, 1, 3)
    handed = [piece_to(table_rows(flip), at, (flip, y, (1 - hi) * 2 + at // 2), at) for at in order] + [
        piece_to(table_rows(i), at, (i, y, sibling), 4 + at) for at in order
    ]
    forward = [piece_to(rows, core * 2 + k, (i, y, sibling), k) for k in range(2)]

    @pl.when(t == y)
    def _():
        for copy in handed:
            copy.start()
        for at in range(4):
            pltpu.make_async_copy(piece(table_rows(i), at), piece(rows, at), rows_sem.at[at]).start()

    for device in columns_of:
        pl.semaphore_signal(ready, inc=1, device_id=device, device_id_type=MESH)

    own_copy.wait()
    mine = own[...].astype(F32)
    sums = jnp.sum(mine * mine, axis=1, keepdims=True)
    diagonal = iota((ROWS, 128), 0) == iota((ROWS, 128), 1)
    flat = jnp.sum(jnp.where(diagonal, sums, 0.0), axis=0, keepdims=True)
    squares[t] = jnp.broadcast_to(flat, (8, 128))

    def squares_to(k):
        return pltpu.make_async_remote_copy(
            src_ref=squares.at[t], dst_ref=squares.at[t], send_sem=sq_send.at[k], recv_sem=sq_recv.at[t],
            device_id=(i, y, lax.rem(t + k, TP)), device_id_type=MESH,
        )

    for k in range(1, TP):
        squares_to(k).start()

    for copy in small:
        copy.wait()
    stacked = jnp.concatenate(
        [poles_buf[:, here], res_buf[:, here]]
        + [taps_buf[s, n : n + 1, here] for s in range(3) for n in range(3)]
        + [skip_buf[:, here], jnp.zeros((128 - 2 * POLES - 10, 128), F32)],
        axis=0,
    )
    params[...] = stacked.T

    lag = iota((SUB, STEPS), 1).astype(F32)
    for g in range(SLICE // SUB):
        block = params[pl.ds(pl.multiple_of(y * SLICE + g * SUB, SUB), SUB), :]
        rates = jnp.log(block)
        total = jnp.zeros((SUB, STEPS), F32)
        for n in range(POLES):
            rate = rates[:, n : n + 1]
            lifted = block[:, POLES + n : POLES + n + 1] * jnp.exp(lag * rate)
            total = total + lifted
            at = pl.ds(n * SUB, SUB)
            gmat[g, at, :] = (lifted * block[:, n : n + 1]).astype(BF16)
            vmat[g, at, :] = jnp.exp((STEPS - 1 - lag) * rate).astype(BF16)
        kern[0, pl.ds(g * SUB, SUB), :] = total[:, :128]
        kern[1, pl.ds(g * SUB, SUB), :] = total[:, 128:]

    @pl.when(hi != home)
    def _():
        for k in range(2):
            arrived(core * 2 + k).wait()
            forward[k].start()

    def ids_to(other, device):
        return pltpu.make_async_remote_copy(
            src_ref=ids_ref, dst_ref=all_ids.at[y, pl.ds(i, 1), :], send_sem=ids_send.at[other],
            recv_sem=ids_recv.at[me], device_id=device, device_id_type=MESH,
        )

    pltpu.make_async_copy(ids_ref, all_ids.at[y, pl.ds(i, 1), :], ids_recv.at[me]).start()
    pl.semaphore_wait(ready, CTX - 1)
    for other, device in others:
        ids_to(other, device).start()

    for k in range(1, TP):
        source = lax.rem(t + k, TP)
        pltpu.make_async_copy(squares.at[source], squares.at[source], sq_recv.at[source]).wait()
    total = squares[0] + squares[1] + squares[2] + squares[3]
    scale = lax.rsqrt(total[0:1, :] * (1.0 / (FEAT * FSDP)) + norm_eps)
    scale = jnp.sum(jnp.where(diagonal, scale, 0.0), axis=1, keepdims=True)

    @pl.when(hi == home)
    def _():
        for k in range(2):
            arrived(core * 2 + k).wait()

    for k in range(2):
        arrived((1 - core) * 2 + k).wait()
    gain = gain_buf[:, pl.ds(pl.multiple_of(y * FEAT, FEAT), FEAT)]
    normed = (rows[...].astype(F32) * scale * gain).astype(BF16)

    lane_block = lax.div(iota((48, 128), 1), SLICE)

    def part_to(slot, device):
        return pltpu.make_async_remote_copy(
            src_ref=send_buf.at[slot], dst_ref=parts.at[me], send_sem=part_send.at[slot], recv_sem=part_recv.at[i],
            device_id=device, device_id_type=MESH,
        )

    mine_at = lax.rem(me, 8)

    def receivers(step):
        for dx, dz, dy in OFFSETS:
            if dx == FAR_X[step]:
                oz, oy = lax.rem(lax.rem(i, 2) + dz, 2), lax.rem(y + dy, FSDP)
                yield oz * FSDP + oy, (turn[step] * 2 + oz, oy, t)

    for step in range(CHUNKS):
        weight_copy(step).wait()
        dots = [jnp.dot(normed, weight_buf[step, stream], preferred_element_type=F32) for stream in range(3)]
        for half in range(CHUNK // 128):
            cols = [dot[:, half * 128 : half * 128 + 128] for dot in dots]
            for b in range(4):
                base = [pltpu.roll(c, (32 * (s - b)) % 128, 1) if (s - b) % 4 else c for s, c in enumerate(cols)]
                tail = jnp.concatenate(
                    [pltpu.roll(c[48:64], (32 * (3 - b)) % 128, 1) if (3 - b) % 4 else c[48:64] for c in cols], axis=0
                )
                piece = jnp.where(
                    lane_block == 0,
                    base[0][:48],
                    jnp.where(lane_block == 1, base[1][:48], jnp.where(lane_block == 2, base[2][:48], tail)),
                )
                send_buf[step * 8 + half * 4 + b] = piece.astype(BF16)
        for slot, device in receivers(step):
            part_to(step * 8 + slot, device).start()
        if FAR_X[step] == 0:
            pltpu.make_async_copy(send_buf.at[step * 8 + mine_at], parts.at[me], part_recv.at[i]).start()

    odd = [lax.rem(lax.div(iota((8, 128), 0), 2**bit), 2) == 1 for bit in range(3)]
    above = iota((128, 128), 1) >= iota((128, 128), 0)

    def fill(g, carry):
        block = pl.ds(pl.multiple_of(g * SUB, SUB), SUB)
        lags = [kern[half, block, :] for half in range(2)]
        bases = [[jnp.broadcast_to(x[k : k + 1], (8, 128)) for x in lags] for k in range(SUB)]
        for bit in range(3):
            bases = [[jnp.where(odd[bit], pltpu.roll(x, 2**bit, 1), x) for x in pair] for pair in bases]
        for k in range(SUB):
            shifted = [
                jnp.concatenate([pltpu.roll(x, 8 * m, 1) if m else x for m in range(16)], axis=0) for x in bases[k]
            ]
            kmat[g * SUB + k, :, pl.ds(0, 128)] = jnp.where(above, shifted[0], 0.0).astype(BF16)
            kmat[g * SUB + k, :, pl.ds(128, 128)] = jnp.where(above, shifted[1], shifted[0]).astype(BF16)
        return carry

    vocab_row = iota((VOCAB // 2, STEPS), 0)

    def hot(s, carry):
        for j in range(CTX):
            landed = all_ids.at[s, pl.ds(j, 1), :]
            pltpu.make_async_copy(ids_ref, landed, ids_recv.at[j * FSDP + s]).wait()
            row = all_ids[s, pl.ds(j, 1), :]
            low = jnp.where(row >= VOCAB // 2, row - VOCAB // 2, row)
            onehot[s * CTX + j] = jnp.where(vocab_row == low, 1.0, 0.0).astype(BF16)
        return carry

    lax.fori_loop(0, SLICE // SUB, fill, 0)
    diagonal128 = iota((128, 128), 0) == iota((128, 128), 1)
    for g in range(SLICE // SUB):
        block = params[pl.ds(pl.multiple_of(y * SLICE + g * SUB, SUB), SUB), :]
        decay = jnp.concatenate(
            [jnp.broadcast_to(block[:, n : n + 1], (SUB, 128)) for n in range(POLES)], axis=0
        )
        decay = jnp.sum(jnp.where(diagonal128, decay, 0.0), axis=0, keepdims=True)
        for _ in range(8):
            decay = decay * decay
        decays[g] = jnp.broadcast_to(decay, (8, 128))

    lax.fori_loop(0, FSDP, hot, 0)

    block16 = lax.div(iota((16, 128), 1), SLICE)
    for step in range(CHUNKS):
        pair = lax.rem(lax.div(i, 2) + 4 - FAR_X[step], CHUNKS)
        for z in range(2):
            four = parts.at[pl.ds((pair * 2 + z) * 4, 4)]
            pltpu.make_async_copy(four, four, part_recv.at[pair * 2 + z]).wait()
            a = parts[(pair * 2 + z) * 4].astype(F32)
            for k in range(1, 4):
                a = a + parts[(pair * 2 + z) * 4 + k].astype(F32)
            tail = [pltpu.roll(a[16 * s : 16 * s + 16], SLICE * (s + 1), 1) for s in range(3)]
            whole[pl.ds(z * ROWS, 48), :] = a
            whole[pl.ds(z * ROWS + 48, 16), :] = jnp.where(
                block16 == 0, tail[0], jnp.where(block16 == 1, tail[1], tail[2])
            )
        to = pl.ds(pl.multiple_of(lax.div(pair, 2) * (3 * SLICE), 3 * SLICE), 3 * SLICE)
        cols = pl.ds(pl.multiple_of(lax.rem(pair, 2) * 128, 128), 128)
        table[to, cols] = whole[...].T[: 3 * SLICE].astype(BF16)

    def gather(s, carry):
        for j in range(CTX):
            at = s * CTX + j
            both = jnp.dot(table[...], onehot[at], preferred_element_type=F32)
            upper = all_ids[s, pl.ds(j, 1), :] >= VOCAB // 2
            for half in range(2):
                cols = slice(half * 128, half * 128 + 128)
                raw[half, at] = jnp.where(upper[:, cols], both[3 * SLICE :, cols], both[: 3 * SLICE, cols])
        return carry

    lax.fori_loop(0, FSDP, gather, 0)

    lane = iota((SUB, 128), 1)

    def featurize(g):
        block = params[pl.ds(pl.multiple_of(y * SLICE + g * SUB, SUB), SUB), :]
        taps = [
            [
                jnp.broadcast_to(block[:, 2 * POLES + 3 * s + n : 2 * POLES + 3 * s + n + 1], (SUB, 128))
                for n in range(3)
            ]
            for s in range(3)
        ]
        for at in range(GROUP):
            if at % CTX == 0:
                before = [[jnp.zeros((SUB, 128), F32)] * 2] * 3
            for half in range(2):
                done = []
                for s in range(3):
                    now = raw[half, at, pl.ds(s * SLICE + g * SUB, SUB), :]
                    moved = [pltpu.roll(now, n, 1) for n in (1, 2)]
                    total = taps[s][0] * now
                    for n in (1, 2):
                        total = total + taps[s][n] * jnp.where(lane < n, before[s][n - 1], moved[n - 1])
                    before = before[:s] + [moved] + before[s + 1 :]
                    done.append(total)
                to = pl.ds(at * SUB, SUB)
                query[g][half, to, :] = done[0]
                product[g][half, to, :] = done[1] * done[2]

    channel = lax.rem(iota((GROUP, 128), 1), SUB)
    chunk = lax.rem(iota((GROUP, 128), 0), CTX)

    def convolve(g):
        decay = decays[g, 0:1, :]
        halves = [
            [product[g][half, pl.ds(k, GROUP, stride=SUB), :].astype(BF16) for half in range(2)] for k in range(SUB)
        ]
        inputs = jnp.concatenate([jnp.concatenate(x, axis=1) for x in halves], axis=0)
        states = lax.dot_general(inputs, vmat[g], (((1,), (1,)), ((), ())), preferred_element_type=F32)
        inner = []
        for k in range(SUB):
            both = jnp.dot(jnp.concatenate(halves[k], axis=0), kmat[g * SUB + k], preferred_element_type=F32)
            inner.append([both[:GROUP, :128], both[:GROUP, 128:] + both[GROUP:, :128]])
        stacked = states[:GROUP]
        for k in range(1, SUB):
            stacked = jnp.where(channel == k, states[k * GROUP : (k + 1) * GROUP], stacked)
        states = stacked
        states = jnp.where(chunk < 1, 0.0, pltpu.roll(states, 1, 0))
        for by in (1, 2, 4):
            states = states + decay * jnp.where(chunk < by, 0.0, pltpu.roll(states, by, 0))
            decay = decay * decay
        states = jnp.concatenate([jnp.where(channel == k, states, 0.0) for k in range(SUB)], axis=0)
        carried = jnp.dot(states.astype(BF16), gmat[g], preferred_element_type=F32)
        for k in range(SUB):
            for half in range(2):
                mixed[g][half, pl.ds(k, GROUP, stride=SUB), :] = (
                    inner[k][half] + carried[k * GROUP : (k + 1) * GROUP, half * 128 : half * 128 + 128]
                )

    mine_params = params[pl.ds(pl.multiple_of(y * SLICE, SLICE), SLICE), :]
    skip = jnp.broadcast_to(mine_params[:, 2 * POLES + 9 : 2 * POLES + 10], (SLICE, 128))
    pieces = onehot

    def share(part):
        return pl.ds(part * 2 * SUB, 2 * SUB)

    def out_to(part, other, device):
        return pltpu.make_async_remote_copy(
            src_ref=pieces.at[other, share(part), :], dst_ref=out_ref.at[me, share(part), :],
            send_sem=out_send.at[part, other], recv_sem=out_recv, device_id=device, device_id_type=MESH,
        )

    def gate(part, other):
        s = lax.rem(other, FSDP)
        j = lax.div(other, FSDP)
        at = pl.ds(pl.multiple_of((s * CTX + j) * SUB, SUB), SUB)
        for half in range(2):
            q, u, c = [
                jnp.concatenate([x[2 * part + g][half, at, :] for g in range(2)], axis=0)
                for x in (query, product, mixed)
            ]
            gated = q * (c + skip[part * 2 * SUB : (part + 1) * 2 * SUB] * u)
            pieces[other, share(part), pl.ds(half * 128, 128)] = gated.astype(BF16)

    for part in range(2):
        featurize(2 * part)
        featurize(2 * part + 1)
        convolve(2 * part)
        convolve(2 * part + 1)
        for other, device in others:
            gate(part, other)
            out_to(part, other, device).start()
        gate(part, me)
        pltpu.make_async_copy(pieces.at[me, share(part), :], out_ref.at[me, share(part), :], out_recv).start()

    for k in range(1, TP):
        squares_to(k).wait_send()

    @pl.when(t == y)
    def _():
        for copy in handed:
            copy.wait_send()

    @pl.when(hi != home)
    def _():
        for copy in forward:
            copy.wait_send()

    for step in range(CHUNKS):
        for slot, device in receivers(step):
            part_to(step * 8 + slot, device).wait_send()

    for other, device in others:
        ids_to(other, device).wait_send()
        for part in range(2):
            out_to(part, other, device).wait_send()

    pltpu.make_async_copy(out_ref, out_ref, out_recv).wait()


def block(*args):
    hbm = pl.BlockSpec(memory_space=pltpu.HBM)
    dma = pltpu.SemaphoreType.DMA
    groups = SLICE // SUB
    return pl.pallas_call(
        block_kernel,
        out_shape=jax.ShapeDtypeStruct((GROUP, SLICE, STEPS), BF16),
        in_specs=[hbm] * 8,
        out_specs=hbm,
        scratch_shapes=[
            pltpu.VMEM((CHUNKS, 3, FEAT, CHUNK), BF16),
            pltpu.VMEM((ROWS, FEAT), BF16),
            pltpu.VMEM((ROWS, FEAT), BF16),
            pltpu.VMEM((TP, 8, 128), F32),
            pltpu.VMEM((GROUP, 48, 128), BF16),
            pltpu.VMEM((GROUP, 48, 128), BF16),
            pltpu.VMEM((FSDP, CTX, STEPS), jnp.int32),
            pltpu.VMEM((1, FEAT * FSDP), F32),
            pltpu.VMEM((3, 3, CHAN), F32),
            pltpu.VMEM((POLES, CHAN), F32),
            pltpu.VMEM((POLES, CHAN), F32),
            pltpu.VMEM((1, CHAN), F32),
            pltpu.VMEM((128, 128), F32),
            pltpu.VMEM((groups, 8, 128), F32),
            pltpu.VMEM((2, SLICE, 128), F32),
            pltpu.VMEM((SLICE, STEPS // 2, STEPS), BF16),
            pltpu.VMEM((groups, POLES * SUB, STEPS), BF16),
            pltpu.VMEM((groups, POLES * SUB, STEPS), BF16),
            pltpu.VMEM((GROUP, VOCAB // 2, STEPS), BF16),
            pltpu.VMEM((6 * SLICE, VOCAB // 2), BF16),
            pltpu.VMEM((2 * ROWS, 128), F32),
            pltpu.VMEM((2, GROUP, 3 * SLICE, 128), F32),
            [pltpu.VMEM((2, GROUP * SUB, 128), F32) for _ in range(groups)],
            [pltpu.VMEM((2, GROUP * SUB, 128), F32) for _ in range(groups)],
            [pltpu.VMEM((2, GROUP * SUB, 128), F32) for _ in range(groups)],
            dma((CHUNKS,)),
            dma,
            dma((5,)),
            dma((4,)),
            dma((8,)),
            dma((TP,)),
            dma((TP,)),
            dma((GROUP,)),
            dma((GROUP,)),
            dma((GROUP,)),
            dma((CTX,)),
            dma((2, GROUP)),
            dma,
            pltpu.SemaphoreType.REGULAR,
        ],
        compiler_params=pltpu.CompilerParams(
            collective_id=0, has_side_effects=True, vmem_limit_bytes=56 * 2**20
        ),
        name="hyena_block",
    )(*args)


def shards(
    base_ids, embed_table, norm_gain, in_weight, conv_taps, modal_poles, residues, skip_gain
):
    landed = block(
        base_ids, embed_table, norm_gain.reshape(1, -1), jnp.transpose(in_weight, (1, 0, 2)),
        conv_taps, modal_poles, residues, skip_gain.reshape(1, -1),
    )
    return landed.reshape(CHAN, STEPS).T[None]


def solution(mesh):
    in_specs = (
        P("fsdp", "ctx"),
        P(None, "tp"),
        P(),
        P("fsdp", None, "tp"),
        P(None, None, "tp"),
        P(None, "tp"),
        P(None, "tp"),
        P("tp"),
    )
    out_specs = P("fsdp", "ctx", "tp")
    return jax.shard_map(shards, mesh=mesh, in_specs=in_specs, out_specs=out_specs, check_vma=False)
```

```python
import jax
import jax.numpy as jnp
from jax import lax
from jax.experimental import pallas as pl
from jax.experimental.pallas import tpu as pltpu
from jax.sharding import PartitionSpec as P

MESH = pl.DeviceIdType.MESH
F32 = jnp.float32
BF16 = jnp.bfloat16
norm_eps = 1e-06

CTX, FSDP, TP = 8, 4, 4
GROUP = CTX * FSDP
VOCAB = 512
ROWS = VOCAB // CTX
FEAT = 2048
CHAN = 1024
SLICE = CHAN // GROUP
STEPS = 256
POLES = 16
CHUNK = 256
CHUNKS = CHAN // CHUNK
SUB = 8


def iota(shape, dim):
    return lax.broadcasted_iota(jnp.int32, shape, dim)


OFFSETS = sorted(
    [(x, z, y) for x in range(4) for z in range(2) for y in range(4) if (x, z, y) != (0, 0, 0)],
    key=lambda o: -(min(o[0], 4 - o[0]) + o[1] + min(o[2], 4 - o[2])),
)


FAR_X = (2, 1, 3, 0)


def block_kernel(
    ids_ref, table_ref, gain_ref, weight_ref, taps_ref, poles_ref, res_ref, skip_ref, out_ref,
    weight_buf, own, rows, squares, send_buf, parts, all_ids, gain_buf, taps_buf, poles_buf, res_buf, skip_buf,
    params, decays, kern, kmat, vmat, gmat, onehot, table, whole, raw, product, query, mixed,
    weight_sem, own_sem, small_sem, rows_sem, rows_send, sq_send, sq_recv, ids_send, ids_recv, part_send, part_recv,
    out_send, out_recv, ready,
):
    i = lax.axis_index("ctx")
    y = lax.axis_index("fsdp")
    t = lax.axis_index("tp")
    me = i * FSDP + y
    hi = lax.div(t, 2)
    flip = i + 1 - 2 * lax.rem(i, 2)
    turn = [lax.rem(lax.div(i, 2) + x, CHUNKS) for x in FAR_X]
    here = pl.ds(pl.multiple_of(i * 128, 128), 128)

    others = []
    for dx, dz, dy in OFFSETS:
        oi = lax.rem(lax.div(i, 2) + dx, 4) * 2 + lax.rem(lax.rem(i, 2) + dz, 2)
        oy = lax.rem(y + dy, FSDP)
        others.append((oi * FSDP + oy, (oi, oy, t)))

    barrier = pltpu.get_barrier_semaphore()

    def greet(device):
        pl.semaphore_signal(barrier, inc=1, device_id=device, device_id_type=MESH)

    for k in range(1, TP):
        greet((i, y, lax.rem(t + k, TP)))
    for core in range(2):
        greet((flip, y, (1 - hi) * 2 + core))
    for k in range(1, FSDP):
        greet((i, lax.rem(y + k, FSDP), t))
    columns_of = [(lax.rem(i + k, CTX), y, t) for k in range(1, CTX)]
    for device in columns_of:
        greet(device)

    def table_rows(block):
        return table_ref.at[pl.ds(pl.multiple_of(block * ROWS, ROWS), ROWS), :]

    def columns(step):
        return pl.ds(pl.multiple_of(turn[step] * CHUNK, CHUNK), CHUNK)

    def weight_copy(step):
        return pltpu.make_async_copy(weight_ref.at[:, :, columns(step)], weight_buf.at[step], weight_sem.at[step])

    own_copy = pltpu.make_async_copy(table_rows(i), own, own_sem)
    own_copy.start()
    small = [
        pltpu.make_async_copy(poles_ref, poles_buf, small_sem.at[0]),
        pltpu.make_async_copy(res_ref, res_buf, small_sem.at[1]),
        pltpu.make_async_copy(taps_ref, taps_buf, small_sem.at[2]),
        pltpu.make_async_copy(skip_ref, skip_buf, small_sem.at[3]),
        pltpu.make_async_copy(gain_ref, gain_buf, small_sem.at[4]),
    ]
    for copy in small:
        copy.start()
    for step in range(CHUNKS):
        weight_copy(step).start()

    pl.semaphore_wait(barrier, TP - 1 + 2 + FSDP - 1 + CTX - 1)

    piece_rows = ROWS // 4
    core = lax.rem(t, 2)
    sibling = hi * 2 + 1 - core
    home = lax.div(y, 2)

    def piece(ref, at):
        return ref.at[pl.ds(pl.multiple_of(at * piece_rows, piece_rows), piece_rows), :]

    def piece_to(source, at, device, slot):
        return pltpu.make_async_remote_copy(
            src_ref=piece(source, at), dst_ref=piece(rows, at), send_sem=rows_send.at[slot], recv_sem=rows_sem.at[at],
            device_id=device, device_id_type=MESH,
        )

    def arrived(at):
        return pltpu.make_async_copy(piece(rows, at), piece(rows, at), rows_sem.at[at])

    order = (0, 2, 1, 3)
    handed = [piece_to(table_rows(flip), at, (flip, y, (1 - hi) * 2 + at // 2), at) for at in order] + [
        piece_to(table_rows(i), at, (i, y, sibling), 4 + at) for at in order
    ]
    forward = [piece_to(rows, core * 2 + k, (i, y, sibling), k) for k in range(2)]

    @pl.when(t == y)
    def _():
        for copy in handed:
            copy.start()
        for at in range(4):
            pltpu.make_async_copy(piece(table_rows(i), at), piece(rows, at), rows_sem.at[at]).start()

    for device in columns_of:
        pl.semaphore_signal(ready, inc=1, device_id=device, device_id_type=MESH)

    own_copy.wait()
    mine = own[...].astype(F32)
    sums = jnp.sum(mine * mine, axis=1, keepdims=True)
    diagonal = iota((ROWS, 128), 0) == iota((ROWS, 128), 1)
    flat = jnp.sum(jnp.where(diagonal, sums, 0.0), axis=0, keepdims=True)
    squares[t] = jnp.broadcast_to(flat, (8, 128))

    def squares_to(k):
        return pltpu.make_async_remote_copy(
            src_ref=squares.at[t], dst_ref=squares.at[t], send_sem=sq_send.at[k], recv_sem=sq_recv.at[t],
            device_id=(i, y, lax.rem(t + k, TP)), device_id_type=MESH,
        )

    for k in range(1, TP):
        squares_to(k).start()

    for copy in small:
        copy.wait()
    stacked = jnp.concatenate(
        [poles_buf[:, here], res_buf[:, here]]
        + [taps_buf[s, n : n + 1, here] for s in range(3) for n in range(3)]
        + [skip_buf[:, here], jnp.zeros((128 - 2 * POLES - 10, 128), F32)],
        axis=0,
    )
    params[...] = stacked.T

    lag = iota((SUB, STEPS), 1).astype(F32)
    for g in range(SLICE // SUB):
        block = params[pl.ds(pl.multiple_of(y * SLICE + g * SUB, SUB), SUB), :]
        rates = jnp.log(block)
        total = jnp.zeros((SUB, STEPS), F32)
        for n in range(POLES):
            rate = rates[:, n : n + 1]
            lifted = block[:, POLES + n : POLES + n + 1] * jnp.exp(lag * rate)
            total = total + lifted
            at = pl.ds(n * SUB, SUB)
            gmat[g, at, :] = (lifted * block[:, n : n + 1]).astype(BF16)
            vmat[g, at, :] = jnp.exp((STEPS - 1 - lag) * rate).astype(BF16)
        kern[0, pl.ds(g * SUB, SUB), :] = total[:, :128]
        kern[1, pl.ds(g * SUB, SUB), :] = total[:, 128:]

    @pl.when(hi != home)
    def _():
        for k in range(2):
            arrived(core * 2 + k).wait()
            forward[k].start()

    def ids_to(other, device):
        return pltpu.make_async_remote_copy(
            src_ref=ids_ref, dst_ref=all_ids.at[y, pl.ds(i, 1), :], send_sem=ids_send.at[other],
            recv_sem=ids_recv.at[me], device_id=device, device_id_type=MESH,
        )

    pltpu.make_async_copy(ids_ref, all_ids.at[y, pl.ds(i, 1), :], ids_recv.at[me]).start()
    pl.semaphore_wait(ready, CTX - 1)
    for other, device in others:
        ids_to(other, device).start()

    for k in range(1, TP):
        source = lax.rem(t + k, TP)
        pltpu.make_async_copy(squares.at[source], squares.at[source], sq_recv.at[source]).wait()
    total = squares[0] + squares[1] + squares[2] + squares[3]
    scale = lax.rsqrt(total[0:1, :] * (1.0 / (FEAT * FSDP)) + norm_eps)
    scale = jnp.sum(jnp.where(diagonal, scale, 0.0), axis=1, keepdims=True)

    @pl.when(hi == home)
    def _():
        for k in range(2):
            arrived(core * 2 + k).wait()

    for k in range(2):
        arrived((1 - core) * 2 + k).wait()
    gain = gain_buf[:, pl.ds(pl.multiple_of(y * FEAT, FEAT), FEAT)]
    normed = (rows[...].astype(F32) * scale * gain).astype(BF16)

    lane_block = lax.div(iota((48, 128), 1), SLICE)

    def part_to(slot, device):
        return pltpu.make_async_remote_copy(
            src_ref=send_buf.at[slot], dst_ref=parts.at[me], send_sem=part_send, recv_sem=part_recv.at[i],
            device_id=device, device_id_type=MESH,
        )

    mine_at = lax.rem(me, 8)

    def receivers(step):
        for dx, dz, dy in OFFSETS:
            if dx == FAR_X[step]:
                oz, oy = lax.rem(lax.rem(i, 2) + dz, 2), lax.rem(y + dy, FSDP)
                yield oz * FSDP + oy, (turn[step] * 2 + oz, oy, t)

    for step in range(CHUNKS):
        weight_copy(step).wait()
        dots = [jnp.dot(normed, weight_buf[step, stream], preferred_element_type=F32) for stream in range(3)]
        for half in range(CHUNK // 128):
            cols = [dot[:, half * 128 : half * 128 + 128] for dot in dots]
            for b in range(4):
                base = [pltpu.roll(c, (32 * (s - b)) % 128, 1) if (s - b) % 4 else c for s, c in enumerate(cols)]
                tail = jnp.concatenate(
                    [pltpu.roll(c[48:64], (32 * (3 - b)) % 128, 1) if (3 - b) % 4 else c[48:64] for c in cols], axis=0
                )
                piece = jnp.where(
                    lane_block == 0,
                    base[0][:48],
                    jnp.where(lane_block == 1, base[1][:48], jnp.where(lane_block == 2, base[2][:48], tail)),
                )
                send_buf[step * 8 + half * 4 + b] = piece.astype(BF16)
        for slot, device in receivers(step):
            part_to(step * 8 + slot, device).start()
        if FAR_X[step] == 0:
            pltpu.make_async_copy(send_buf.at[step * 8 + mine_at], parts.at[me], part_recv.at[i]).start()

    odd = [lax.rem(lax.div(iota((8, 128), 0), 2**bit), 2) == 1 for bit in range(3)]
    above = iota((128, 128), 1) >= iota((128, 128), 0)

    def fill(g, carry):
        block = pl.ds(pl.multiple_of(g * SUB, SUB), SUB)
        lags = [kern[half, block, :] for half in range(2)]
        bases = [[jnp.broadcast_to(x[k : k + 1], (8, 128)) for x in lags] for k in range(SUB)]
        for bit in range(3):
            bases = [[jnp.where(odd[bit], pltpu.roll(x, 2**bit, 1), x) for x in pair] for pair in bases]
        for k in range(SUB):
            shifted = [
                jnp.concatenate([pltpu.roll(x, 8 * m, 1) if m else x for m in range(16)], axis=0) for x in bases[k]
            ]
            kmat[g * SUB + k, :, pl.ds(0, 128)] = jnp.where(above, shifted[0], 0.0).astype(BF16)
            kmat[g * SUB + k, :, pl.ds(128, 128)] = jnp.where(above, shifted[1], shifted[0]).astype(BF16)
        return carry

    vocab_row = iota((VOCAB // 2, STEPS), 0)

    def hot(s, carry):
        for j in range(CTX):
            landed = all_ids.at[s, pl.ds(j, 1), :]
            pltpu.make_async_copy(ids_ref, landed, ids_recv.at[j * FSDP + s]).wait()
            row = all_ids[s, pl.ds(j, 1), :]
            low = jnp.where(row >= VOCAB // 2, row - VOCAB // 2, row)
            onehot[s * CTX + j] = jnp.where(vocab_row == low, 1.0, 0.0).astype(BF16)
        return carry

    lax.fori_loop(0, SLICE // SUB, fill, 0)
    diagonal128 = iota((128, 128), 0) == iota((128, 128), 1)
    for g in range(SLICE // SUB):
        block = params[pl.ds(pl.multiple_of(y * SLICE + g * SUB, SUB), SUB), :]
        decay = jnp.concatenate(
            [jnp.broadcast_to(block[:, n : n + 1], (SUB, 128)) for n in range(POLES)], axis=0
        )
        decay = jnp.sum(jnp.where(diagonal128, decay, 0.0), axis=0, keepdims=True)
        for _ in range(8):
            decay = decay * decay
        decays[g] = jnp.broadcast_to(decay, (8, 128))

    lax.fori_loop(0, FSDP, hot, 0)

    for k in range(1, TP):
        squares_to(k).wait_send()

    @pl.when(t == y)
    def _():
        for copy in handed:
            copy.wait_send()

    @pl.when(hi != home)
    def _():
        for copy in forward:
            copy.wait_send()

    for other, device in others:
        ids_to(other, device).wait_send()

    block16 = lax.div(iota((16, 128), 1), SLICE)
    for step in range(CHUNKS):
        pair = lax.rem(lax.div(i, 2) + 4 - FAR_X[step], CHUNKS)
        for z in range(2):
            four = parts.at[pl.ds((pair * 2 + z) * 4, 4)]
            pltpu.make_async_copy(four, four, part_recv.at[pair * 2 + z]).wait()
            a = parts[(pair * 2 + z) * 4].astype(F32)
            for k in range(1, 4):
                a = a + parts[(pair * 2 + z) * 4 + k].astype(F32)
            tail = [pltpu.roll(a[16 * s : 16 * s + 16], SLICE * (s + 1), 1) for s in range(3)]
            whole[pl.ds(z * ROWS, 48), :] = a
            whole[pl.ds(z * ROWS + 48, 16), :] = jnp.where(
                block16 == 0, tail[0], jnp.where(block16 == 1, tail[1], tail[2])
            )
        to = pl.ds(pl.multiple_of(lax.div(pair, 2) * (3 * SLICE), 3 * SLICE), 3 * SLICE)
        cols = pl.ds(pl.multiple_of(lax.rem(pair, 2) * 128, 128), 128)
        table[to, cols] = whole[...].T[: 3 * SLICE].astype(BF16)

    def gather(s, carry):
        for j in range(CTX):
            at = s * CTX + j
            both = jnp.dot(table[...], onehot[at], preferred_element_type=F32)
            upper = all_ids[s, pl.ds(j, 1), :] >= VOCAB // 2
            for half in range(2):
                cols = slice(half * 128, half * 128 + 128)
                raw[half, at] = jnp.where(upper[:, cols], both[3 * SLICE :, cols], both[: 3 * SLICE, cols])
        return carry

    lax.fori_loop(0, FSDP, gather, 0)

    lane = iota((SUB, 128), 1)

    def featurize(g):
        block = params[pl.ds(pl.multiple_of(y * SLICE + g * SUB, SUB), SUB), :]
        taps = [
            [
                jnp.broadcast_to(block[:, 2 * POLES + 3 * s + n : 2 * POLES + 3 * s + n + 1], (SUB, 128))
                for n in range(3)
            ]
            for s in range(3)
        ]
        for at in range(GROUP):
            if at % CTX == 0:
                before = [[jnp.zeros((SUB, 128), F32)] * 2] * 3
            for half in range(2):
                done = []
                for s in range(3):
                    now = raw[half, at, pl.ds(s * SLICE + g * SUB, SUB), :]
                    moved = [pltpu.roll(now, n, 1) for n in (1, 2)]
                    total = taps[s][0] * now
                    for n in (1, 2):
                        total = total + taps[s][n] * jnp.where(lane < n, before[s][n - 1], moved[n - 1])
                    before = before[:s] + [moved] + before[s + 1 :]
                    done.append(total)
                to = pl.ds(at * SUB, SUB)
                query[g][half, to, :] = done[0]
                product[g][half, to, :] = done[1] * done[2]

    channel = lax.rem(iota((GROUP, 128), 1), SUB)
    chunk = lax.rem(iota((GROUP, 128), 0), CTX)

    def convolve(g):
        decay = decays[g, 0:1, :]
        halves = [
            [product[g][half, pl.ds(k, GROUP, stride=SUB), :].astype(BF16) for half in range(2)] for k in range(SUB)
        ]
        inputs = jnp.concatenate([jnp.concatenate(x, axis=1) for x in halves], axis=0)
        states = lax.dot_general(inputs, vmat[g], (((1,), (1,)), ((), ())), preferred_element_type=F32)
        inner = []
        for k in range(SUB):
            both = jnp.dot(jnp.concatenate(halves[k], axis=0), kmat[g * SUB + k], preferred_element_type=F32)
            inner.append([both[:GROUP, :128], both[:GROUP, 128:] + both[GROUP:, :128]])
        stacked = states[:GROUP]
        for k in range(1, SUB):
            stacked = jnp.where(channel == k, states[k * GROUP : (k + 1) * GROUP], stacked)
        states = stacked
        states = jnp.where(chunk < 1, 0.0, pltpu.roll(states, 1, 0))
        for by in (1, 2, 4):
            states = states + decay * jnp.where(chunk < by, 0.0, pltpu.roll(states, by, 0))
            decay = decay * decay
        states = jnp.concatenate([jnp.where(channel == k, states, 0.0) for k in range(SUB)], axis=0)
        carried = jnp.dot(states.astype(BF16), gmat[g], preferred_element_type=F32)
        for k in range(SUB):
            for half in range(2):
                mixed[g][half, pl.ds(k, GROUP, stride=SUB), :] = (
                    inner[k][half] + carried[k * GROUP : (k + 1) * GROUP, half * 128 : half * 128 + 128]
                )

    mine_params = params[pl.ds(pl.multiple_of(y * SLICE, SLICE), SLICE), :]
    skip = jnp.broadcast_to(mine_params[:, 2 * POLES + 9 : 2 * POLES + 10], (SLICE, 128))
    pieces = onehot

    def share(part):
        return pl.ds(part * 2 * SUB, 2 * SUB)

    def out_to(part, other, device):
        return pltpu.make_async_remote_copy(
            src_ref=pieces.at[other, share(part), :], dst_ref=out_ref.at[me, share(part), :],
            send_sem=out_send.at[part], recv_sem=out_recv, device_id=device, device_id_type=MESH,
        )

    def gate(part, other):
        s = lax.rem(other, FSDP)
        j = lax.div(other, FSDP)
        at = pl.ds(pl.multiple_of((s * CTX + j) * SUB, SUB), SUB)
        for half in range(2):
            q, u, c = [
                jnp.concatenate([x[2 * part + g][half, at, :] for g in range(2)], axis=0)
                for x in (query, product, mixed)
            ]
            gated = q * (c + skip[part * 2 * SUB : (part + 1) * 2 * SUB] * u)
            pieces[other, share(part), pl.ds(half * 128, 128)] = gated.astype(BF16)

    for part in range(2):
        featurize(2 * part)
        featurize(2 * part + 1)
        convolve(2 * part)
        convolve(2 * part + 1)
        for other, device in others:
            gate(part, other)
            out_to(part, other, device).start()
        gate(part, me)
        pltpu.make_async_copy(pieces.at[me, share(part), :], out_ref.at[me, share(part), :], out_recv).start()

    sent = send_buf.at[pl.ds(0, GROUP - 1)]
    pltpu.make_async_copy(sent, sent, part_send).wait()
    for part in range(2):
        sent = pieces.at[pl.ds(0, GROUP - 1), share(part), :]
        pltpu.make_async_copy(sent, sent, out_send.at[part]).wait()
    pltpu.make_async_copy(out_ref, out_ref, out_recv).wait()


def block(*args):
    hbm = pl.BlockSpec(memory_space=pltpu.HBM)
    dma = pltpu.SemaphoreType.DMA
    groups = SLICE // SUB
    return pl.pallas_call(
        block_kernel,
        out_shape=jax.ShapeDtypeStruct((GROUP, SLICE, STEPS), BF16),
        in_specs=[hbm] * 8,
        out_specs=hbm,
        scratch_shapes=[
            pltpu.VMEM((CHUNKS, 3, FEAT, CHUNK), BF16),
            pltpu.VMEM((ROWS, FEAT), BF16),
            pltpu.VMEM((ROWS, FEAT), BF16),
            pltpu.VMEM((TP, 8, 128), F32),
            pltpu.VMEM((GROUP, 48, 128), BF16),
            pltpu.VMEM((GROUP, 48, 128), BF16),
            pltpu.VMEM((FSDP, CTX, STEPS), jnp.int32),
            pltpu.VMEM((1, FEAT * FSDP), F32),
            pltpu.VMEM((3, 3, CHAN), F32),
            pltpu.VMEM((POLES, CHAN), F32),
            pltpu.VMEM((POLES, CHAN), F32),
            pltpu.VMEM((1, CHAN), F32),
            pltpu.VMEM((128, 128), F32),
            pltpu.VMEM((groups, 8, 128), F32),
            pltpu.VMEM((2, SLICE, 128), F32),
            pltpu.VMEM((SLICE, STEPS // 2, STEPS), BF16),
            pltpu.VMEM((groups, POLES * SUB, STEPS), BF16),
            pltpu.VMEM((groups, POLES * SUB, STEPS), BF16),
            pltpu.VMEM((GROUP, VOCAB // 2, STEPS), BF16),
            pltpu.VMEM((6 * SLICE, VOCAB // 2), BF16),
            pltpu.VMEM((2 * ROWS, 128), F32),
            pltpu.VMEM((2, GROUP, 3 * SLICE, 128), F32),
            [pltpu.VMEM((2, GROUP * SUB, 128), F32) for _ in range(groups)],
            [pltpu.VMEM((2, GROUP * SUB, 128), F32) for _ in range(groups)],
            [pltpu.VMEM((2, GROUP * SUB, 128), F32) for _ in range(groups)],
            dma((CHUNKS,)),
            dma,
            dma((5,)),
            dma((4,)),
            dma((8,)),
            dma((TP,)),
            dma((TP,)),
            dma((GROUP,)),
            dma((GROUP,)),
            dma,
            dma((CTX,)),
            dma((2,)),
            dma,
            pltpu.SemaphoreType.REGULAR,
        ],
        compiler_params=pltpu.CompilerParams(
            collective_id=0, has_side_effects=True, vmem_limit_bytes=56 * 2**20
        ),
        name="hyena_block",
    )(*args)


def shards(
    base_ids, embed_table, norm_gain, in_weight, conv_taps, modal_poles, residues, skip_gain
):
    landed = block(
        base_ids, embed_table, norm_gain.reshape(1, -1), jnp.transpose(in_weight, (1, 0, 2)),
        conv_taps, modal_poles, residues, skip_gain.reshape(1, -1),
    )
    return landed.reshape(CHAN, STEPS).T[None]


def solution(mesh):
    in_specs = (
        P("fsdp", "ctx"),
        P(None, "tp"),
        P(),
        P("fsdp", None, "tp"),
        P(None, None, "tp"),
        P(None, "tp"),
        P(None, "tp"),
        P("tp"),
    )
    out_specs = P("fsdp", "ctx", "tp")
    return jax.shard_map(shards, mesh=mesh, in_specs=in_specs, out_specs=out_specs, check_vma=False)
```

```python
import jax
import jax.numpy as jnp
from jax import lax
from jax.experimental import pallas as pl
from jax.experimental.pallas import tpu as pltpu
from jax.sharding import PartitionSpec as P

MESH = pl.DeviceIdType.MESH
F32 = jnp.float32
BF16 = jnp.bfloat16
norm_eps = 1e-06

CTX, FSDP, TP = 8, 4, 4
GROUP = CTX * FSDP
VOCAB = 512
ROWS = VOCAB // CTX
FEAT = 2048
CHAN = 1024
SLICE = CHAN // GROUP
STEPS = 256
POLES = 16
CHUNK = 256
CHUNKS = CHAN // CHUNK
SUB = 8


def iota(shape, dim):
    return lax.broadcasted_iota(jnp.int32, shape, dim)


OFFSETS = sorted(
    [(x, z, y) for x in range(4) for z in range(2) for y in range(4) if (x, z, y) != (0, 0, 0)],
    key=lambda o: -(min(o[0], 4 - o[0]) + o[1] + min(o[2], 4 - o[2])),
)


BATCH = 8
FAR_X = (2, 1, 3, 0)


def block_kernel(
    ids_ref, table_ref, gain_ref, weight_ref, taps_ref, poles_ref, res_ref, skip_ref, out_ref,
    weight_buf, own, rows, squares, send_buf, parts, all_ids, gain_buf, taps_buf, poles_buf, res_buf, skip_buf,
    params, decays, kern, kmat, vmat, gmat, onehot, table, whole, raw, product, query, mixed,
    weight_sem, own_sem, small_sem, rows_sem, rows_send, sq_send, sq_recv, ids_send, ids_recv, part_send, part_recv,
    out_send, out_recv, ready,
):
    i = lax.axis_index("ctx")
    y = lax.axis_index("fsdp")
    t = lax.axis_index("tp")
    me = i * FSDP + y
    hi = lax.div(t, 2)
    flip = i + 1 - 2 * lax.rem(i, 2)
    turn = [lax.rem(lax.div(i, 2) + x, CHUNKS) for x in FAR_X]
    here = pl.ds(pl.multiple_of(i * 128, 128), 128)

    others = []
    for dx, dz, dy in OFFSETS:
        oi = lax.rem(lax.div(i, 2) + dx, 4) * 2 + lax.rem(lax.rem(i, 2) + dz, 2)
        oy = lax.rem(y + dy, FSDP)
        others.append((oi * FSDP + oy, (oi, oy, t)))

    barrier = pltpu.get_barrier_semaphore()

    def greet(device):
        pl.semaphore_signal(barrier, inc=1, device_id=device, device_id_type=MESH)

    for k in range(1, TP):
        greet((i, y, lax.rem(t + k, TP)))
    for core in range(2):
        greet((flip, y, (1 - hi) * 2 + core))
    for k in range(1, FSDP):
        greet((i, lax.rem(y + k, FSDP), t))
    columns_of = [(lax.rem(i + k, CTX), y, t) for k in range(1, CTX)]
    for device in columns_of:
        greet(device)

    def table_rows(block):
        return table_ref.at[pl.ds(pl.multiple_of(block * ROWS, ROWS), ROWS), :]

    def columns(step):
        return pl.ds(pl.multiple_of(turn[step] * CHUNK, CHUNK), CHUNK)

    def weight_copy(step):
        return pltpu.make_async_copy(weight_ref.at[:, :, columns(step)], weight_buf.at[step], weight_sem.at[step])

    own_copy = pltpu.make_async_copy(table_rows(i), own, own_sem)
    own_copy.start()
    small = [
        pltpu.make_async_copy(poles_ref, poles_buf, small_sem.at[0]),
        pltpu.make_async_copy(res_ref, res_buf, small_sem.at[1]),
        pltpu.make_async_copy(taps_ref, taps_buf, small_sem.at[2]),
        pltpu.make_async_copy(skip_ref, skip_buf, small_sem.at[3]),
        pltpu.make_async_copy(gain_ref, gain_buf, small_sem.at[4]),
    ]
    for copy in small:
        copy.start()
    for step in range(CHUNKS):
        weight_copy(step).start()

    pl.semaphore_wait(barrier, TP - 1 + 2 + FSDP - 1 + CTX - 1)

    piece_rows = ROWS // 4
    core = lax.rem(t, 2)
    sibling = hi * 2 + 1 - core
    home = lax.div(y, 2)

    def piece(ref, at):
        return ref.at[pl.ds(pl.multiple_of(at * piece_rows, piece_rows), piece_rows), :]

    def piece_to(source, at, device, slot):
        return pltpu.make_async_remote_copy(
            src_ref=piece(source, at), dst_ref=piece(rows, at), send_sem=rows_send.at[slot], recv_sem=rows_sem.at[at],
            device_id=device, device_id_type=MESH,
        )

    def arrived(at):
        return pltpu.make_async_copy(piece(rows, at), piece(rows, at), rows_sem.at[at])

    order = (0, 2, 1, 3)
    handed = [piece_to(table_rows(flip), at, (flip, y, (1 - hi) * 2 + at // 2), at) for at in order] + [
        piece_to(table_rows(i), at, (i, y, sibling), 4 + at) for at in order
    ]
    forward = [piece_to(rows, core * 2 + k, (i, y, sibling), k) for k in range(2)]

    @pl.when(t == y)
    def _():
        for copy in handed:
            copy.start()
        for at in range(4):
            pltpu.make_async_copy(piece(table_rows(i), at), piece(rows, at), rows_sem.at[at]).start()

    for device in columns_of:
        pl.semaphore_signal(ready, inc=1, device_id=device, device_id_type=MESH)

    own_copy.wait()
    mine = own[...].astype(F32)
    sums = jnp.sum(mine * mine, axis=1, keepdims=True)
    diagonal = iota((ROWS, 128), 0) == iota((ROWS, 128), 1)
    flat = jnp.sum(jnp.where(diagonal, sums, 0.0), axis=0, keepdims=True)
    squares[t] = jnp.broadcast_to(flat, (8, 128))

    def squares_to(k):
        return pltpu.make_async_remote_copy(
            src_ref=squares.at[t], dst_ref=squares.at[t], send_sem=sq_send.at[k], recv_sem=sq_recv.at[t],
            device_id=(i, y, lax.rem(t + k, TP)), device_id_type=MESH,
        )

    for k in range(1, TP):
        squares_to(k).start()

    for copy in small:
        copy.wait()
    stacked = jnp.concatenate(
        [poles_buf[:, here], res_buf[:, here]]
        + [taps_buf[s, n : n + 1, here] for s in range(3) for n in range(3)]
        + [skip_buf[:, here], jnp.zeros((128 - 2 * POLES - 10, 128), F32)],
        axis=0,
    )
    params[...] = stacked.T

    lag = iota((SUB, STEPS), 1).astype(F32)
    for g in range(SLICE // SUB):
        block = params[pl.ds(pl.multiple_of(y * SLICE + g * SUB, SUB), SUB), :]
        rates = jnp.log(block)
        total = jnp.zeros((SUB, STEPS), F32)
        for n in range(POLES):
            rate = rates[:, n : n + 1]
            lifted = block[:, POLES + n : POLES + n + 1] * jnp.exp(lag * rate)
            total = total + lifted
            at = pl.ds(n * SUB, SUB)
            gmat[g, at, :] = (lifted * block[:, n : n + 1]).astype(BF16)
            vmat[g, at, :] = jnp.exp((STEPS - 1 - lag) * rate).astype(BF16)
        kern[0, pl.ds(g * SUB, SUB), :] = total[:, :128]
        kern[1, pl.ds(g * SUB, SUB), :] = total[:, 128:]

    @pl.when(hi != home)
    def _():
        for k in range(2):
            arrived(core * 2 + k).wait()
            forward[k].start()

    def ids_to(other, device):
        return pltpu.make_async_remote_copy(
            src_ref=ids_ref, dst_ref=all_ids.at[y, pl.ds(i, 1), :], send_sem=ids_send.at[other],
            recv_sem=ids_recv.at[me], device_id=device, device_id_type=MESH,
        )

    pltpu.make_async_copy(ids_ref, all_ids.at[y, pl.ds(i, 1), :], ids_recv.at[me]).start()
    pl.semaphore_wait(ready, CTX - 1)
    for other, device in others:
        ids_to(other, device).start()

    for k in range(1, TP):
        source = lax.rem(t + k, TP)
        pltpu.make_async_copy(squares.at[source], squares.at[source], sq_recv.at[source]).wait()
    total = squares[0] + squares[1] + squares[2] + squares[3]
    scale = lax.rsqrt(total[0:1, :] * (1.0 / (FEAT * FSDP)) + norm_eps)
    scale = jnp.sum(jnp.where(diagonal, scale, 0.0), axis=1, keepdims=True)

    @pl.when(hi == home)
    def _():
        for k in range(2):
            arrived(core * 2 + k).wait()

    for k in range(2):
        arrived((1 - core) * 2 + k).wait()
    gain = gain_buf[:, pl.ds(pl.multiple_of(y * FEAT, FEAT), FEAT)]
    normed = (rows[...].astype(F32) * scale * gain).astype(BF16)

    lane_block = lax.div(iota((48, 128), 1), SLICE)

    def part_to(slot, device):
        return pltpu.make_async_remote_copy(
            src_ref=send_buf.at[slot], dst_ref=parts.at[me], send_sem=part_send, recv_sem=part_recv.at[i],
            device_id=device, device_id_type=MESH,
        )

    mine_at = lax.rem(me, 8)

    def receivers(step):
        for dx, dz, dy in OFFSETS:
            if dx == FAR_X[step]:
                oz, oy = lax.rem(lax.rem(i, 2) + dz, 2), lax.rem(y + dy, FSDP)
                yield oz * FSDP + oy, (turn[step] * 2 + oz, oy, t)

    for step in range(CHUNKS):
        weight_copy(step).wait()
        dots = [jnp.dot(normed, weight_buf[step, stream], preferred_element_type=F32) for stream in range(3)]
        for half in range(CHUNK // 128):
            cols = [dot[:, half * 128 : half * 128 + 128] for dot in dots]
            for b in range(4):
                base = [pltpu.roll(c, (32 * (s - b)) % 128, 1) if (s - b) % 4 else c for s, c in enumerate(cols)]
                tail = jnp.concatenate(
                    [pltpu.roll(c[48:64], (32 * (3 - b)) % 128, 1) if (3 - b) % 4 else c[48:64] for c in cols], axis=0
                )
                piece = jnp.where(
                    lane_block == 0,
                    base[0][:48],
                    jnp.where(lane_block == 1, base[1][:48], jnp.where(lane_block == 2, base[2][:48], tail)),
                )
                send_buf[step * 8 + half * 4 + b] = piece.astype(BF16)
        for slot, device in receivers(step):
            part_to(step * 8 + slot, device).start()
        if FAR_X[step] == 0:
            pltpu.make_async_copy(send_buf.at[step * 8 + mine_at], parts.at[me], part_recv.at[i]).start()

    odd = [lax.rem(lax.div(iota((8, 128), 0), 2**bit), 2) == 1 for bit in range(3)]
    above = iota((128, 128), 1) >= iota((128, 128), 0)

    def fill(g, carry):
        block = pl.ds(pl.multiple_of(g * SUB, SUB), SUB)
        lags = [kern[half, block, :] for half in range(2)]
        bases = [[jnp.broadcast_to(x[k : k + 1], (8, 128)) for x in lags] for k in range(SUB)]
        for bit in range(3):
            bases = [[jnp.where(odd[bit], pltpu.roll(x, 2**bit, 1), x) for x in pair] for pair in bases]
        for k in range(SUB):
            shifted = [
                jnp.concatenate([pltpu.roll(x, 8 * m, 1) if m else x for m in range(16)], axis=0) for x in bases[k]
            ]
            kmat[g * SUB + k, :, pl.ds(0, 128)] = jnp.where(above, shifted[0], 0.0).astype(BF16)
            kmat[g * SUB + k, :, pl.ds(128, 128)] = jnp.where(above, shifted[1], shifted[0]).astype(BF16)
        return carry

    vocab_row = iota((VOCAB // 2, STEPS), 0)

    def hot(s, carry):
        for j in range(CTX):
            landed = all_ids.at[s, pl.ds(j, 1), :]
            pltpu.make_async_copy(ids_ref, landed, ids_recv.at[j * FSDP + s]).wait()
            row = all_ids[s, pl.ds(j, 1), :]
            low = jnp.where(row >= VOCAB // 2, row - VOCAB // 2, row)
            onehot[s * CTX + j] = jnp.where(vocab_row == low, 1.0, 0.0).astype(BF16)
        return carry

    lax.fori_loop(0, SLICE // SUB, fill, 0)
    diagonal128 = iota((128, 128), 0) == iota((128, 128), 1)
    for g in range(SLICE // SUB):
        block = params[pl.ds(pl.multiple_of(y * SLICE + g * SUB, SUB), SUB), :]
        decay = jnp.concatenate(
            [jnp.broadcast_to(block[:, n : n + 1], (SUB, 128)) for n in range(POLES)], axis=0
        )
        decay = jnp.sum(jnp.where(diagonal128, decay, 0.0), axis=0, keepdims=True)
        for _ in range(8):
            decay = decay * decay
        decays[g] = jnp.broadcast_to(decay, (8, 128))

    lax.fori_loop(0, FSDP, hot, 0)

    for k in range(1, TP):
        squares_to(k).wait_send()

    @pl.when(t == y)
    def _():
        for copy in handed:
            copy.wait_send()

    @pl.when(hi != home)
    def _():
        for copy in forward:
            copy.wait_send()

    for other, device in others:
        ids_to(other, device).wait_send()

    block16 = lax.div(iota((16, 128), 1), SLICE)
    for step in range(CHUNKS):
        pair = lax.rem(lax.div(i, 2) + 4 - FAR_X[step], CHUNKS)
        for z in range(2):
            four = parts.at[pl.ds((pair * 2 + z) * 4, 4)]
            pltpu.make_async_copy(four, four, part_recv.at[pair * 2 + z]).wait()
            a = parts[(pair * 2 + z) * 4].astype(F32)
            for k in range(1, 4):
                a = a + parts[(pair * 2 + z) * 4 + k].astype(F32)
            tail = [pltpu.roll(a[16 * s : 16 * s + 16], SLICE * (s + 1), 1) for s in range(3)]
            whole[pl.ds(z * ROWS, 48), :] = a
            whole[pl.ds(z * ROWS + 48, 16), :] = jnp.where(
                block16 == 0, tail[0], jnp.where(block16 == 1, tail[1], tail[2])
            )
        to = pl.ds(pl.multiple_of(lax.div(pair, 2) * (3 * SLICE), 3 * SLICE), 3 * SLICE)
        cols = pl.ds(pl.multiple_of(lax.rem(pair, 2) * 128, 128), 128)
        table[to, cols] = whole[...].T[: 3 * SLICE].astype(BF16)

    def gather(s, carry):
        for j in range(CTX):
            at = s * CTX + j
            both = jnp.dot(table[...], onehot[at], preferred_element_type=F32)
            upper = all_ids[s, pl.ds(j, 1), :] >= VOCAB // 2
            for half in range(2):
                cols = slice(half * 128, half * 128 + 128)
                raw[half, at] = jnp.where(upper[:, cols], both[3 * SLICE :, cols], both[: 3 * SLICE, cols])
        return carry

    lax.fori_loop(0, FSDP, gather, 0)

    lane = iota((SUB, 128), 1)

    def featurize(g):
        block = params[pl.ds(pl.multiple_of(y * SLICE + g * SUB, SUB), SUB), :]
        taps = [
            [
                jnp.broadcast_to(block[:, 2 * POLES + 3 * s + n : 2 * POLES + 3 * s + n + 1], (SUB, 128))
                for n in range(3)
            ]
            for s in range(3)
        ]
        for at in range(GROUP):
            if at % CTX == 0:
                before = [[jnp.zeros((SUB, 128), F32)] * 2] * 3
            for half in range(2):
                done = []
                for s in range(3):
                    now = raw[half, at, pl.ds(s * SLICE + g * SUB, SUB), :]
                    moved = [pltpu.roll(now, n, 1) for n in (1, 2)]
                    total = taps[s][0] * now
                    for n in (1, 2):
                        total = total + taps[s][n] * jnp.where(lane < n, before[s][n - 1], moved[n - 1])
                    before = before[:s] + [moved] + before[s + 1 :]
                    done.append(total)
                to = pl.ds(at * SUB, SUB)
                query[g][half, to, :] = done[0]
                product[g][half, to, :] = done[1] * done[2]

    channel = lax.rem(iota((GROUP, 128), 1), SUB)
    chunk = lax.rem(iota((GROUP, 128), 0), CTX)

    def convolve(g):
        decay = decays[g, 0:1, :]
        halves = [
            [product[g][half, pl.ds(k, GROUP, stride=SUB), :].astype(BF16) for half in range(2)] for k in range(SUB)
        ]
        inputs = jnp.concatenate([jnp.concatenate(x, axis=1) for x in halves], axis=0)
        states = lax.dot_general(inputs, vmat[g], (((1,), (1,)), ((), ())), preferred_element_type=F32)
        inner = []
        for k in range(SUB):
            both = jnp.dot(jnp.concatenate(halves[k], axis=0), kmat[g * SUB + k], preferred_element_type=F32)
            inner.append([both[:GROUP, :128], both[:GROUP, 128:] + both[GROUP:, :128]])
        stacked = states[:GROUP]
        for k in range(1, SUB):
            stacked = jnp.where(channel == k, states[k * GROUP : (k + 1) * GROUP], stacked)
        states = stacked
        states = jnp.where(chunk < 1, 0.0, pltpu.roll(states, 1, 0))
        for by in (1, 2, 4):
            states = states + decay * jnp.where(chunk < by, 0.0, pltpu.roll(states, by, 0))
            decay = decay * decay
        states = jnp.concatenate([jnp.where(channel == k, states, 0.0) for k in range(SUB)], axis=0)
        carried = jnp.dot(states.astype(BF16), gmat[g], preferred_element_type=F32)
        for k in range(SUB):
            for half in range(2):
                mixed[g][half, pl.ds(k, GROUP, stride=SUB), :] = (
                    inner[k][half] + carried[k * GROUP : (k + 1) * GROUP, half * 128 : half * 128 + 128]
                )

    mine_params = params[pl.ds(pl.multiple_of(y * SLICE, SLICE), SLICE), :]
    skip = jnp.broadcast_to(mine_params[:, 2 * POLES + 9 : 2 * POLES + 10], (SLICE, 128))
    pieces = onehot

    def share(part):
        return pl.ds(part * 2 * SUB, 2 * SUB)

    def out_to(part, other, device):
        return pltpu.make_async_remote_copy(
            src_ref=pieces.at[other, share(part), :], dst_ref=out_ref.at[me, share(part), :],
            send_sem=out_send.at[part], recv_sem=out_recv, device_id=device, device_id_type=MESH,
        )

    def gate(part, other, j, s):
        at = pl.ds(pl.multiple_of((s * CTX + j) * SUB, SUB), SUB)
        for half in range(2):
            q, u, c = [
                jnp.concatenate([x[2 * part + g][half, at, :] for g in range(2)], axis=0)
                for x in (query, product, mixed)
            ]
            gated = q * (c + skip[part * 2 * SUB : (part + 1) * 2 * SUB] * u)
            pieces[other, share(part), pl.ds(half * 128, 128)] = gated.astype(BF16)

    for part in range(2):
        featurize(2 * part)
        featurize(2 * part + 1)
        convolve(2 * part)
        convolve(2 * part + 1)
        for first in range(0, len(others), BATCH):
            batch = others[first : first + BATCH]
            for other, device in batch:
                gate(part, other, device[0], device[1])
            for other, device in batch:
                out_to(part, other, device).start()
        gate(part, me, i, y)
        pltpu.make_async_copy(pieces.at[me, share(part), :], out_ref.at[me, share(part), :], out_recv).start()

    sent = send_buf.at[pl.ds(0, GROUP - 1)]
    pltpu.make_async_copy(sent, sent, part_send).wait()
    for part in range(2):
        sent = pieces.at[pl.ds(0, GROUP - 1), share(part), :]
        pltpu.make_async_copy(sent, sent, out_send.at[part]).wait()
    pltpu.make_async_copy(out_ref, out_ref, out_recv).wait()


def block(*args):
    hbm = pl.BlockSpec(memory_space=pltpu.HBM)
    dma = pltpu.SemaphoreType.DMA
    groups = SLICE // SUB
    return pl.pallas_call(
        block_kernel,
        out_shape=jax.ShapeDtypeStruct((GROUP, SLICE, STEPS), BF16),
        in_specs=[hbm] * 8,
        out_specs=hbm,
        scratch_shapes=[
            pltpu.VMEM((CHUNKS, 3, FEAT, CHUNK), BF16),
            pltpu.VMEM((ROWS, FEAT), BF16),
            pltpu.VMEM((ROWS, FEAT), BF16),
            pltpu.VMEM((TP, 8, 128), F32),
            pltpu.VMEM((GROUP, 48, 128), BF16),
            pltpu.VMEM((GROUP, 48, 128), BF16),
            pltpu.VMEM((FSDP, CTX, STEPS), jnp.int32),
            pltpu.VMEM((1, FEAT * FSDP), F32),
            pltpu.VMEM((3, 3, CHAN), F32),
            pltpu.VMEM((POLES, CHAN), F32),
            pltpu.VMEM((POLES, CHAN), F32),
            pltpu.VMEM((1, CHAN), F32),
            pltpu.VMEM((128, 128), F32),
            pltpu.VMEM((groups, 8, 128), F32),
            pltpu.VMEM((2, SLICE, 128), F32),
            pltpu.VMEM((SLICE, STEPS // 2, STEPS), BF16),
            pltpu.VMEM((groups, POLES * SUB, STEPS), BF16),
            pltpu.VMEM((groups, POLES * SUB, STEPS), BF16),
            pltpu.VMEM((GROUP, VOCAB // 2, STEPS), BF16),
            pltpu.VMEM((6 * SLICE, VOCAB // 2), BF16),
            pltpu.VMEM((2 * ROWS, 128), F32),
            pltpu.VMEM((2, GROUP, 3 * SLICE, 128), F32),
            [pltpu.VMEM((2, GROUP * SUB, 128), F32) for _ in range(groups)],
            [pltpu.VMEM((2, GROUP * SUB, 128), F32) for _ in range(groups)],
            [pltpu.VMEM((2, GROUP * SUB, 128), F32) for _ in range(groups)],
            dma((CHUNKS,)),
            dma,
            dma((5,)),
            dma((4,)),
            dma((8,)),
            dma((TP,)),
            dma((TP,)),
            dma((GROUP,)),
            dma((GROUP,)),
            dma,
            dma((CTX,)),
            dma((2,)),
            dma,
            pltpu.SemaphoreType.REGULAR,
        ],
        compiler_params=pltpu.CompilerParams(
            collective_id=0, has_side_effects=True, vmem_limit_bytes=56 * 2**20
        ),
        name="hyena_block",
    )(*args)


def shards(
    base_ids, embed_table, norm_gain, in_weight, conv_taps, modal_poles, residues, skip_gain
):
    landed = block(
        base_ids, embed_table, norm_gain.reshape(1, -1), jnp.transpose(in_weight, (1, 0, 2)),
        conv_taps, modal_poles, residues, skip_gain.reshape(1, -1),
    )
    return landed.reshape(CHAN, STEPS).T[None]


def solution(mesh):
    in_specs = (
        P("fsdp", "ctx"),
        P(None, "tp"),
        P(),
        P("fsdp", None, "tp"),
        P(None, None, "tp"),
        P(None, "tp"),
        P(None, "tp"),
        P("tp"),
    )
    out_specs = P("fsdp", "ctx", "tp")
    return jax.shard_map(shards, mesh=mesh, in_specs=in_specs, out_specs=out_specs, check_vma=False)
```
